32 devices in a mesh: stream: 4 (over z), span: 8 (over y, x, core).
Axes of the slice: x: 2, y: 2, z: 4, core: 2. Of those that a mesh axis runs over, the one named last changes fastest.
Arguments:
- pre_pops: float32 [19, 32, 64, 128], P(None, 'stream', 'span'), may hold values from 0.7 to 1.3
- main_pops: float32 [19, 32, 64, 256], P(None, 'stream', 'span'), may hold values from 0.7 to 1.3
- tile_map: int32 [8], replicated, may hold values from 0 to 7, each once
- layer_phase: int32 [8], replicated, may hold values from 0 to 1
- wall_flags: int32 [256], replicated, may hold values 0 or 1
Outputs:
- pre_out: float32 [19, 32, 64, 128], P(None, 'stream', 'span')
- main_out: float32 [19, 32, 64, 256], P(None, 'stream', 'span')
The draws below stay inside these ranges and needn't reach their ends.
Inputs may be any that keep to these rules, and one draw needn't show every extreme that they name: `tile_map`: each precursor tile feeds exactly one inlet tile.
All inputs are finite; a program needn't handle non-finite values.
Results may differ from the reference program's by a relative error of at most 0.0003.
Values sent between devices are 32-bit elements; how exact they have to be, the bound alone decides.
No kernel may reach another device: no remote copies, remote signals or barrier semaphores. Data moves between devices by JAX's collectives and lax.ppermute only.
A program may use at most 64 MiB of HBM per device.

```python
import jax
import jax.numpy as jnp
from jax import lax

CX = 8
NW = 256
STEPS = 2
NWC = 128
NX = 32
NZ = 64
SPAN_TILES = 8


def place_ends(drawn, stream_key, least, top_value):
    index_at = [jax.random.randint(jax.random.fold_in(stream_key, axis), (), 0, length) for axis, length in enumerate(drawn.shape)]
    main_axis = drawn.shape.index(max(drawn.shape))
    next_to = index_at[:main_axis] + [(index_at[main_axis] + 1) % drawn.shape[main_axis]] + index_at[main_axis + 1:]
    return drawn.at[tuple(index_at)].set(least).at[tuple(next_to)].set(top_value)


def levels(rng, shape, pieces, least, top_value):
    gain = 1.0
    for axis_at, blocks in pieces:
        steps = jax.random.uniform(jax.random.fold_in(jax.random.fold_in(rng, 6), axis_at), (blocks,), jnp.float32, least / len(pieces), top_value / len(pieces))
        gain = gain * jnp.repeat(jnp.exp(steps), shape[axis_at] // blocks).reshape((-1,) + (1,) * (len(shape) - 1 - axis_at))
    return gain


def setup_inputs(seed: int = 0) -> dict:
    keys = jax.random.split(jax.random.key(seed), 6)
    return {
        "pre_pops": jnp.clip(0.7 + 0.59999996 * jax.random.uniform(keys[0], (19, NX, NZ, NWC), jnp.float32) ** levels(keys[0], (19, NX, NZ, NWC), ((1, 4), (2, 8)), -0.2, 0.2), 0.7, 1.3),
        "main_pops": jnp.clip(0.7 + 0.59999996 * jax.random.uniform(keys[1], (19, NX, NZ, NW), jnp.float32) ** levels(keys[1], (19, NX, NZ, NW), ((1, 4), (2, 8)), -0.2, 0.2), 0.7, 1.3),
        "tile_map": jax.random.permutation(keys[2], SPAN_TILES).astype(jnp.int32),
        "layer_phase": place_ends(jax.random.randint(keys[3], (SPAN_TILES,), 0, 2), jax.random.fold_in(keys[3], 1), 0, 1).astype(jnp.int32),
        "wall_flags": place_ends((jax.random.randint(keys[4], (NW,), 0, 8) < 1).astype(jnp.int32), jax.random.fold_in(keys[4], 1), 0, 1),
    }


velocities = ((0, 0, 0), (1, 0, 0), (-1, 0, 0), (0, 1, 0), (0, -1, 0), (0, 0, 1), (0, 0, -1), (1, 1, 0), (-1, -1, 0), (1, -1, 0), (-1, 1, 0), (1, 0, 1), (-1, 0, -1), (1, 0, -1), (-1, 0, 1), (0, 1, 1), (0, -1, -1), (0, 1, -1), (0, -1, 1))
opposite = (0, 2, 1, 4, 3, 6, 5, 8, 7, 10, 9, 12, 11, 14, 13, 16, 15, 18, 17)
lattice_weights = (1.0 / 3.0,) + (1.0 / 18.0,) * 6 + (1.0 / 36.0,) * 12
incoming = (1, 7, 9, 11, 13)
relax_rate = 1.25


def collide(pops):
    density = jnp.zeros_like(pops[0])
    moment = [jnp.zeros_like(pops[0]) for axis_num in range(3)]
    for which_pop in range(19):
        weighted = lattice_weights[which_pop] * pops[which_pop]
        density = density + weighted
        for axis_num in range(3):
            if velocities[which_pop][axis_num] != 0:
                moment[axis_num] = moment[axis_num] + velocities[which_pop][axis_num] * weighted
    speed = [component / density for component in moment]
    square = speed[0] * speed[0] + speed[1] * speed[1] + speed[2] * speed[2]
    result = []
    for which_pop in range(19):
        projected = jnp.zeros_like(density)
        for axis_num in range(3):
            if velocities[which_pop][axis_num] != 0:
                projected = projected + velocities[which_pop][axis_num] * speed[axis_num]
        balance = density * (1.0 + 3.0 * projected + 4.5 * projected * projected - 1.5 * square)
        result.append(pops[which_pop] - relax_rate * (pops[which_pop] - balance))
    return jnp.stack(result)


def stream(padded, collided, solid):
    row_len = collided.shape[1]
    span_len = collided.shape[2]
    layers = collided.shape[3]
    walled = jnp.concatenate([jnp.ones((1,), jnp.int32), solid.astype(jnp.int32), jnp.ones((1,), jnp.int32)])
    result = []
    for which_pop in range(19):
        step_x, step_y, step_z = velocities[which_pop]
        source = padded[which_pop, 1 - step_x:1 - step_x + row_len, 1 - step_z:1 - step_z + span_len, :]
        if step_y == 1:
            source = jnp.concatenate([jnp.zeros_like(source[..., :1]), source[..., :-1]], axis=-1)
        elif step_y == -1:
            source = jnp.concatenate([source[..., 1:], jnp.zeros_like(source[..., :1])], axis=-1)
        blocked = walled[1 - step_y:1 - step_y + layers] > 0
        result.append(jnp.where(blocked, collided[opposite[which_pop]], source))
    return jnp.stack(result)


def spread_matrix(coarse_len, fine_len, tile_phase):
    fine_pos = jnp.arange(fine_len, dtype=jnp.int32) + tile_phase.astype(jnp.int32)
    lower = (fine_pos - 1) // 2
    upper_wt = jnp.where(fine_pos % 2 == 0, 0.75, 0.25).astype(jnp.float32)
    low_idx = jnp.clip(lower, 0, coarse_len - 1)
    high_idx = jnp.clip(lower + 1, 0, coarse_len - 1)
    coarse_rows = jnp.arange(coarse_len, dtype=jnp.int32)[:, None]
    return jnp.where(coarse_rows == low_idx[None, :], 1.0 - upper_wt[None, :], 0.0).astype(jnp.float32) + jnp.where(coarse_rows == high_idx[None, :], upper_wt[None, :], 0.0).astype(jnp.float32)


def refine(coarse, tile_phase, fine_len):
    matrix = spread_matrix(coarse.shape[-1], fine_len, tile_phase)
    return jnp.dot(coarse, matrix, precision=lax.Precision.HIGHEST, preferred_element_type=jnp.float32)


def reference(pre_pops, main_pops, tile_map, layer_phase, wall_flags):
    coarse_len = pre_pops.shape[3]
    fine_len = main_pops.shape[3]
    solid_coarse = jnp.max(wall_flags.reshape(coarse_len, 2), axis=1)
    tile_count = tile_map.shape[0]
    tile_width = main_pops.shape[2] // tile_count
    for step_num in range(STEPS):
        pre_star = collide(pre_pops)
        main_star = collide(main_pops)
        pre_pad = jnp.pad(pre_star, ((0, 0), (1, 1), (1, 1), (0, 0)), mode="wrap")
        outflow = jnp.stack([pre_star[which_pop, CX - 1] for which_pop in incoming])
        blocks = outflow.reshape(5, tile_count, tile_width, coarse_len).transpose(1, 0, 2, 3)
        chosen = blocks[tile_map]
        fine_blocks = jax.vmap(lambda chosen_block, tile_phase: refine(chosen_block, tile_phase, fine_len))(chosen, layer_phase)
        inflow = fine_blocks.transpose(1, 0, 2, 3).reshape(5, tile_count * tile_width, fine_len)
        inflow = jnp.pad(inflow, ((0, 0), (1, 1), (0, 0)), mode="wrap")
        span_padded = jnp.pad(main_star, ((0, 0), (0, 0), (1, 1), (0, 0)), mode="wrap")
        ghost_plane = jnp.zeros_like(span_padded[:, 0])
        ghost_plane = ghost_plane.at[jnp.array(incoming, dtype=jnp.int32)].set(inflow)
        main_pad = jnp.concatenate([ghost_plane[:, None], span_padded, span_padded[:, -1:]], axis=1)
        pre_pops = stream(pre_pad, pre_star, solid_coarse)
        main_pops = stream(main_pad, main_star, wall_flags)
    return pre_pops, main_pops
```

```python
import jax
import jax.numpy as jnp
from jax import lax
from jax.experimental import pallas as pl
from jax.experimental.pallas import tpu as pltpu
from jax.sharding import PartitionSpec as P

velocities = (
    (0, 0, 0),
    (1, 0, 0),
    (-1, 0, 0),
    (0, 1, 0),
    (0, -1, 0),
    (0, 0, 1),
    (0, 0, -1),
    (1, 1, 0),
    (-1, -1, 0),
    (1, -1, 0),
    (-1, 1, 0),
    (1, 0, 1),
    (-1, 0, -1),
    (1, 0, -1),
    (-1, 0, 1),
    (0, 1, 1),
    (0, -1, -1),
    (0, 1, -1),
    (0, -1, 1),
)
opposite = (0, 2, 1, 4, 3, 6, 5, 8, 7, 10, 9, 12, 11, 14, 13, 16, 15, 18, 17)
pairs = tuple((k, k + 1) for k in range(1, 19, 2))
incoming = (1, 7, 9, 11, 13)
backward_x = (2, 8, 10, 12, 14)
forward_z = (5, 11, 14, 15, 18)
backward_z = (6, 12, 13, 16, 17)
POPS = 19
KEPT = POPS + 5
VMEM_BYTES = 56 * 1024 * 1024


def collide(pops, wanted=range(POPS)):
    sums = [pops[a] + pops[b] for a, b in pairs]
    difs = [pops[a] - pops[b] for a, b in pairs]
    density = (
        pops[0] * (1.0 / 3.0)
        + (sums[0] + sums[1] + sums[2]) * (1.0 / 18.0)
        + ((sums[3] + sums[4]) + (sums[5] + sums[6]) + (sums[7] + sums[8])) * (1.0 / 36.0)
    )
    moment = [
        difs[0] * (1.0 / 18.0) + ((difs[3] + difs[4]) + (difs[5] + difs[6])) * (1.0 / 36.0),
        difs[1] * (1.0 / 18.0) + ((difs[3] - difs[4]) + (difs[7] + difs[8])) * (1.0 / 36.0),
        difs[2] * (1.0 / 18.0) + ((difs[5] - difs[6]) + (difs[7] - difs[8])) * (1.0 / 36.0),
    ]
    inverse = 1.0 / density
    speed = [component * inverse for component in moment]
    kinetic = moment[0] * speed[0] + moment[1] * speed[1] + moment[2] * speed[2]
    base = 1.25 * density - 1.875 * kinetic
    result = [None] * POPS
    if 0 in wanted:
        result[0] = base - 0.25 * pops[0]
    for a, b in pairs:
        if a not in wanted and b not in wanted:
            continue
        flux = None
        along = None
        for axis_num, step in enumerate(velocities[a]):
            if step == 0:
                continue
            if flux is None:
                flux, along = moment[axis_num], speed[axis_num]
            elif step == 1:
                flux, along = flux + moment[axis_num], along + speed[axis_num]
            else:
                flux, along = flux - moment[axis_num], along - speed[axis_num]
        even = base + 5.625 * (flux * along)
        odd = 3.75 * flux
        if a in wanted:
            result[a] = even + odd - 0.25 * pops[a]
        if b in wanted:
            result[b] = even - odd - 0.25 * pops[b]
    return result


def shift_layers(value, step_y):
    if step_y == 0:
        return value
    size = value.shape[-1]
    return pltpu.roll(value, step_y % size, value.ndim - 1)


def moved_row(base, left, right, masks, x_at):
    result = []
    sub = None
    for which_pop in range(POPS):
        step_x, step_y, step_z = velocities[which_pop]
        source = base(which_pop, x_at - step_x)
        if step_z != 0 and sub is None:
            sub = lax.broadcasted_iota(jnp.int32, source.shape, 0)
        width = source.shape[0]
        if step_z == 1:
            source = jnp.where(
                sub == 0, left(which_pop, x_at - step_x), pltpu.roll(source, 1, 0)
            )
        elif step_z == -1:
            source = jnp.where(
                sub == width - 1,
                right(which_pop, x_at - step_x),
                pltpu.roll(source, width - 1, 0),
            )
        source = shift_layers(source, step_y)
        result.append(
            jnp.where(masks[step_y] != 0, base(opposite[which_pop], x_at), source)
        )
    return result


def first_kernel(pre, main, star_pre, star_main, x_hi, x_lo, z_same, z_cross, x_small):
    rows = pre.shape[1]
    coarse = pre.shape[3]
    parity = lax.rem(lax.axis_index("span"), 2)
    domains = ((pre, star_pre, slice(0, coarse)), (main, star_main, slice(coarse, None)))
    for x_at in range(rows):
        for pops, star, lanes in domains:
            out = collide([pops[which_pop, x_at] for which_pop in range(POPS)])
            for which_pop in range(POPS):
                star[which_pop, x_at] = out[which_pop]
                if x_at == 0:
                    x_lo[which_pop, :, lanes] = out[which_pop]
                if x_at == rows - 1:
                    x_hi[which_pop, :, lanes] = out[which_pop]
            for k in range(5):
                if x_at == 1:
                    x_lo[POPS + k, :, lanes] = out[backward_x[k]]
                if x_at == rows - 2:
                    x_hi[POPS + k, :, lanes] = out[incoming[k]]
                if x_at == 0 and star is star_pre:
                    x_small[k] = out[backward_x[k]]

    def edges(hi, lo):
        for _, star, lanes in domains:
            width = star.shape[2]
            for which_pop in range(POPS):
                hi[which_pop, :, lanes] = star[which_pop, :, width - 1, :]
                lo[which_pop, :, lanes] = star[which_pop, :, 0, :]
            for k in range(5):
                hi[POPS + k, :, lanes] = star[forward_z[k], :, width - 2, :]
                lo[POPS + k, :, lanes] = star[backward_z[k], :, 1, :]

    @pl.when(parity == 0)
    def _():
        edges(z_same, z_cross)

    @pl.when(parity == 1)
    def _():
        edges(z_cross, z_same)


def corner_kernel(same, cross, c_hi, c_lo):
    last = same.shape[1] - 1
    for side, halo in enumerate((same, cross)):
        for k in range(KEPT):
            c_hi[side, k : k + 1, :] = halo[k, last : last + 1, :]
            c_lo[side, k : k + 1, :] = halo[k, 0:1, :]
        for k in range(5):
            at = KEPT + k
            c_hi[side, at : at + 1, :] = halo[incoming[k], last - 1 : last, :]
            c_lo[side, at : at + 1, :] = halo[backward_x[k], 1:2, :]
        for k in (1, 2):
            at = KEPT + 4 + k
            c_hi[side, at : at + 1, :] = halo[POPS + k, last - 1 : last, :]
            c_lo[side, at : at + 1, :] = halo[POPS + k, 1:2, :]


def build_columns(is_left, col, halo, edge, side, x_low, x_high, c_low, c_high):
    inward = backward_z if is_left else forward_z
    rim = 0 if is_left else x_low.shape[1] - 1
    for k in range(KEPT):
        col[k, 8:16, :] = halo[k]
        col[k, 7:8, :] = c_low[side, k : k + 1, :]
        col[k, 16:17, :] = c_high[side, k : k + 1, :]
    for k in range(5):
        col[incoming[k], 6:7, :] = c_low[side, KEPT + k : KEPT + k + 1, :]
        col[backward_x[k], 17:18, :] = c_high[side, KEPT + k : KEPT + k + 1, :]
    hi_k, lo_k = (1, 2) if is_left else (2, 1)
    col[POPS + hi_k, 6:7, :] = c_low[side, KEPT + 4 + hi_k : KEPT + 5 + hi_k, :]
    col[POPS + lo_k, 17:18, :] = c_high[side, KEPT + 4 + lo_k : KEPT + 5 + lo_k, :]
    for k in range(5):
        pop = inward[k]
        at = KEPT + k
        col[at, 8:16, :] = edge[pop]
        col[at, 7:8, :] = x_low[pop, rim : rim + 1, :]
        col[at, 16:17, :] = x_high[pop, rim : rim + 1, :]
        if pop in incoming:
            second = POPS + incoming.index(pop)
            col[at, 6:7, :] = x_low[second, rim : rim + 1, :]
        if pop in backward_x:
            second = POPS + backward_x.index(pop)
            col[at, 17:18, :] = x_high[second, rim : rim + 1, :]


def refine(coarse, phases, fine_len):
    coarse_len = coarse.shape[1]
    count = coarse.shape[0] // 3
    rows = lax.broadcasted_iota(jnp.int32, (coarse_len, fine_len), 0)
    fine = lax.broadcasted_iota(jnp.int32, (coarse_len, fine_len), 1)
    outs = []
    for phase in (0, 1):
        position = fine + phase
        lower = lax.shift_right_arithmetic(position - 1, 1)
        upper_wt = jnp.where(position % 2 == 0, 0.75, 0.25)
        low_idx = jnp.clip(lower, 0, coarse_len - 1)
        high_idx = jnp.clip(lower + 1, 0, coarse_len - 1)
        matrix = jnp.where(rows == low_idx, 1.0 - upper_wt, 0.0) + jnp.where(
            rows == high_idx, upper_wt, 0.0
        )
        outs.append(
            jnp.dot(
                coarse,
                matrix,
                precision=lax.Precision.HIGHEST,
                preferred_element_type=jnp.float32,
            )
        )
    return [
        jnp.where(
            phases[tile] > 0,
            outs[1][tile * count : (tile + 1) * count],
            outs[0][tile * count : (tile + 1) * count],
        )
        for tile in range(3)
    ]


def second_kernel(
    tile_map,
    layer_phase,
    walls,
    star_pre,
    star_main,
    x_low,
    x_high,
    same,
    cross,
    edge_same,
    edge_cross,
    c_low,
    c_high,
    tiles,
    out_pre,
    out_main,
    col_left,
    col_right,
    in_low,
    in_high,
    mask_pre,
    mask_main,
    inflow,
    next_pre,
    next_main,
    rim_left,
    rim_right,
):
    rows, width, coarse = star_pre.shape[1:]
    fine = star_main.shape[3]
    pre_lanes, main_lanes = slice(0, coarse), slice(coarse, coarse + fine)
    span_pos = lax.axis_index("span")
    stream_pos = lax.axis_index("stream")
    span_count = lax.axis_size("span")
    is_first = stream_pos == 0
    is_last = stream_pos == lax.axis_size("stream") - 1
    parity = lax.rem(span_pos, 2)

    def masks_of(solid, ref):
        layers = solid.shape[1]
        lane = lax.broadcasted_iota(jnp.int32, solid.shape, 1)
        ref[0] = solid
        ref[1] = jnp.where(lane == 0, 1.0, pltpu.roll(solid, 1, 1))
        ref[2] = jnp.where(lane == layers - 1, 1.0, pltpu.roll(solid, layers - 1, 1))

    solid = jnp.broadcast_to(jnp.where(walls[...] > 0, 1.0, 0.0), (8, fine))
    fine_at = lax.broadcasted_iota(jnp.int32, (fine, coarse), 0)
    coarse_at = lax.broadcasted_iota(jnp.int32, (fine, coarse), 1)
    halves = jnp.where(lax.shift_right_logical(fine_at, 1) == coarse_at, 1.0, 0.0)
    hits = jnp.dot(solid, halves, preferred_element_type=jnp.float32)
    masks_of(solid, mask_main)
    masks_of(jnp.where(hits > 0.5, 1.0, 0.0), mask_pre)
    masks = {step: (mask_pre[step % 3], mask_main[step % 3]) for step in (0, 1, -1)}

    def masks_for(domain, height=8):
        if height == 8:
            return {step: masks[step][domain] for step in masks}
        return {
            step: jnp.broadcast_to(masks[step][domain][:1], (height, masks[step][domain].shape[1]))
            for step in masks
        }

    @pl.when(parity == 0)
    def _():
        build_columns(True, col_left, cross, edge_cross, 1, x_low, x_high, c_low, c_high)
        build_columns(False, col_right, same, edge_same, 0, x_low, x_high, c_low, c_high)

    @pl.when(parity == 1)
    def _():
        build_columns(True, col_left, same, edge_same, 0, x_low, x_high, c_low, c_high)
        build_columns(False, col_right, cross, edge_cross, 1, x_low, x_high, c_low, c_high)

    for k in range(5):
        in_low[k] = x_low[incoming[k], :, main_lanes]
        in_high[k] = x_high[backward_x[k], :, main_lanes]

    @pl.when(is_last)
    def _():
        for k in range(5):
            in_high[k] = star_main[backward_x[k], rows - 1]
        for col in (col_left, col_right):
            for k in range(KEPT + 5):
                col[k, 16:17, main_lanes] = col[k, 15:16, main_lanes]

    @pl.when(is_first)
    def _():
        chosen, phases = [], []
        for offset in (span_count - 1, 0, 1):
            at = lax.rem(span_pos + offset, span_count)
            chosen.append(tile_map[at])
            phases.append(layer_phase[at])

        planes = [[tiles[tile, pop] for pop in incoming] for tile in chosen]
        planes_next = []
        for tile in chosen:
            before = lax.rem(tile + span_count - 1, span_count)
            after = lax.rem(tile + 1, span_count)

            def slot(pop, x_at):
                if x_at == 0:
                    return pop
                if x_at == -1:
                    return POPS + incoming.index(pop)
                return KEPT + backward_x.index(pop)

            new = moved_row(
                lambda pop, x_at: tiles[tile, slot(pop, x_at)],
                lambda pop, x_at: tiles[before, slot(pop, x_at), width - 1 : width, :],
                lambda pop, x_at: tiles[after, slot(pop, x_at), 0:1, :],
                masks_for(0),
                0,
            )
            out = collide(new, incoming)
            planes_next.append([out[pop] for pop in incoming])
        for step_num, found in enumerate((planes, planes_next)):
            stacked = jnp.concatenate([plane for group in found for plane in group], axis=0)
            for tile, value in enumerate(refine(stacked, phases, fine)):
                inflow[step_num, tile] = value.reshape(5, width, fine)
        before, own, after = (inflow.at[0, tile] for tile in range(3))
        for k in range(5):
            in_low[k] = own[k]
            col_left[incoming[k], 7:8, main_lanes] = before[k, width - 1 : width]
            col_right[incoming[k], 7:8, main_lanes] = after[k, 0:1]
        col_left[POPS + 1, 7:8, main_lanes] = before[3, width - 2 : width - 1]
        col_left[KEPT + 2, 7:8, main_lanes] = own[4, 0:1]
        col_right[POPS + 2, 7:8, main_lanes] = after[4, 1:2]
        col_right[KEPT + 1, 7:8, main_lanes] = own[3, width - 1 : width]

    for is_left, col, rim in ((True, col_left, rim_left), (False, col_right, rim_right)):
        moving = forward_z if is_left else backward_z
        for domain, lanes in enumerate((pre_lanes, main_lanes)):
            tall = masks_for(domain, 16)
            new = []
            for pop in range(POPS):
                step_x, step_y, step_z = velocities[pop]
                if step_z == 0:
                    at = pop
                elif pop in moving:
                    at = POPS + moving.index(pop)
                else:
                    at = KEPT + (backward_z if is_left else forward_z).index(pop)
                source = shift_layers(col[at, 7 - step_x : 23 - step_x, lanes], step_y)
                new.append(
                    jnp.where(tall[step_y] != 0, col[opposite[pop], 7:23, lanes], source)
                )
            out = collide(new, moving)
            for k in range(5):
                rim[k, :, lanes] = out[moving[k]]

    stars = (star_pre, star_main)
    nexts = (next_pre, next_main)

    def base_of(domain, lanes):
        def base(pop, x_at):
            if 0 <= x_at < rows:
                return stars[domain][pop, x_at]
            if x_at == -1:
                if domain == 1 and pop in incoming:
                    return in_low[incoming.index(pop)]
                return x_low[pop, :, lanes]
            if x_at == rows:
                if domain == 1 and pop in backward_x:
                    return in_high[backward_x.index(pop)]
                return x_high[pop, :, lanes]
            if x_at < 0:
                return x_low[POPS + incoming.index(pop), :, lanes]
            return x_high[POPS + backward_x.index(pop), :, lanes]

        return base

    for x_at in range(-1, rows + 1):
        for domain, lanes in enumerate((pre_lanes, main_lanes)):
            new = moved_row(
                base_of(domain, lanes),
                lambda pop, at: col_left[pop, 8 + at : 9 + at, lanes],
                lambda pop, at: col_right[pop, 8 + at : 9 + at, lanes],
                masks_for(domain),
                x_at,
            )
            wanted = range(POPS)
            if x_at == -1:
                wanted = incoming
            elif x_at == rows:
                wanted = backward_x
            out = collide(new, wanted)
            for pop in wanted:
                nexts[domain][pop, x_at + 1] = out[pop]

    @pl.when(is_first)
    def _():
        for k in range(5):
            next_main[incoming[k], 0] = inflow[1, 1, k]
        rim_left[1, 0:1, main_lanes] = inflow[1, 0, 3, width - 1 : width]
        rim_right[2, 0:1, main_lanes] = inflow[1, 2, 4, 0:1]

    @pl.when(is_last)
    def _():
        for k in range(5):
            next_main[backward_x[k], rows + 1] = next_main[backward_x[k], rows]
            for rim in (rim_left, rim_right):
                rim[k, rows + 1 : rows + 2, main_lanes] = rim[k, rows : rows + 1, main_lanes]

    for x_at in range(rows):
        for domain, lanes in enumerate((pre_lanes, main_lanes)):
            new = moved_row(
                lambda pop, at: nexts[domain][pop, at + 1],
                lambda pop, at: rim_left[forward_z.index(pop), at + 1 : at + 2, lanes],
                lambda pop, at: rim_right[backward_z.index(pop), at + 1 : at + 2, lanes],
                masks_for(domain),
                x_at,
            )
            for pop in range(POPS):
                (out_pre, out_main)[domain][pop, x_at] = new[pop]


def f32(*shape):
    return jax.ShapeDtypeStruct(shape, jnp.float32)


def local(pre_pops, main_pops, tile_map, layer_phase, wall_flags):
    span_count = lax.axis_size("span")
    stream_count = lax.axis_size("stream")
    _, rows, width, coarse = pre_pops.shape
    fine = main_pops.shape[3]
    lanes = coarse + fine

    def send(value, step_x, place, only=None):
        moves = []
        for s in range(stream_count):
            if only is not None and s != only:
                continue
            for j in range(span_count):
                target = (s + step_x) % stream_count * span_count + place(j) % span_count
                moves.append((s * span_count + j, target))
        return lax.ppermute(value, ("stream", "span"), moves)

    stay = lambda j: j
    sibling = lambda j: j + 1 if j % 2 == 0 else j - 1
    beyond = lambda j: j - 1 if j % 2 == 0 else j + 1
    params = pltpu.CompilerParams(vmem_limit_bytes=VMEM_BYTES)

    star_pre, star_main, x_hi, x_lo, z_same, z_cross, x_small = pl.pallas_call(
        first_kernel,
        out_shape=(
            f32(*pre_pops.shape),
            f32(*main_pops.shape),
            f32(KEPT, width, lanes),
            f32(KEPT, width, lanes),
            f32(KEPT, rows, lanes),
            f32(KEPT, rows, lanes),
            f32(5, width, coarse),
        ),
        compiler_params=params,
        name="collide_and_pack",
    )(pre_pops, main_pops)

    beside = send(x_small, -1, stay, only=1 % stream_count)
    same = send(z_same, 0, sibling)
    cross = send(z_cross, 0, beyond)
    x_low = send(x_hi, 1, stay)
    x_high = send(x_lo, -1, stay)
    c_hi, c_lo = pl.pallas_call(
        corner_kernel,
        out_shape=(f32(2, 32, lanes), f32(2, 32, lanes)),
        compiler_params=params,
        name="corners",
    )(same, cross)
    c_low = send(c_hi, 1, stay)
    c_high = send(c_lo, -1, stay)
    plane = jnp.concatenate([x_hi[:, :, :coarse], beside], axis=0)
    tiles = lax.all_gather(plane, "span", axis=0, tiled=False)

    whole = pl.BlockSpec(memory_space=pltpu.VMEM)
    scalars = pl.BlockSpec(memory_space=pltpu.SMEM)
    return pl.pallas_call(
        second_kernel,
        out_shape=(f32(*pre_pops.shape), f32(*main_pops.shape)),
        in_specs=[scalars, scalars] + [whole] * 12,
        scratch_shapes=[
            pltpu.VMEM((KEPT + 5, 24, lanes), jnp.float32),
            pltpu.VMEM((KEPT + 5, 24, lanes), jnp.float32),
            pltpu.VMEM((5, width, fine), jnp.float32),
            pltpu.VMEM((5, width, fine), jnp.float32),
            pltpu.VMEM((3, 8, coarse), jnp.float32),
            pltpu.VMEM((3, 8, fine), jnp.float32),
            pltpu.VMEM((2, 3, 5, width, fine), jnp.float32),
            pltpu.VMEM((POPS, rows + 2, width, coarse), jnp.float32),
            pltpu.VMEM((POPS, rows + 2, width, fine), jnp.float32),
            pltpu.VMEM((5, 16, lanes), jnp.float32),
            pltpu.VMEM((5, 16, lanes), jnp.float32),
        ],
        compiler_params=params,
        name="two_steps",
    )(
        tile_map,
        layer_phase,
        wall_flags.reshape(1, fine),
        star_pre,
        star_main,
        x_low,
        x_high,
        same,
        cross,
        z_same,
        z_cross,
        c_low,
        c_high,
        tiles,
    )


def solution(mesh):
    return jax.shard_map(
        local,
        mesh=mesh,
        in_specs=(P(None, "stream", "span", None), P(None, "stream", "span", None), P(), P(), P()),
        out_specs=(P(None, "stream", "span", None), P(None, "stream", "span", None)),
        check_vma=False,
    )
```

```python
import jax
import jax.numpy as jnp
from jax import lax
from jax.experimental import pallas as pl
from jax.experimental.pallas import tpu as pltpu
from jax.sharding import PartitionSpec as P

velocities = (
    (0, 0, 0),
    (1, 0, 0),
    (-1, 0, 0),
    (0, 1, 0),
    (0, -1, 0),
    (0, 0, 1),
    (0, 0, -1),
    (1, 1, 0),
    (-1, -1, 0),
    (1, -1, 0),
    (-1, 1, 0),
    (1, 0, 1),
    (-1, 0, -1),
    (1, 0, -1),
    (-1, 0, 1),
    (0, 1, 1),
    (0, -1, -1),
    (0, 1, -1),
    (0, -1, 1),
)
opposite = (0, 2, 1, 4, 3, 6, 5, 8, 7, 10, 9, 12, 11, 14, 13, 16, 15, 18, 17)
pairs = tuple((k, k + 1) for k in range(1, 19, 2))
incoming = (1, 7, 9, 11, 13)
backward_x = (2, 8, 10, 12, 14)
forward_z = (5, 11, 14, 15, 18)
backward_z = (6, 12, 13, 16, 17)
POPS = 19
KEPT = POPS + 5
VMEM_SMALL = 10 * 1024 * 1024
VMEM_LARGE = 20 * 1024 * 1024


def collide(pops, wanted=range(POPS)):
    sums = [pops[a] + pops[b] for a, b in pairs]
    difs = [pops[a] - pops[b] for a, b in pairs]
    density = (
        pops[0] * (1.0 / 3.0)
        + (sums[0] + sums[1] + sums[2]) * (1.0 / 18.0)
        + ((sums[3] + sums[4]) + (sums[5] + sums[6]) + (sums[7] + sums[8])) * (1.0 / 36.0)
    )
    moment = [
        difs[0] * (1.0 / 18.0) + ((difs[3] + difs[4]) + (difs[5] + difs[6])) * (1.0 / 36.0),
        difs[1] * (1.0 / 18.0) + ((difs[3] - difs[4]) + (difs[7] + difs[8])) * (1.0 / 36.0),
        difs[2] * (1.0 / 18.0) + ((difs[5] - difs[6]) + (difs[7] - difs[8])) * (1.0 / 36.0),
    ]
    inverse = 1.0 / density
    speed = [component * inverse for component in moment]
    kinetic = moment[0] * speed[0] + moment[1] * speed[1] + moment[2] * speed[2]
    base = 1.25 * density - 1.875 * kinetic
    result = [None] * POPS
    if 0 in wanted:
        result[0] = base - 0.25 * pops[0]
    for a, b in pairs:
        if a not in wanted and b not in wanted:
            continue
        flux = None
        along = None
        for axis_num, step in enumerate(velocities[a]):
            if step == 0:
                continue
            if flux is None:
                flux, along = moment[axis_num], speed[axis_num]
            elif step == 1:
                flux, along = flux + moment[axis_num], along + speed[axis_num]
            else:
                flux, along = flux - moment[axis_num], along - speed[axis_num]
        even = base + 5.625 * (flux * along)
        odd = 3.75 * flux
        if a in wanted:
            result[a] = even + odd - 0.25 * pops[a]
        if b in wanted:
            result[b] = even - odd - 0.25 * pops[b]
    return result


def shift_layers(value, step_y):
    if step_y == 0:
        return value
    size = value.shape[-1]
    return pltpu.roll(value, step_y % size, value.ndim - 1)


def moved_row(base, left, right, masks, x_at):
    result = []
    sub = None
    for which_pop in range(POPS):
        step_x, step_y, step_z = velocities[which_pop]
        source = base(which_pop, x_at - step_x)
        if step_z != 0 and sub is None:
            sub = lax.broadcasted_iota(jnp.int32, source.shape, 0)
        width = source.shape[0]
        if step_z == 1:
            source = jnp.where(
                sub == 0, left(which_pop, x_at - step_x), pltpu.roll(source, 1, 0)
            )
        elif step_z == -1:
            source = jnp.where(
                sub == width - 1,
                right(which_pop, x_at - step_x),
                pltpu.roll(source, width - 1, 0),
            )
        source = shift_layers(source, step_y)
        result.append(
            jnp.where(masks[step_y] != 0, base(opposite[which_pop], x_at), source)
        )
    return result


def first_kernel(pre, main, star_pre, star_main, x_hi, x_lo, z_same, z_cross, x_small):
    rows = pre.shape[1]
    coarse = pre.shape[3]
    parity = lax.rem(lax.axis_index("span"), 2)
    domains = ((pre, star_pre, slice(0, coarse)), (main, star_main, slice(coarse, None)))
    for x_at in range(rows):
        for pops, star, lanes in domains:
            out = collide([pops[which_pop, x_at] for which_pop in range(POPS)])
            for which_pop in range(POPS):
                star[which_pop, x_at] = out[which_pop]
                if x_at == 0:
                    x_lo[which_pop, :, lanes] = out[which_pop]
                if x_at == rows - 1:
                    x_hi[which_pop, :, lanes] = out[which_pop]
            for k in range(5):
                if x_at == 1:
                    x_lo[POPS + k, :, lanes] = out[backward_x[k]]
                if x_at == rows - 2:
                    x_hi[POPS + k, :, lanes] = out[incoming[k]]
                if x_at == 0 and star is star_pre:
                    x_small[k] = out[backward_x[k]]

    def edges(hi, lo):
        for _, star, lanes in domains:
            width = star.shape[2]
            for which_pop in range(POPS):
                hi[which_pop, :, lanes] = star[which_pop, :, width - 1, :]
                lo[which_pop, :, lanes] = star[which_pop, :, 0, :]
            for k in range(5):
                hi[POPS + k, :, lanes] = star[forward_z[k], :, width - 2, :]
                lo[POPS + k, :, lanes] = star[backward_z[k], :, 1, :]

    @pl.when(parity == 0)
    def _():
        edges(z_same, z_cross)

    @pl.when(parity == 1)
    def _():
        edges(z_cross, z_same)


def corner_kernel(same, cross, c_hi, c_lo):
    last = same.shape[1] - 1
    for side, halo in enumerate((same, cross)):
        for k in range(KEPT):
            c_hi[side, k : k + 1, :] = halo[k, last : last + 1, :]
            c_lo[side, k : k + 1, :] = halo[k, 0:1, :]
        for k in range(5):
            at = KEPT + k
            c_hi[side, at : at + 1, :] = halo[incoming[k], last - 1 : last, :]
            c_lo[side, at : at + 1, :] = halo[backward_x[k], 1:2, :]
        for k in (1, 2):
            at = KEPT + 4 + k
            c_hi[side, at : at + 1, :] = halo[POPS + k, last - 1 : last, :]
            c_lo[side, at : at + 1, :] = halo[POPS + k, 1:2, :]


def build_columns(is_left, col, halo, edge, side, x_low, x_high, c_low, c_high):
    inward = backward_z if is_left else forward_z
    rim = 0 if is_left else x_low.shape[1] - 1
    for k in range(KEPT):
        col[k, 8:16, :] = halo[k]
        col[k, 7:8, :] = c_low[side, k : k + 1, :]
        col[k, 16:17, :] = c_high[side, k : k + 1, :]
    for k in range(5):
        col[incoming[k], 6:7, :] = c_low[side, KEPT + k : KEPT + k + 1, :]
        col[backward_x[k], 17:18, :] = c_high[side, KEPT + k : KEPT + k + 1, :]
    hi_k, lo_k = (1, 2) if is_left else (2, 1)
    col[POPS + hi_k, 6:7, :] = c_low[side, KEPT + 4 + hi_k : KEPT + 5 + hi_k, :]
    col[POPS + lo_k, 17:18, :] = c_high[side, KEPT + 4 + lo_k : KEPT + 5 + lo_k, :]
    for k in range(5):
        pop = inward[k]
        at = KEPT + k
        col[at, 8:16, :] = edge[pop]
        col[at, 7:8, :] = x_low[pop, rim : rim + 1, :]
        col[at, 16:17, :] = x_high[pop, rim : rim + 1, :]
        if pop in incoming:
            second = POPS + incoming.index(pop)
            col[at, 6:7, :] = x_low[second, rim : rim + 1, :]
        if pop in backward_x:
            second = POPS + backward_x.index(pop)
            col[at, 17:18, :] = x_high[second, rim : rim + 1, :]


def refine(coarse, phases, fine_len):
    coarse_len = coarse.shape[1]
    count = coarse.shape[0] // 3
    rows = lax.broadcasted_iota(jnp.int32, (coarse_len, fine_len), 0)
    fine = lax.broadcasted_iota(jnp.int32, (coarse_len, fine_len), 1)
    outs = []
    for phase in (0, 1):
        position = fine + phase
        lower = lax.shift_right_arithmetic(position - 1, 1)
        upper_wt = jnp.where(position % 2 == 0, 0.75, 0.25)
        low_idx = jnp.clip(lower, 0, coarse_len - 1)
        high_idx = jnp.clip(lower + 1, 0, coarse_len - 1)
        matrix = jnp.where(rows == low_idx, 1.0 - upper_wt, 0.0) + jnp.where(
            rows == high_idx, upper_wt, 0.0
        )
        outs.append(
            jnp.dot(
                coarse,
                matrix,
                precision=lax.Precision.HIGHEST,
                preferred_element_type=jnp.float32,
            )
        )
    return [
        jnp.where(
            phases[tile] > 0,
            outs[1][tile * count : (tile + 1) * count],
            outs[0][tile * count : (tile + 1) * count],
        )
        for tile in range(3)
    ]


def second_kernel(
    tile_map,
    layer_phase,
    walls,
    star_pre,
    star_main,
    x_low,
    x_high,
    same,
    cross,
    edge_same,
    edge_cross,
    c_low,
    c_high,
    tiles,
    out_pre,
    out_main,
    col_left,
    col_right,
    in_low,
    in_high,
    mask_pre,
    mask_main,
    inflow,
    next_pre,
    next_main,
    rim_left,
    rim_right,
):
    rows, width, coarse = star_pre.shape[1:]
    fine = star_main.shape[3]
    pre_lanes, main_lanes = slice(0, coarse), slice(coarse, coarse + fine)
    span_pos = lax.axis_index("span")
    stream_pos = lax.axis_index("stream")
    span_count = lax.axis_size("span")
    is_first = stream_pos == 0
    is_last = stream_pos == lax.axis_size("stream") - 1
    parity = lax.rem(span_pos, 2)

    def masks_of(solid, ref):
        layers = solid.shape[1]
        lane = lax.broadcasted_iota(jnp.int32, solid.shape, 1)
        ref[0] = solid
        ref[1] = jnp.where(lane == 0, 1.0, pltpu.roll(solid, 1, 1))
        ref[2] = jnp.where(lane == layers - 1, 1.0, pltpu.roll(solid, layers - 1, 1))

    solid = jnp.broadcast_to(jnp.where(walls[...] > 0, 1.0, 0.0), (8, fine))
    fine_at = lax.broadcasted_iota(jnp.int32, (fine, coarse), 0)
    coarse_at = lax.broadcasted_iota(jnp.int32, (fine, coarse), 1)
    halves = jnp.where(lax.shift_right_logical(fine_at, 1) == coarse_at, 1.0, 0.0)
    hits = jnp.dot(solid, halves, preferred_element_type=jnp.float32)
    masks_of(solid, mask_main)
    masks_of(jnp.where(hits > 0.5, 1.0, 0.0), mask_pre)
    masks = {step: (mask_pre[step % 3], mask_main[step % 3]) for step in (0, 1, -1)}

    def masks_for(domain, height=8):
        if height == 8:
            return {step: masks[step][domain] for step in masks}
        return {
            step: jnp.broadcast_to(masks[step][domain][:1], (height, masks[step][domain].shape[1]))
            for step in masks
        }

    @pl.when(parity == 0)
    def _():
        build_columns(True, col_left, cross, edge_cross, 1, x_low, x_high, c_low, c_high)
        build_columns(False, col_right, same, edge_same, 0, x_low, x_high, c_low, c_high)

    @pl.when(parity == 1)
    def _():
        build_columns(True, col_left, same, edge_same, 0, x_low, x_high, c_low, c_high)
        build_columns(False, col_right, cross, edge_cross, 1, x_low, x_high, c_low, c_high)

    for k in range(5):
        in_low[k] = x_low[incoming[k], :, main_lanes]
        in_high[k] = x_high[backward_x[k], :, main_lanes]

    @pl.when(is_last)
    def _():
        for k in range(5):
            in_high[k] = star_main[backward_x[k], rows - 1]
        for col in (col_left, col_right):
            for k in range(KEPT + 5):
                col[k, 16:17, main_lanes] = col[k, 15:16, main_lanes]

    @pl.when(is_first)
    def _():
        chosen, phases = [], []
        for offset in (span_count - 1, 0, 1):
            at = lax.rem(span_pos + offset, span_count)
            chosen.append(tile_map[at])
            phases.append(layer_phase[at])

        planes = [[tiles[tile, pop] for pop in incoming] for tile in chosen]
        planes_next = []
        for tile in chosen:
            before = lax.rem(tile + span_count - 1, span_count)
            after = lax.rem(tile + 1, span_count)

            def slot(pop, x_at):
                if x_at == 0:
                    return pop
                if x_at == -1:
                    return POPS + incoming.index(pop)
                return KEPT + backward_x.index(pop)

            new = moved_row(
                lambda pop, x_at: tiles[tile, slot(pop, x_at)],
                lambda pop, x_at: tiles[before, slot(pop, x_at), width - 1 : width, :],
                lambda pop, x_at: tiles[after, slot(pop, x_at), 0:1, :],
                masks_for(0),
                0,
            )
            out = collide(new, incoming)
            planes_next.append([out[pop] for pop in incoming])
        for step_num, found in enumerate((planes, planes_next)):
            stacked = jnp.concatenate([plane for group in found for plane in group], axis=0)
            for tile, value in enumerate(refine(stacked, phases, fine)):
                inflow[step_num, tile] = value.reshape(5, width, fine)
        before, own, after = (inflow.at[0, tile] for tile in range(3))
        for k in range(5):
            in_low[k] = own[k]
            col_left[incoming[k], 7:8, main_lanes] = before[k, width - 1 : width]
            col_right[incoming[k], 7:8, main_lanes] = after[k, 0:1]
        col_left[POPS + 1, 7:8, main_lanes] = before[3, width - 2 : width - 1]
        col_left[KEPT + 2, 7:8, main_lanes] = own[4, 0:1]
        col_right[POPS + 2, 7:8, main_lanes] = after[4, 1:2]
        col_right[KEPT + 1, 7:8, main_lanes] = own[3, width - 1 : width]

    for is_left, col, rim in ((True, col_left, rim_left), (False, col_right, rim_right)):
        moving = forward_z if is_left else backward_z
        for domain, lanes in enumerate((pre_lanes, main_lanes)):
            tall = masks_for(domain, 16)
            new = []
            for pop in range(POPS):
                step_x, step_y, step_z = velocities[pop]
                if step_z == 0:
                    at = pop
                elif pop in moving:
                    at = POPS + moving.index(pop)
                else:
                    at = KEPT + (backward_z if is_left else forward_z).index(pop)
                source = shift_layers(col[at, 7 - step_x : 23 - step_x, lanes], step_y)
                new.append(
                    jnp.where(tall[step_y] != 0, col[opposite[pop], 7:23, lanes], source)
                )
            out = collide(new, moving)
            for k in range(5):
                rim[k, :, lanes] = out[moving[k]]

    stars = (star_pre, star_main)
    nexts = (next_pre, next_main)

    def base_of(domain, lanes):
        def base(pop, x_at):
            if 0 <= x_at < rows:
                return stars[domain][pop, x_at]
            if x_at == -1:
                if domain == 1 and pop in incoming:
                    return in_low[incoming.index(pop)]
                return x_low[pop, :, lanes]
            if x_at == rows:
                if domain == 1 and pop in backward_x:
                    return in_high[backward_x.index(pop)]
                return x_high[pop, :, lanes]
            if x_at < 0:
                return x_low[POPS + incoming.index(pop), :, lanes]
            return x_high[POPS + backward_x.index(pop), :, lanes]

        return base

    for x_at in range(-1, rows + 1):
        for domain, lanes in enumerate((pre_lanes, main_lanes)):
            new = moved_row(
                base_of(domain, lanes),
                lambda pop, at: col_left[pop, 8 + at : 9 + at, lanes],
                lambda pop, at: col_right[pop, 8 + at : 9 + at, lanes],
                masks_for(domain),
                x_at,
            )
            wanted = range(POPS)
            if x_at == -1:
                wanted = incoming
            elif x_at == rows:
                wanted = backward_x
            out = collide(new, wanted)
            for pop in wanted:
                nexts[domain][pop, x_at + 1] = out[pop]

    @pl.when(is_first)
    def _():
        for k in range(5):
            next_main[incoming[k], 0] = inflow[1, 1, k]
        rim_left[1, 0:1, main_lanes] = inflow[1, 0, 3, width - 1 : width]
        rim_right[2, 0:1, main_lanes] = inflow[1, 2, 4, 0:1]

    @pl.when(is_last)
    def _():
        for k in range(5):
            next_main[backward_x[k], rows + 1] = next_main[backward_x[k], rows]
            for rim in (rim_left, rim_right):
                rim[k, rows + 1 : rows + 2, main_lanes] = rim[k, rows : rows + 1, main_lanes]

    for x_at in range(rows):
        for domain, lanes in enumerate((pre_lanes, main_lanes)):
            new = moved_row(
                lambda pop, at: nexts[domain][pop, at + 1],
                lambda pop, at: rim_left[forward_z.index(pop), at + 1 : at + 2, lanes],
                lambda pop, at: rim_right[backward_z.index(pop), at + 1 : at + 2, lanes],
                masks_for(domain),
                x_at,
            )
            for pop in range(POPS):
                (out_pre, out_main)[domain][pop, x_at] = new[pop]


def f32(*shape):
    return jax.ShapeDtypeStruct(shape, jnp.float32)


def local(pre_pops, main_pops, tile_map, layer_phase, wall_flags):
    span_count = lax.axis_size("span")
    stream_count = lax.axis_size("stream")
    _, rows, width, coarse = pre_pops.shape
    fine = main_pops.shape[3]
    lanes = coarse + fine

    def send(value, step_x, place, only=None):
        moves = []
        for s in range(stream_count):
            if only is not None and s != only:
                continue
            for j in range(span_count):
                target = (s + step_x) % stream_count * span_count + place(j) % span_count
                moves.append((s * span_count + j, target))
        return lax.ppermute(value, ("stream", "span"), moves)

    stay = lambda j: j
    sibling = lambda j: j + 1 if j % 2 == 0 else j - 1
    beyond = lambda j: j - 1 if j % 2 == 0 else j + 1
    params = pltpu.CompilerParams(vmem_limit_bytes=VMEM_SMALL)

    star_pre, star_main, x_hi, x_lo, z_same, z_cross, x_small = pl.pallas_call(
        first_kernel,
        out_shape=(
            f32(*pre_pops.shape),
            f32(*main_pops.shape),
            f32(KEPT, width, lanes),
            f32(KEPT, width, lanes),
            f32(KEPT, rows, lanes),
            f32(KEPT, rows, lanes),
            f32(5, width, coarse),
        ),
        compiler_params=params,
        name="collide_and_pack",
    )(pre_pops, main_pops)

    beside = send(x_small, -1, stay, only=1 % stream_count)
    same = send(z_same, 0, sibling)
    cross = send(z_cross, 0, beyond)
    x_low = send(x_hi, 1, stay)
    x_high = send(x_lo, -1, stay)
    c_hi, c_lo = pl.pallas_call(
        corner_kernel,
        out_shape=(f32(2, 32, lanes), f32(2, 32, lanes)),
        compiler_params=params,
        name="corners",
    )(same, cross)
    c_low = send(c_hi, 1, stay)
    c_high = send(c_lo, -1, stay)
    plane = jnp.concatenate([x_hi[:, :, :coarse], beside], axis=0)
    tiles = lax.all_gather(plane, "span", axis=0, tiled=False)

    whole = pl.BlockSpec(memory_space=pltpu.VMEM)
    scalars = pl.BlockSpec(memory_space=pltpu.SMEM)
    return pl.pallas_call(
        second_kernel,
        out_shape=(f32(*pre_pops.shape), f32(*main_pops.shape)),
        in_specs=[scalars, scalars] + [whole] * 12,
        scratch_shapes=[
            pltpu.VMEM((KEPT + 5, 24, lanes), jnp.float32),
            pltpu.VMEM((KEPT + 5, 24, lanes), jnp.float32),
            pltpu.VMEM((5, width, fine), jnp.float32),
            pltpu.VMEM((5, width, fine), jnp.float32),
            pltpu.VMEM((3, 8, coarse), jnp.float32),
            pltpu.VMEM((3, 8, fine), jnp.float32),
            pltpu.VMEM((2, 3, 5, width, fine), jnp.float32),
            pltpu.VMEM((POPS, rows + 2, width, coarse), jnp.float32),
            pltpu.VMEM((POPS, rows + 2, width, fine), jnp.float32),
            pltpu.VMEM((5, 16, lanes), jnp.float32),
            pltpu.VMEM((5, 16, lanes), jnp.float32),
        ],
        compiler_params=pltpu.CompilerParams(vmem_limit_bytes=VMEM_LARGE),
        name="two_steps",
    )(
        tile_map,
        layer_phase,
        wall_flags.reshape(1, fine),
        star_pre,
        star_main,
        x_low,
        x_high,
        same,
        cross,
        z_same,
        z_cross,
        c_low,
        c_high,
        tiles,
    )


def solution(mesh):
    return jax.shard_map(
        local,
        mesh=mesh,
        in_specs=(P(None, "stream", "span", None), P(None, "stream", "span", None), P(), P(), P()),
        out_specs=(P(None, "stream", "span", None), P(None, "stream", "span", None)),
        check_vma=False,
    )
```

```python
import jax
import jax.numpy as jnp
from jax import lax
from jax.experimental import pallas as pl
from jax.experimental.pallas import tpu as pltpu
from jax.sharding import PartitionSpec as P

velocities = (
    (0, 0, 0),
    (1, 0, 0),
    (-1, 0, 0),
    (0, 1, 0),
    (0, -1, 0),
    (0, 0, 1),
    (0, 0, -1),
    (1, 1, 0),
    (-1, -1, 0),
    (1, -1, 0),
    (-1, 1, 0),
    (1, 0, 1),
    (-1, 0, -1),
    (1, 0, -1),
    (-1, 0, 1),
    (0, 1, 1),
    (0, -1, -1),
    (0, 1, -1),
    (0, -1, 1),
)
opposite = (0, 2, 1, 4, 3, 6, 5, 8, 7, 10, 9, 12, 11, 14, 13, 16, 15, 18, 17)
pairs = tuple((k, k + 1) for k in range(1, 19, 2))
incoming = (1, 7, 9, 11, 13)
backward_x = (2, 8, 10, 12, 14)
forward_z = (5, 11, 14, 15, 18)
backward_z = (6, 12, 13, 16, 17)
POPS = 19
PLANE = 16
FACE = 13
SIDE = 16
stays_x = tuple(k for k in range(POPS) if velocities[k][0] == 0)
KEPT = POPS + 5
VMEM_SMALL = 10 * 1024 * 1024
VMEM_LARGE = 20 * 1024 * 1024


def moments_of(pops):
    density = None
    moment = [None, None, None]

    def add(total, value):
        return value if total is None else total + value

    for group, weight in ((range(1, 7), 1.0 / 18.0), (range(7, POPS), 1.0 / 36.0)):
        part = None
        parts = [None, None, None]
        for a, b in ((k, k + 1) for k in group[::2]):
            if pops[a] is None and pops[b] is None:
                continue
            if pops[b] is None:
                both, diff = pops[a], pops[a]
            elif pops[a] is None:
                both, diff = pops[b], -pops[b]
            else:
                both, diff = pops[a] + pops[b], pops[a] - pops[b]
            part = add(part, both)
            for axis_num, step in enumerate(velocities[a]):
                if step != 0:
                    parts[axis_num] = add(parts[axis_num], diff if step == 1 else -diff)
        if part is not None:
            density = add(density, part * weight)
        for axis_num in range(3):
            if parts[axis_num] is not None:
                moment[axis_num] = add(moment[axis_num], parts[axis_num] * weight)
    if pops[0] is not None:
        density = add(density, pops[0] * (1.0 / 3.0))
    return density, moment


def relax(pops, density, moment, wanted):
    inverse = 1.0 / density
    speed = [component * inverse for component in moment]
    kinetic = moment[0] * speed[0] + moment[1] * speed[1] + moment[2] * speed[2]
    base = 1.25 * density - 1.875 * kinetic
    result = [None] * POPS
    if 0 in wanted:
        result[0] = base - 0.25 * pops[0]
    for a, b in pairs:
        if a not in wanted and b not in wanted:
            continue
        flux = None
        along = None
        for axis_num, step in enumerate(velocities[a]):
            if step == 0:
                continue
            if flux is None:
                flux, along = moment[axis_num], speed[axis_num]
            elif step == 1:
                flux, along = flux + moment[axis_num], along + speed[axis_num]
            else:
                flux, along = flux - moment[axis_num], along - speed[axis_num]
        even = base + 5.625 * (flux * along)
        odd = 3.75 * flux
        if a in wanted:
            result[a] = even + odd - 0.25 * pops[a]
        if b in wanted:
            result[b] = even - odd - 0.25 * pops[b]
    return result


def collide(pops, wanted=range(POPS)):
    density, moment = moments_of(pops)
    return relax(pops, density, moment, wanted)


def shift_layers(value, step_y):
    if step_y == 0:
        return value
    size = value.shape[-1]
    return pltpu.roll(value, step_y % size, value.ndim - 1)


def moved_row(base, left, right, masks, x_at, wanted=range(POPS)):
    result = []
    sub = None
    for which_pop in range(POPS):
        if which_pop not in wanted:
            result.append(None)
            continue
        step_x, step_y, step_z = velocities[which_pop]
        source = base(which_pop, x_at - step_x)
        if step_z != 0 and sub is None:
            sub = lax.broadcasted_iota(jnp.int32, source.shape, 0)
        width = source.shape[0]
        if step_z == 1:
            source = jnp.where(
                sub == 0, left(which_pop, x_at - step_x), pltpu.roll(source, 1, 0)
            )
        elif step_z == -1:
            source = jnp.where(
                sub == width - 1,
                right(which_pop, x_at - step_x),
                pltpu.roll(source, width - 1, 0),
            )
        source = shift_layers(source, step_y)
        result.append(
            jnp.where(masks[step_y] != 0, base(opposite[which_pop], x_at), source)
        )
    return result


def fill_masks(walls, masks):
    fine = walls.shape[1]
    coarse = masks.shape[2] - fine

    def fill(solid, lanes):
        layers = solid.shape[1]
        lane = lax.broadcasted_iota(jnp.int32, solid.shape, 1)
        masks[0, :, lanes] = solid
        masks[1, :, lanes] = jnp.where(lane == 0, 1.0, pltpu.roll(solid, 1, 1))
        masks[2, :, lanes] = jnp.where(lane == layers - 1, 1.0, pltpu.roll(solid, layers - 1, 1))

    solid = jnp.broadcast_to(jnp.where(walls[...] > 0, 1.0, 0.0), (8, fine))
    fine_at = lax.broadcasted_iota(jnp.int32, (fine, coarse), 0)
    coarse_at = lax.broadcasted_iota(jnp.int32, (fine, coarse), 1)
    halves = jnp.where(lax.shift_right_logical(fine_at, 1) == coarse_at, 1.0, 0.0)
    hits = jnp.dot(solid, halves, preferred_element_type=jnp.float32)
    fill(jnp.where(hits > 0.5, 1.0, 0.0), slice(0, coarse))
    fill(solid, slice(coarse, coarse + fine))


def first_kernel(
    pre,
    main,
    star_pre,
    star_main,
    z_same,
    z_cross,
):
    rows = pre.shape[1]
    coarse = pre.shape[3]
    parity = lax.rem(lax.axis_index("span"), 2)
    domains = ((pre, star_pre, slice(0, coarse)), (main, star_main, slice(coarse, None)))
    for x_at in range(rows):
        for pops, star, lanes in domains:
            out = collide([pops[which_pop, x_at] for which_pop in range(POPS)])
            for which_pop in range(POPS):
                star[which_pop, x_at] = out[which_pop]

    def edges(hi, lo):
        for _, star, lanes in domains:
            width = star.shape[2]
            for which_pop in range(POPS):
                hi[which_pop, :, lanes] = star[which_pop, :, width - 1, :]
                lo[which_pop, :, lanes] = star[which_pop, :, 0, :]
            for k in range(5):
                hi[POPS + k, :, lanes] = star[forward_z[k], :, width - 2, :]
                lo[POPS + k, :, lanes] = star[backward_z[k], :, 1, :]

    @pl.when(parity == 0)
    def _():
        edges(z_same, z_cross)

    @pl.when(parity == 1)
    def _():
        edges(z_cross, z_same)


def fill_face(star, lanes, blocked, at_top, face):
    last = star.shape[1] - 1
    moving = incoming if at_top else backward_x
    rim = last if at_top else 0
    none = lambda pop, x_at: 0.0
    base = lambda pop, x_at: star[pop, x_at]
    new = moved_row(base, none, none, blocked, rim, moving + stays_x)
    for k, pop in enumerate(moving):
        face[k, :, lanes] = star[pop, rim]
        face[5 + k, :, lanes] = new[pop]
        new[pop] = None
    density, moment = moments_of(new)
    face[10, :, lanes] = density
    face[11, :, lanes] = moment[1]
    face[12, :, lanes] = moment[2]


def face_kernel(walls, star_pre, star_main, masks, x_hi, x_lo, plane):
    coarse = star_pre.shape[3]
    fill_masks(walls, masks)
    for star, lanes in zip((star_pre, star_main), lanes_of(coarse, star_main.shape[3])):
        blocked = masks_of(masks, lanes)
        fill_face(star, lanes, blocked, True, x_hi)
        fill_face(star, lanes, blocked, False, x_lo)
    fill_plane(star_pre, masks_of(masks, slice(0, coarse)), plane)


def fill_plane(star, blocked, plane):
    width, coarse = plane.shape[1:]
    last = star.shape[1] - 1
    zero = jnp.zeros((width, coarse), jnp.float32)
    stream_pos = lax.axis_index("stream")

    @pl.when(stream_pos != 1)
    def _():
        base = lambda pop, x_at: zero if x_at > last else star[pop, x_at]
        none = lambda pop, x_at: 0.0
        new = moved_row(base, none, none, blocked, last)
        density, moment = moments_of(new)
        for k, pop in enumerate(incoming):
            plane[k] = star[pop, last]
            plane[5 + k] = new[pop]
        plane[10] = density
        for axis_num in range(3):
            plane[11 + axis_num] = moment[axis_num]
        plane[14] = zero
        plane[15] = zero
        for k in range(5):
            hi, lo = forward_z[k], backward_z[k]
            plane[14, k : k + 1, :] = base(hi, last - velocities[hi][0])[width - 1 : width]
            plane[15, k : k + 1, :] = base(lo, last - velocities[lo][0])[0:1]

    @pl.when(stream_pos == 1)
    def _():
        none = lambda pop, x_at: 0.0
        back = moved_row(
            lambda pop, x_at: star[pop, x_at] if pop in backward_x else zero,
            none,
            none,
            blocked,
            -1,
            backward_x,
        )
        density, moment = moments_of(back)
        for k, value in enumerate([density] + moment):
            plane[k] = value
        for k in range(4, PLANE):
            plane[k] = zero
        plane[14, 1:2, :] = star[14, 0, width - 1 : width, :]
        plane[15, 1:2, :] = star[12, 0, 0:1, :]


def column_values(is_left, first, second, inner, shift, blocked):
    inward, outward = (forward_z, backward_z) if is_left else (backward_z, forward_z)
    result = []
    for pop in range(POPS):
        step_x, step_y, _ = velocities[pop]
        if pop in inward:
            source = shift(second, inward.index(pop), step_x)
        elif pop in outward:
            source = shift(inner, outward.index(pop), step_x)
        else:
            source = shift(first, pop, step_x)
        result.append(
            jnp.where(blocked[step_y] != 0, first(opposite[pop]), shift_layers(source, step_y))
        )
    return result


def turned(read, at, step_x):
    value = read(at)
    return value if step_x == 0 else pltpu.roll(value, step_x % value.shape[0], 0)


def only(pops, values):
    return [values[pop] if pop in pops else None for pop in range(POPS)]


def corner_lines(is_left, side, halo, edge, masks, lanes, c_hi, c_lo):
    inward, outward = (forward_z, backward_z) if is_left else (backward_z, forward_z)
    last = halo.shape[1] - 1
    new = column_values(
        is_left,
        lambda pop: halo[pop, :, lanes],
        lambda k: halo[POPS + k, :, lanes],
        lambda k: edge[outward[k], :, lanes],
        turned,
        masks_of(masks, lanes),
    )
    for target, moving, rim, inner in ((c_hi, incoming, last, last - 1), (c_lo, backward_x, 0, 1)):
        turning = [pop for pop in moving if pop in inward][0]
        density, moment = moments_of(only(moving + stays_x, new))
        lines = [halo[pop, rim : rim + 1, lanes] for pop in moving]
        lines += [halo[pop, rim : rim + 1, lanes] for pop in inward if pop in stays_x]
        lines += [halo[turning, inner : inner + 1, lanes]]
        lines += [halo[POPS + inward.index(turning), rim : rim + 1, lanes]]
        lines += [value[rim : rim + 1] for value in [density] + moment + [new[turning]]]
        for k, line in enumerate(lines):
            target[side + k : side + k + 1, lanes] = line


def corner_kernel(
    tile_map, masks, same, cross, edge_same, edge_cross, tiles_hbm, c_hi, c_lo, tiles, arrived
):
    lanes_all = masks.shape[2]
    coarse = tiles.shape[3]
    parity = lax.rem(lax.axis_index("span"), 2)
    on_relay = lax.axis_index("stream") == 1
    copy = pltpu.make_async_copy(tiles_hbm, tiles, arrived)

    @pl.when(on_relay)
    def _():
        copy.start()

    for lanes in lanes_of(coarse, lanes_all - coarse):

        @pl.when(parity == 0)
        def _():
            corner_lines(True, SIDE, cross, edge_cross, masks, lanes, c_hi, c_lo)
            corner_lines(False, 0, same, edge_same, masks, lanes, c_hi, c_lo)

        @pl.when(parity == 1)
        def _():
            corner_lines(True, 0, same, edge_same, masks, lanes, c_hi, c_lo)
            corner_lines(False, SIDE, cross, edge_cross, masks, lanes, c_hi, c_lo)

    @pl.when(on_relay)
    def _():
        copy.wait()
        span_pos = lax.axis_index("span")
        span_count = lax.axis_size("span")
        width = tiles.shape[2]
        sub = lax.broadcasted_iota(jnp.int32, (width, coarse), 0)
        open_layers = masks[0, :, :coarse] == 0
        for at, offset in enumerate((span_count - 1, 0, 1)):
            tile = tile_map[lax.rem(span_pos + offset, span_count)]
            edges = [None] * POPS
            for pop, side, row, slot in ((14, span_count - 1, 0, 14), (12, 1, width - 1, 15)):
                line = tiles[lax.rem(tile + side, span_count), slot, 1:2, :]
                line = jnp.broadcast_to(line, (width, coarse))
                edges[pop] = jnp.where((sub == row) & open_layers, line, 0.0)
            density, moment = moments_of(edges)
            lanes = slice(at * coarse, (at + 1) * coarse)
            base = 2 * SIDE
            c_lo[base : base + 8, lanes] = tiles[tile, 0] + density
            c_lo[base + 8 : base + 16, lanes] = tiles[tile, 2]
            c_lo[base + 16 : base + 24, lanes] = tiles[tile, 3] + moment[2]


def build_columns(is_left, col, corner, halo, edge, side, x_low, x_high, c_low, c_high):
    inward, outward = (forward_z, backward_z) if is_left else (backward_z, forward_z)
    rim = 0 if is_left else x_low.shape[1] - 1
    for k in range(KEPT):
        col[k, 8:16, :] = halo[k]
    for k in range(5):
        col[KEPT + k, 8:16, :] = edge[outward[k]]
    corner[...] = jnp.zeros(corner.shape, jnp.float32)
    for moving, face, lines, near, beyond, row in (
        (incoming, x_low, c_low, 7, 6, 0),
        (backward_x, x_high, c_high, 16, 17, 9),
    ):
        line = lambda k: lines[side + k : side + k + 1, :]
        for k in range(5):
            col[moving[k], near : near + 1, :] = line(k)
        for k, pop in enumerate([pop for pop in inward if pop in stays_x]):
            col[pop, near : near + 1, :] = line(5 + k)
        turning = [pop for pop in moving if pop in inward][0]
        leaving = [pop for pop in moving if pop in outward][0]
        col[turning, beyond : beyond + 1, :] = line(8)
        at = POPS + inward.index(turning)
        col[at, near : near + 1, :] = line(9)
        at = KEPT + outward.index(leaving)
        col[at, near : near + 1, :] = face[moving.index(leaving), rim : rim + 1, :]
        for k in range(4):
            corner[k, row : row + 1, :] = line(10 + k)
        at = 4 if moving is incoming else 5
        corner[at, row : row + 1, :] = line(14)


def refine(coarse, phases, fine_len):
    coarse_len = coarse.shape[1]
    count = coarse.shape[0] // 3
    rows = lax.broadcasted_iota(jnp.int32, (coarse_len, fine_len), 0)
    fine = lax.broadcasted_iota(jnp.int32, (coarse_len, fine_len), 1)
    outs = []
    for phase in (0, 1):
        position = fine + phase
        lower = lax.shift_right_arithmetic(position - 1, 1)
        upper_wt = jnp.where(position % 2 == 0, 0.75, 0.25)
        low_idx = jnp.clip(lower, 0, coarse_len - 1)
        high_idx = jnp.clip(lower + 1, 0, coarse_len - 1)
        matrix = jnp.where(rows == low_idx, 1.0 - upper_wt, 0.0) + jnp.where(
            rows == high_idx, upper_wt, 0.0
        )
        outs.append(
            jnp.dot(
                coarse,
                matrix,
                precision=lax.Precision.HIGHEST,
                preferred_element_type=jnp.float32,
            )
        )
    return [
        jnp.where(
            phases[tile] > 0,
            outs[1][tile * count : (tile + 1) * count],
            outs[0][tile * count : (tile + 1) * count],
        )
        for tile in range(3)
    ]


def lanes_of(coarse, fine):
    return slice(0, coarse), slice(coarse, coarse + fine)


def masks_of(masks, lanes, height=8):
    values = {step: masks[step % 3, :, lanes] for step in (0, 1, -1)}
    if height == 8:
        return values
    return {
        step: jnp.broadcast_to(value[:1], (height, value.shape[1]))
        for step, value in values.items()
    }


def middle_kernel(
    tile_map,
    layer_phase,
    masks,
    star_pre,
    star_main,
    same,
    cross,
    edge_same,
    edge_cross,
    tiles_hbm,
    mid_pre,
    mid_main,
    inflow,
    awaited,
    out_pre_hbm,
    out_main_hbm,
    ghost_left,
    ghost_right,
    rim_left,
    rim_right,
    out_pre,
    out_main,
    tiles,
    arrived,
    sent,
):
    rows, width, coarse = star_pre.shape[1:]
    fine = star_main.shape[3]
    span_pos = lax.axis_index("span")
    span_count = lax.axis_size("span")
    parity = lax.rem(span_pos, 2)

    on_inlet = lax.axis_index("stream") == 0
    copy = pltpu.make_async_copy(tiles_hbm, tiles, arrived)

    @pl.when(on_inlet)
    def _():
        copy.start()

    def ghosts(is_left, ghost, halo, edge, rim):
        inward, outward = (forward_z, backward_z) if is_left else (backward_z, forward_z)
        for k in range(5):
            ghost[k] = halo[inward[k]]
        for lanes in lanes_of(coarse, fine):
            new = column_values(
                is_left,
                lambda pop: halo[pop, :, lanes],
                lambda k: halo[POPS + k, :, lanes],
                lambda k: edge[outward[k], :, lanes],
                turned,
                masks_of(masks, lanes),
            )
            out = collide(new, inward)
            for k in range(5):
                rim[k, :, lanes] = out[inward[k]]

    @pl.when(parity == 0)
    def _():
        ghosts(True, ghost_left, cross, edge_cross, rim_left)
        ghosts(False, ghost_right, same, edge_same, rim_right)

    @pl.when(parity == 1)
    def _():
        ghosts(True, ghost_left, same, edge_same, rim_left)
        ghosts(False, ghost_right, cross, edge_cross, rim_right)

    stars = (star_pre, star_main)
    for x_at in range(1, rows - 1):
        for domain, lanes in enumerate(lanes_of(coarse, fine)):
            new = moved_row(
                lambda pop, at: stars[domain][pop, at],
                lambda pop, at: ghost_left[forward_z.index(pop), at : at + 1, lanes],
                lambda pop, at: ghost_right[backward_z.index(pop), at : at + 1, lanes],
                masks_of(masks, lanes),
                x_at,
            )
            out = collide(new)
            for pop in range(POPS):
                (mid_pre, mid_main)[domain][pop, x_at - 1] = out[pop]

    copies = []
    for x_at in range(2, rows - 2):
        for domain, lanes in enumerate(lanes_of(coarse, fine)):
            new = moved_row(
                lambda pop, at: (mid_pre, mid_main)[domain][pop, at - 1],
                lambda pop, at: rim_left[forward_z.index(pop), at : at + 1, lanes],
                lambda pop, at: rim_right[backward_z.index(pop), at : at + 1, lanes],
                masks_of(masks, lanes),
                x_at,
            )
            kept = (out_pre, out_main)[domain]
            for pop in range(POPS):
                kept[pop, x_at - 2] = new[pop]
            copies.append(
                pltpu.make_async_copy(
                    kept.at[:, x_at - 2],
                    (out_pre_hbm, out_main_hbm)[domain].at[:, x_at],
                    sent.at[domain, x_at - 2],
                )
            )
            copies[-1].start()

    @pl.when(on_inlet)
    def _():
        copy.wait()
        chosen, phases = [], []
        for offset in (span_count - 1, 0, 1):
            at = lax.rem(span_pos + offset, span_count)
            chosen.append(tile_map[at])
            phases.append(layer_phase[at])

        planes = [[tiles[tile, k] for k in range(5)] for tile in chosen]
        blocked = masks_of(masks, slice(0, coarse))
        sub = lax.broadcasted_iota(jnp.int32, (width, coarse), 0)
        for place, tile in enumerate(chosen):
            edges = [None] * POPS
            for k in range(5):
                for pop, at, row, slot in (
                    (forward_z[k], span_count - 1, 0, 14),
                    (backward_z[k], 1, width - 1, 15),
                ):
                    line = tiles[lax.rem(tile + at, span_count), slot, k : k + 1, :]
                    line = shift_layers(jnp.broadcast_to(line, (width, coarse)), velocities[pop][1])
                    keep = (sub == row) & (blocked[velocities[pop][1]] == 0)
                    edges[pop] = jnp.where(keep, line, 0.0)
            density, moment = moments_of(edges)
            density = density + tiles[tile, 10]
            moment = [moment[axis_num] + tiles[tile, 11 + axis_num] for axis_num in range(3)]
            for k, value in enumerate([density] + moment):
                awaited[place, k] = value
            for k, pop in enumerate(incoming):
                new = tiles[tile, 5 + k]
                if edges[pop] is not None:
                    new = new + edges[pop]
                awaited[place, 4 + k] = new
        stacked = jnp.concatenate([plane for group in planes for plane in group], axis=0)
        for place, value in enumerate(refine(stacked, phases, fine)):
            inflow[place] = value.reshape(5, width, fine)

    for copy_out in copies:
        copy_out.wait()


def last_kernel(
    layer_phase,
    masks,
    star_pre,
    star_main,
    mid_pre,
    mid_main,
    inflow,
    awaited,
    x_low,
    x_high,
    same,
    cross,
    edge_same,
    edge_cross,
    c_low,
    c_high,
    part_pre,
    part_main,
    out_pre_hbm,
    out_main_hbm,
    col_left,
    col_right,
    corner_left,
    corner_right,
    in_low,
    in_high,
    next_pre,
    next_main,
    rim_left,
    rim_right,
    out_pre,
    out_main,
    sent,
):
    rows, width, coarse = star_pre.shape[1:]
    fine = star_main.shape[3]
    pre_lanes, main_lanes = lanes_of(coarse, fine)
    is_first = lax.axis_index("stream") == 0
    is_last = lax.axis_index("stream") == lax.axis_size("stream") - 1
    parity = lax.rem(lax.axis_index("span"), 2)
    ends = (x_low, x_high, c_low, c_high)

    @pl.when(parity == 0)
    def _():
        build_columns(True, col_left, corner_left, cross, edge_cross, SIDE, *ends)
        build_columns(False, col_right, corner_right, same, edge_same, 0, *ends)

    @pl.when(parity == 1)
    def _():
        build_columns(True, col_left, corner_left, same, edge_same, 0, *ends)
        build_columns(False, col_right, corner_right, cross, edge_cross, SIDE, *ends)

    for k in range(5):
        in_low[k] = x_low[k, :, main_lanes]
        in_high[k] = x_high[k, :, main_lanes]

    @pl.when(is_last)
    def _():
        for k in range(5):
            in_high[k] = star_main[backward_x[k], rows - 1]
        for col in (col_left, col_right):
            for k in range(KEPT + 5):
                col[k, 16:17, main_lanes] = col[k, 15:16, main_lanes]

    @pl.when(is_first)
    def _():
        before, own, after = (inflow.at[tile] for tile in range(3))
        for k in range(5):
            in_low[k] = own[k]
            col_left[incoming[k], 7:8, main_lanes] = before[k, width - 1 : width]
            col_right[incoming[k], 7:8, main_lanes] = after[k, 0:1]
        col_left[POPS + 1, 7:8, main_lanes] = before[3, width - 2 : width - 1]
        col_left[KEPT + 2, 7:8, main_lanes] = own[4, 0:1]
        col_right[POPS + 2, 7:8, main_lanes] = after[4, 1:2]
        col_right[KEPT + 1, 7:8, main_lanes] = own[3, width - 1 : width]

    for is_left, col, corner, rim in (
        (True, col_left, corner_left, rim_left),
        (False, col_right, corner_right, rim_right),
    ):
        moving = forward_z if is_left else backward_z
        for lanes in (pre_lanes, main_lanes):
            new = column_values(
                is_left,
                lambda pop, step_x=0: col[pop, 7 - step_x : 23 - step_x, lanes],
                lambda k, step_x: col[POPS + k, 7 - step_x : 23 - step_x, lanes],
                lambda k, step_x: col[KEPT + k, 7 - step_x : 23 - step_x, lanes],
                lambda read, at, step_x: read(at, step_x),
                masks_of(masks, lanes, 16),
            )
            row = lax.broadcasted_iota(jnp.int32, new[0].shape, 0)
            for pop in range(POPS):
                if pop not in backward_x:
                    new[pop] = jnp.where(row == 0, 0.0, new[pop])
                if pop not in incoming:
                    new[pop] = jnp.where(row == rows + 1, 0.0, new[pop])
            density, moment = moments_of(new)
            density = density + corner[0, :, lanes]
            moment = [moment[axis_num] + corner[1 + axis_num, :, lanes] for axis_num in range(3)]
            for at, ends_of in ((4, incoming), (5, backward_x)):
                pop = [pop for pop in moving if pop in ends_of][0]
                new[pop] = new[pop] + corner[at, :, lanes]
            out = relax(new, density, moment, moving)
            for k in range(5):
                rim[k, :, lanes] = out[moving[k]]

    stars = (star_pre, star_main)
    outer = {-1: 0, 0: 1, rows - 1: 2, rows: 3}

    def base_of(domain, lanes):
        def base(pop, x_at):
            if 0 <= x_at < rows:
                return stars[domain][pop, x_at]
            if x_at == -1:
                k = incoming.index(pop)
                return in_low[k] if domain == 1 else x_low[k, :, lanes]
            k = backward_x.index(pop)
            return in_high[k] if domain == 1 else x_high[k, :, lanes]

        return base

    def beside_tile(domain, lanes, x_at):
        star = stars[domain]
        face, moving, back = (
            (x_low, incoming, backward_x) if x_at < 0 else (x_high, backward_x, incoming)
        )
        blocked = masks_of(masks, lanes)
        left = lambda pop, at: col_left[pop, 8 + at : 9 + at, lanes]
        right = lambda pop, at: col_right[pop, 8 + at : 9 + at, lanes]

        def base(pop, at):
            return face[moving.index(pop), :, lanes] if at == x_at else star[pop, at]

        new = moved_row(base, left, right, blocked, x_at, back)
        sub = lax.broadcasted_iota(jnp.int32, new[back[0]].shape, 0)
        for pop in range(POPS):
            if pop in back:
                continue
            step_x, step_y, step_z = velocities[pop]
            if step_z != 0:
                line = (left if step_z == 1 else right)(pop, x_at - step_x)
                line = shift_layers(jnp.broadcast_to(line, sub.shape), step_y)
                keep = (sub == (0 if step_z == 1 else width - 1)) & (blocked[step_y] == 0)
                new[pop] = jnp.where(keep, line, 0.0)
            if pop in moving:
                part = face[5 + moving.index(pop), :, lanes]
                new[pop] = part if new[pop] is None else part + new[pop]
        density, moment = moments_of(new)
        density = density + face[10, :, lanes]
        moment = [moment[0], moment[1] + face[11, :, lanes], moment[2] + face[12, :, lanes]]
        return relax(new, density, moment, moving), moving

    for x_at in outer:
        for domain, lanes in enumerate((pre_lanes, main_lanes)):
            if 0 <= x_at < rows:
                new = moved_row(
                    base_of(domain, lanes),
                    lambda pop, at: col_left[pop, 8 + at : 9 + at, lanes],
                    lambda pop, at: col_right[pop, 8 + at : 9 + at, lanes],
                    masks_of(masks, lanes),
                    x_at,
                )
                out, wanted = collide(new), range(POPS)
            else:
                out, wanted = beside_tile(domain, lanes, x_at)
            for pop in wanted:
                (next_pre, next_main)[domain][pop, outer[x_at]] = out[pop]

    @pl.when(is_first)
    def _():
        span_pos, span_count = lax.axis_index("span"), lax.axis_size("span")
        phases, planes = [], []
        for place, offset in enumerate((span_count - 1, 0, 1)):
            phases.append(layer_phase[lax.rem(span_pos + offset, span_count)])
            lanes = slice(place * coarse, (place + 1) * coarse)
            base = 2 * SIDE
            back = c_high[base : base + 8, lanes]
            density = awaited[place, 0] + back
            moment = [
                awaited[place, 1] - back,
                awaited[place, 2] + c_high[base + 8 : base + 16, lanes],
                awaited[place, 3] + c_high[base + 16 : base + 24, lanes],
            ]
            new = [None] * POPS
            for k, pop in enumerate(incoming):
                new[pop] = awaited[place, 4 + k]
            out = relax(new, density, moment, incoming)
            planes += [out[pop] for pop in incoming]
        before, own, after = (
            value.reshape(5, width, fine)
            for value in refine(jnp.concatenate(planes, axis=0), phases, fine)
        )
        for k in range(5):
            next_main[incoming[k], 0] = own[k]
        rim_left[1, 0:1, main_lanes] = before[3, width - 1 : width]
        rim_right[2, 0:1, main_lanes] = after[4, 0:1]

    @pl.when(is_last)
    def _():
        for k in range(5):
            next_main[backward_x[k], 3] = next_main[backward_x[k], 2]
            for rim in (rim_left, rim_right):
                rim[k, rows + 1 : rows + 2, main_lanes] = rim[k, rows : rows + 1, main_lanes]

    def next_of(domain):
        def base(pop, x_at):
            if x_at in outer:
                return (next_pre, next_main)[domain][pop, outer[x_at]]
            return (mid_pre, mid_main)[domain][pop, x_at - 1]

        return base

    copies = []
    for at_end, x_at in enumerate((0, 1, rows - 2, rows - 1)):
        for domain, lanes in enumerate((pre_lanes, main_lanes)):
            new = moved_row(
                next_of(domain),
                lambda pop, at: rim_left[forward_z.index(pop), at + 1 : at + 2, lanes],
                lambda pop, at: rim_right[backward_z.index(pop), at + 1 : at + 2, lanes],
                masks_of(masks, lanes),
                x_at,
            )
            kept = (out_pre, out_main)[domain]
            for pop in range(POPS):
                kept[pop, at_end] = new[pop]
            copy = pltpu.make_async_copy(
                kept.at[:, at_end],
                (out_pre_hbm, out_main_hbm)[domain].at[:, x_at],
                sent.at[domain, at_end],
            )
            copy.start()
            copies.append(copy)
    for copy in copies:
        copy.wait()


def f32(*shape):
    return jax.ShapeDtypeStruct(shape, jnp.float32)


def local(pre_pops, main_pops, tile_map, layer_phase, wall_flags):
    span_count = lax.axis_size("span")
    stream_count = lax.axis_size("stream")
    _, rows, width, coarse = pre_pops.shape
    fine = main_pops.shape[3]
    lanes = coarse + fine

    def send(value, step_x, place, only=range(stream_count)):
        moves = []
        for s in range(stream_count):
            if s not in only:
                continue
            for j in range(span_count):
                target = (s + step_x) % stream_count * span_count + place(j) % span_count
                moves.append((s * span_count + j, target))
        return lax.ppermute(value, ("stream", "span"), moves)

    stay = lambda j: j
    sibling = lambda j: j + 1 if j % 2 == 0 else j - 1
    beyond = lambda j: j - 1 if j % 2 == 0 else j + 1
    params = pltpu.CompilerParams(vmem_limit_bytes=VMEM_SMALL)

    whole = pl.BlockSpec(memory_space=pltpu.VMEM)
    outside = pl.BlockSpec(memory_space=pltpu.HBM)
    scalars = pl.BlockSpec(memory_space=pltpu.SMEM)

    star_pre, star_main, z_same, z_cross = pl.pallas_call(
        first_kernel,
        out_shape=(
            f32(*pre_pops.shape),
            f32(*main_pops.shape),
            f32(KEPT, rows, lanes),
            f32(KEPT, rows, lanes),
        ),
        compiler_params=params,
        name="collide_and_pack",
    )(pre_pops, main_pops)
    masks, x_hi, x_lo, plane = pl.pallas_call(
        face_kernel,
        out_shape=(
            f32(3, 8, lanes),
            f32(FACE, width, lanes),
            f32(FACE, width, lanes),
            f32(PLANE, width, coarse),
        ),
        compiler_params=params,
        name="faces",
    )(wall_flags.reshape(1, fine), star_pre, star_main)

    same = send(z_same, 0, sibling)
    cross = send(z_cross, 0, beyond)
    x_low = send(x_hi, 1, stay)
    x_high = send(x_lo, -1, stay)
    tiles = lax.all_gather(plane, "span", axis=0, tiled=False)
    anywhere = pl.BlockSpec(memory_space=pl.ANY)
    all_tiles = [
        pltpu.VMEM((span_count, PLANE, width, coarse), jnp.float32),
        pltpu.SemaphoreType.DMA,
    ]
    c_hi, c_lo = pl.pallas_call(
        corner_kernel,
        out_shape=(f32(2 * SIDE, lanes), f32(2 * SIDE + 24, lanes)),
        in_specs=[scalars] + [whole] * 5 + [anywhere],
        scratch_shapes=all_tiles,
        compiler_params=params,
        name="corners",
    )(tile_map, masks, same, cross, z_same, z_cross, tiles)
    c_low = send(c_hi, 1, stay)
    c_high = send(c_lo, -1, stay)
    half_pre = pltpu.VMEM((POPS, 4, width, coarse), jnp.float32)
    half_main = pltpu.VMEM((POPS, 4, width, fine), jnp.float32)
    mid_pre, mid_main, inflow, awaited, part_pre, part_main = pl.pallas_call(
        middle_kernel,
        out_shape=(
            f32(POPS, rows - 2, width, coarse),
            f32(POPS, rows - 2, width, fine),
            f32(3, 5, width, fine),
            f32(3, 9, width, coarse),
            f32(*pre_pops.shape),
            f32(*main_pops.shape),
        ),
        in_specs=[scalars, scalars] + [whole] * 7 + [anywhere],
        out_specs=[whole] * 4 + [outside] * 2,
        scratch_shapes=[
            pltpu.VMEM((5, rows, lanes), jnp.float32),
            pltpu.VMEM((5, rows, lanes), jnp.float32),
            pltpu.VMEM((5, rows, lanes), jnp.float32),
            pltpu.VMEM((5, rows, lanes), jnp.float32),
            pltpu.VMEM((POPS, rows - 4, width, coarse), jnp.float32),
            pltpu.VMEM((POPS, rows - 4, width, fine), jnp.float32),
        ]
        + all_tiles
        + [pltpu.SemaphoreType.DMA((2, rows - 4))],
        compiler_params=params,
        name="middle_rows",
    )(tile_map, layer_phase, masks, star_pre, star_main, same, cross, z_same, z_cross, tiles)
    return pl.pallas_call(
        last_kernel,
        out_shape=(f32(*pre_pops.shape), f32(*main_pops.shape)),
        in_specs=[scalars] + [whole] * 15 + [outside] * 2,
        out_specs=(outside, outside),
        input_output_aliases={16: 0, 17: 1},
        scratch_shapes=[
            pltpu.VMEM((KEPT + 5, 24, lanes), jnp.float32),
            pltpu.VMEM((KEPT + 5, 24, lanes), jnp.float32),
            pltpu.VMEM((6, 16, lanes), jnp.float32),
            pltpu.VMEM((6, 16, lanes), jnp.float32),
            pltpu.VMEM((5, width, fine), jnp.float32),
            pltpu.VMEM((5, width, fine), jnp.float32),
            half_pre,
            half_main,
            pltpu.VMEM((5, 16, lanes), jnp.float32),
            pltpu.VMEM((5, 16, lanes), jnp.float32),
            half_pre,
            half_main,
            pltpu.SemaphoreType.DMA((2, 4)),
        ],
        compiler_params=pltpu.CompilerParams(vmem_limit_bytes=VMEM_LARGE),
        name="last_rows",
    )(
        layer_phase,
        masks,
        star_pre,
        star_main,
        mid_pre,
        mid_main,
        inflow,
        awaited,
        x_low,
        x_high,
        same,
        cross,
        z_same,
        z_cross,
        c_low,
        c_high,
        part_pre,
        part_main,
    )


def solution(mesh):
    return jax.shard_map(
        local,
        mesh=mesh,
        in_specs=(P(None, "stream", "span", None), P(None, "stream", "span", None), P(), P(), P()),
        out_specs=(P(None, "stream", "span", None), P(None, "stream", "span", None)),
        check_vma=False,
    )
```

```python
import jax
import jax.numpy as jnp
from jax import lax
from jax.experimental import pallas as pl
from jax.experimental.pallas import tpu as pltpu
from jax.sharding import PartitionSpec as P

velocities = (
    (0, 0, 0),
    (1, 0, 0),
    (-1, 0, 0),
    (0, 1, 0),
    (0, -1, 0),
    (0, 0, 1),
    (0, 0, -1),
    (1, 1, 0),
    (-1, -1, 0),
    (1, -1, 0),
    (-1, 1, 0),
    (1, 0, 1),
    (-1, 0, -1),
    (1, 0, -1),
    (-1, 0, 1),
    (0, 1, 1),
    (0, -1, -1),
    (0, 1, -1),
    (0, -1, 1),
)
opposite = (0, 2, 1, 4, 3, 6, 5, 8, 7, 10, 9, 12, 11, 14, 13, 16, 15, 18, 17)
pairs = tuple((k, k + 1) for k in range(1, 19, 2))
incoming = (1, 7, 9, 11, 13)
backward_x = (2, 8, 10, 12, 14)
forward_z = (5, 11, 14, 15, 18)
backward_z = (6, 12, 13, 16, 17)
POPS = 19
PLANE = 16
FACE = 14
SIDE = 16
stays_x = tuple(k for k in range(POPS) if velocities[k][0] == 0)
KEPT = POPS + 5
VMEM_SMALL = 10 * 1024 * 1024
VMEM_LARGE = 20 * 1024 * 1024


def moments_of(pops):
    density = None
    moment = [None, None, None]

    def add(total, value):
        return value if total is None else total + value

    for group, weight in ((range(1, 7), 1.0 / 18.0), (range(7, POPS), 1.0 / 36.0)):
        part = None
        parts = [None, None, None]
        for a, b in ((k, k + 1) for k in group[::2]):
            if pops[a] is None and pops[b] is None:
                continue
            if pops[b] is None:
                both, diff = pops[a], pops[a]
            elif pops[a] is None:
                both, diff = pops[b], -pops[b]
            else:
                both, diff = pops[a] + pops[b], pops[a] - pops[b]
            part = add(part, both)
            for axis_num, step in enumerate(velocities[a]):
                if step != 0:
                    parts[axis_num] = add(parts[axis_num], diff if step == 1 else -diff)
        if part is not None:
            density = add(density, part * weight)
        for axis_num in range(3):
            if parts[axis_num] is not None:
                moment[axis_num] = add(moment[axis_num], parts[axis_num] * weight)
    if pops[0] is not None:
        density = add(density, pops[0] * (1.0 / 3.0))
    return density, moment


def relax(pops, density, moment, wanted):
    inverse = 1.0 / density
    speed = [component * inverse for component in moment]
    kinetic = moment[0] * speed[0] + moment[1] * speed[1] + moment[2] * speed[2]
    base = 1.25 * density - 1.875 * kinetic
    result = [None] * POPS
    if 0 in wanted:
        result[0] = base - 0.25 * pops[0]
    for a, b in pairs:
        if a not in wanted and b not in wanted:
            continue
        flux = None
        along = None
        for axis_num, step in enumerate(velocities[a]):
            if step == 0:
                continue
            if flux is None:
                flux, along = moment[axis_num], speed[axis_num]
            elif step == 1:
                flux, along = flux + moment[axis_num], along + speed[axis_num]
            else:
                flux, along = flux - moment[axis_num], along - speed[axis_num]
        even = base + 5.625 * (flux * along)
        odd = 3.75 * flux
        if a in wanted:
            result[a] = even + odd - 0.25 * pops[a]
        if b in wanted:
            result[b] = even - odd - 0.25 * pops[b]
    return result


def collide(pops, wanted=range(POPS)):
    density, moment = moments_of(pops)
    return relax(pops, density, moment, wanted)


def shift_layers(value, step_y):
    if step_y == 0:
        return value
    size = value.shape[-1]
    return pltpu.roll(value, step_y % size, value.ndim - 1)


def moved_row(base, left, right, masks, x_at, wanted=range(POPS)):
    result = []
    sub = None
    for which_pop in range(POPS):
        if which_pop not in wanted:
            result.append(None)
            continue
        step_x, step_y, step_z = velocities[which_pop]
        source = base(which_pop, x_at - step_x)
        if step_z != 0 and sub is None:
            sub = lax.broadcasted_iota(jnp.int32, source.shape, 0)
        width = source.shape[0]
        if step_z == 1:
            source = jnp.where(
                sub == 0, left(which_pop, x_at - step_x), pltpu.roll(source, 1, 0)
            )
        elif step_z == -1:
            source = jnp.where(
                sub == width - 1,
                right(which_pop, x_at - step_x),
                pltpu.roll(source, width - 1, 0),
            )
        source = shift_layers(source, step_y)
        result.append(
            jnp.where(masks[step_y] != 0, base(opposite[which_pop], x_at), source)
        )
    return result


def fill_masks(walls, masks):
    fine = walls.shape[1]
    coarse = masks.shape[2] - fine

    def fill(solid, lanes):
        layers = solid.shape[1]
        lane = lax.broadcasted_iota(jnp.int32, solid.shape, 1)
        masks[0, :, lanes] = solid
        masks[1, :, lanes] = jnp.where(lane == 0, 1.0, pltpu.roll(solid, 1, 1))
        masks[2, :, lanes] = jnp.where(lane == layers - 1, 1.0, pltpu.roll(solid, layers - 1, 1))

    solid = jnp.broadcast_to(jnp.where(walls[...] > 0, 1.0, 0.0), (8, fine))
    fine_at = lax.broadcasted_iota(jnp.int32, (fine, coarse), 0)
    coarse_at = lax.broadcasted_iota(jnp.int32, (fine, coarse), 1)
    halves = jnp.where(lax.shift_right_logical(fine_at, 1) == coarse_at, 1.0, 0.0)
    hits = jnp.dot(solid, halves, preferred_element_type=jnp.float32)
    fill(jnp.where(hits > 0.5, 1.0, 0.0), slice(0, coarse))
    fill(solid, slice(coarse, coarse + fine))


def first_kernel(
    pre_hbm,
    main_hbm,
    star_pre,
    star_main,
    z_same,
    z_cross,
    pre,
    main,
    arrived,
):
    rows = pre.shape[1]
    coarse = pre.shape[3]
    parity = lax.rem(lax.axis_index("span"), 2)
    domains = ((pre, star_pre, slice(0, coarse)), (main, star_main, slice(coarse, None)))
    copies = [
        [
            pltpu.make_async_copy(source.at[:, x_at], target.at[:, x_at], arrived.at[at, x_at])
            for at, (source, target) in enumerate(((pre_hbm, pre), (main_hbm, main)))
        ]
        for x_at in range(rows)
    ]
    for row in copies:
        for copy in row:
            copy.start()
    for x_at in range(rows):
        for copy in copies[x_at]:
            copy.wait()
        for pops, star, lanes in domains:
            out = collide([pops[which_pop, x_at] for which_pop in range(POPS)])
            for which_pop in range(POPS):
                star[which_pop, x_at] = out[which_pop]

    def edges(hi, lo):
        for _, star, lanes in domains:
            width = star.shape[2]
            for which_pop in range(POPS):
                hi[which_pop, :, lanes] = star[which_pop, :, width - 1, :]
                lo[which_pop, :, lanes] = star[which_pop, :, 0, :]
            for k in range(5):
                hi[POPS + k, :, lanes] = star[forward_z[k], :, width - 2, :]
                lo[POPS + k, :, lanes] = star[backward_z[k], :, 1, :]

    @pl.when(parity == 0)
    def _():
        edges(z_same, z_cross)

    @pl.when(parity == 1)
    def _():
        edges(z_cross, z_same)


def edge_lines(pops, moving, rim, inner):
    return [(pop, rim) for pop in pops if pop in stays_x] + [
        (pop, inner) for pop in pops if pop in moving
    ]


def fill_face(star, lanes, blocked, at_top, face):
    last = star.shape[1] - 1
    moving = incoming if at_top else backward_x
    rim = last if at_top else 0
    none = lambda pop, x_at: 0.0
    base = lambda pop, x_at: star[pop, x_at]
    new = moved_row(base, none, none, blocked, rim, moving + stays_x)
    for k, pop in enumerate(moving):
        face[k, :, lanes] = star[pop, rim]
        face[5 + k, :, lanes] = new[pop]
        new[pop] = None
    density, moment = moments_of(new)
    face[10, :, lanes] = density
    face[11, :, lanes] = moment[1]
    face[12, :, lanes] = moment[2]
    inner = rim - 1 if at_top else rim + 1
    for first, pops, z_at in ((0, backward_z, 0), (4, forward_z, star.shape[2] - 1)):
        for k, (pop, x_at) in enumerate(edge_lines(pops, moving, rim, inner)):
            row = first + k
            face[13, row : row + 1, lanes] = star[pop, x_at, z_at : z_at + 1, :]


def face_kernel(walls, star_pre, star_main, masks, x_hi, x_lo, plane):
    coarse = star_pre.shape[3]
    fill_masks(walls, masks)
    for star, lanes in zip((star_pre, star_main), lanes_of(coarse, star_main.shape[3])):
        blocked = masks_of(masks, lanes)
        fill_face(star, lanes, blocked, True, x_hi)
        fill_face(star, lanes, blocked, False, x_lo)
    fill_plane(star_pre, masks_of(masks, slice(0, coarse)), plane)


def fill_plane(star, blocked, plane):
    width, coarse = plane.shape[1:]
    last = star.shape[1] - 1
    zero = jnp.zeros((width, coarse), jnp.float32)
    stream_pos = lax.axis_index("stream")

    @pl.when(stream_pos != 1)
    def _():
        base = lambda pop, x_at: zero if x_at > last else star[pop, x_at]
        none = lambda pop, x_at: 0.0
        new = moved_row(base, none, none, blocked, last)
        density, moment = moments_of(new)
        for k, pop in enumerate(incoming):
            plane[k] = star[pop, last]
            plane[5 + k] = new[pop]
        plane[10] = density
        for axis_num in range(3):
            plane[11 + axis_num] = moment[axis_num]
        plane[14] = zero
        plane[15] = zero
        for k in range(5):
            hi, lo = forward_z[k], backward_z[k]
            plane[14, k : k + 1, :] = base(hi, last - velocities[hi][0])[width - 1 : width]
            plane[15, k : k + 1, :] = base(lo, last - velocities[lo][0])[0:1]

    @pl.when(stream_pos == 1)
    def _():
        none = lambda pop, x_at: 0.0
        back = moved_row(
            lambda pop, x_at: star[pop, x_at] if pop in backward_x else zero,
            none,
            none,
            blocked,
            -1,
            backward_x,
        )
        density, moment = moments_of(back)
        for k, value in enumerate([density] + moment):
            plane[k] = value
        for k in range(4, PLANE):
            plane[k] = zero
        plane[14, 1:2, :] = star[14, 0, width - 1 : width, :]
        plane[15, 1:2, :] = star[12, 0, 0:1, :]


def column_values(is_left, first, second, inner, shift, blocked):
    inward, outward = (forward_z, backward_z) if is_left else (backward_z, forward_z)
    result = []
    for pop in range(POPS):
        step_x, step_y, _ = velocities[pop]
        if pop in inward:
            source = shift(second, inward.index(pop), step_x)
        elif pop in outward:
            source = shift(inner, outward.index(pop), step_x)
        else:
            source = shift(first, pop, step_x)
        result.append(
            jnp.where(blocked[step_y] != 0, first(opposite[pop]), shift_layers(source, step_y))
        )
    return result


def turned(read, at, step_x):
    value = read(at)
    return value if step_x == 0 else pltpu.roll(value, step_x % value.shape[0], 0)


def only(pops, values):
    return [values[pop] if pop in pops else None for pop in range(POPS)]


def corner_kernel(x_low, x_high, tiles, e_same, e_cross):
    def lines(is_left, target):
        inward = forward_z if is_left else backward_z
        edge, second, first = (7, 6, 4) if is_left else (0, 1, 0)
        for start, moving, face in ((0, incoming, x_low), (SIDE, backward_x, x_high)):
            turning = moving.index([pop for pop in moving if pop in inward][0])
            new = [None] * POPS
            for k, pop in enumerate(moving):
                new[pop] = face[5 + k]
            density, moment = moments_of(new)
            sums = [
                density + face[10],
                moment[0],
                moment[1] + face[11],
                moment[2] + face[12],
                face[5 + turning],
            ]
            found = [face[k, edge : edge + 1, :] for k in range(5)]
            found += [face[13, first + k : first + k + 1, :] for k in range(4)]
            found += [face[turning, second : second + 1, :]]
            found += [value[edge : edge + 1] for value in sums]
            for k, line in enumerate(found):
                target[start + k : start + k + 1, :] = line

    parity = lax.rem(lax.axis_index("span"), 2)

    @pl.when(parity == 0)
    def _():
        lines(True, e_same)
        lines(False, e_cross)

    @pl.when(parity == 1)
    def _():
        lines(False, e_same)
        lines(True, e_cross)


def back_kernel(tile_map, masks, tiles_hbm, back, tiles, arrived):
    @pl.when(lax.axis_index("stream") == 1)
    def _():
        copy = pltpu.make_async_copy(tiles_hbm, tiles, arrived)
        copy.start()
        copy.wait()
        span_pos = lax.axis_index("span")
        span_count = lax.axis_size("span")
        width, coarse = tiles.shape[2:]
        sub = lax.broadcasted_iota(jnp.int32, (width, coarse), 0)
        open_layers = masks[0, :, :coarse] == 0
        for at, offset in enumerate((span_count - 1, 0, 1)):
            tile = tile_map[lax.rem(span_pos + offset, span_count)]
            edges = [None] * POPS
            for pop, side, row, slot in ((14, span_count - 1, 0, 14), (12, 1, width - 1, 15)):
                line = tiles[lax.rem(tile + side, span_count), slot, 1:2, :]
                line = jnp.broadcast_to(line, (width, coarse))
                edges[pop] = jnp.where((sub == row) & open_layers, line, 0.0)
            density, moment = moments_of(edges)
            back[at, 0] = tiles[tile, 0] + density
            back[at, 1] = tiles[tile, 2]
            back[at, 2] = tiles[tile, 3] + moment[2]


def build_columns(is_left, col, corner, halo, edge, lines, x_low, x_high, masks):
    inward, outward = (forward_z, backward_z) if is_left else (backward_z, forward_z)
    rim, first = (0, 0) if is_left else (7, 4)
    for k in range(KEPT):
        col[k, 8:16, :] = halo[k]
    for k in range(5):
        col[KEPT + k, 8:16, :] = edge[outward[k]]
    corner[...] = jnp.zeros(corner.shape, jnp.float32)
    for moving, face, start, near, beyond, row in (
        (incoming, x_low, 0, 7, 6, 0),
        (backward_x, x_high, SIDE, 16, 17, 9),
    ):
        line = lambda k: lines[start + k : start + k + 1, :]
        for k in range(5):
            col[moving[k], near : near + 1, :] = line(k)
        for k, pop in enumerate([pop for pop in inward if pop in stays_x]):
            col[pop, near : near + 1, :] = line(5 + k)
        turning = [pop for pop in moving if pop in inward][0]
        leaving = [pop for pop in moving if pop in outward][0]
        col[turning, beyond : beyond + 1, :] = line(8)
        at = POPS + inward.index(turning)
        col[at, near : near + 1, :] = line(9)
        at = KEPT + outward.index(leaving)
        col[at, near : near + 1, :] = face[moving.index(leaving), rim : rim + 1, :]
        for k in range(4):
            corner[k, row : row + 1, :] = line(10 + k)
        at = 4 if moving is incoming else 5
        corner[at, row : row + 1, :] = line(14)
        for lanes, blocked in masks:
            missing = [None] * POPS
            for k, (pop, _) in enumerate(edge_lines(outward, moving, 0, 0)):
                step_y = velocities[pop][1]
                value = face[13, first + k : first + k + 1, lanes]
                value = shift_layers(jnp.broadcast_to(value, blocked[0].shape), step_y)
                missing[pop] = jnp.where(blocked[step_y] != 0, 0.0, value)
            density, moment = moments_of(missing)
            for k, value in enumerate([density] + moment):
                corner[k, row : row + 1, lanes] += value[:1]


def refine(coarse, phases, fine_len):
    coarse_len = coarse.shape[1]
    count = coarse.shape[0] // 3
    rows = lax.broadcasted_iota(jnp.int32, (coarse_len, fine_len), 0)
    fine = lax.broadcasted_iota(jnp.int32, (coarse_len, fine_len), 1)
    outs = []
    for phase in (0, 1):
        position = fine + phase
        lower = lax.shift_right_arithmetic(position - 1, 1)
        upper_wt = jnp.where(position % 2 == 0, 0.75, 0.25)
        low_idx = jnp.clip(lower, 0, coarse_len - 1)
        high_idx = jnp.clip(lower + 1, 0, coarse_len - 1)
        matrix = jnp.where(rows == low_idx, 1.0 - upper_wt, 0.0) + jnp.where(
            rows == high_idx, upper_wt, 0.0
        )
        outs.append(
            jnp.dot(
                coarse,
                matrix,
                precision=lax.Precision.HIGHEST,
                preferred_element_type=jnp.float32,
            )
        )
    return [
        jnp.where(
            phases[tile] > 0,
            outs[1][tile * count : (tile + 1) * count],
            outs[0][tile * count : (tile + 1) * count],
        )
        for tile in range(3)
    ]


def lanes_of(coarse, fine):
    return slice(0, coarse), slice(coarse, coarse + fine)


def masks_of(masks, lanes, height=8):
    values = {step: masks[step % 3, :, lanes] for step in (0, 1, -1)}
    if height == 8:
        return values
    return {
        step: jnp.broadcast_to(value[:1], (height, value.shape[1]))
        for step, value in values.items()
    }


def middle_kernel(
    tile_map,
    layer_phase,
    masks,
    star_pre,
    star_main,
    same,
    cross,
    edge_same,
    edge_cross,
    tiles_hbm,
    mid_pre,
    mid_main,
    inflow,
    awaited,
    out_pre_hbm,
    out_main_hbm,
    ghost_left,
    ghost_right,
    rim_left,
    rim_right,
    out_pre,
    out_main,
    tiles,
    arrived,
    sent,
):
    rows, width, coarse = star_pre.shape[1:]
    fine = star_main.shape[3]
    span_pos = lax.axis_index("span")
    span_count = lax.axis_size("span")
    parity = lax.rem(span_pos, 2)

    on_inlet = lax.axis_index("stream") == 0
    copy = pltpu.make_async_copy(tiles_hbm, tiles, arrived)

    @pl.when(on_inlet)
    def _():
        copy.start()

    def ghosts(is_left, ghost, halo, edge, rim):
        inward, outward = (forward_z, backward_z) if is_left else (backward_z, forward_z)
        for k in range(5):
            ghost[k] = halo[inward[k]]
        for lanes in lanes_of(coarse, fine):
            new = column_values(
                is_left,
                lambda pop: halo[pop, :, lanes],
                lambda k: halo[POPS + k, :, lanes],
                lambda k: edge[outward[k], :, lanes],
                turned,
                masks_of(masks, lanes),
            )
            out = collide(new, inward)
            for k in range(5):
                rim[k, :, lanes] = out[inward[k]]

    @pl.when(parity == 0)
    def _():
        ghosts(True, ghost_left, cross, edge_cross, rim_left)
        ghosts(False, ghost_right, same, edge_same, rim_right)

    @pl.when(parity == 1)
    def _():
        ghosts(True, ghost_left, same, edge_same, rim_left)
        ghosts(False, ghost_right, cross, edge_cross, rim_right)

    stars = (star_pre, star_main)
    for x_at in range(1, rows - 1):
        for domain, lanes in enumerate(lanes_of(coarse, fine)):
            new = moved_row(
                lambda pop, at: stars[domain][pop, at],
                lambda pop, at: ghost_left[forward_z.index(pop), at : at + 1, lanes],
                lambda pop, at: ghost_right[backward_z.index(pop), at : at + 1, lanes],
                masks_of(masks, lanes),
                x_at,
            )
            out = collide(new)
            for pop in range(POPS):
                (mid_pre, mid_main)[domain][pop, x_at - 1] = out[pop]

    copies = []
    for x_at in range(2, rows - 2):
        for domain, lanes in enumerate(lanes_of(coarse, fine)):
            new = moved_row(
                lambda pop, at: (mid_pre, mid_main)[domain][pop, at - 1],
                lambda pop, at: rim_left[forward_z.index(pop), at : at + 1, lanes],
                lambda pop, at: rim_right[backward_z.index(pop), at : at + 1, lanes],
                masks_of(masks, lanes),
                x_at,
            )
            kept = (out_pre, out_main)[domain]
            for pop in range(POPS):
                kept[pop, x_at - 2] = new[pop]
            copies.append(
                pltpu.make_async_copy(
                    kept.at[:, x_at - 2],
                    (out_pre_hbm, out_main_hbm)[domain].at[:, x_at],
                    sent.at[domain, x_at - 2],
                )
            )
            copies[-1].start()

    @pl.when(on_inlet)
    def _():
        copy.wait()
        chosen, phases = [], []
        for offset in (span_count - 1, 0, 1):
            at = lax.rem(span_pos + offset, span_count)
            chosen.append(tile_map[at])
            phases.append(layer_phase[at])

        planes = [[tiles[tile, k] for k in range(5)] for tile in chosen]
        blocked = masks_of(masks, slice(0, coarse))
        sub = lax.broadcasted_iota(jnp.int32, (width, coarse), 0)
        for place, tile in enumerate(chosen):
            edges = [None] * POPS
            for k in range(5):
                for pop, at, row, slot in (
                    (forward_z[k], span_count - 1, 0, 14),
                    (backward_z[k], 1, width - 1, 15),
                ):
                    line = tiles[lax.rem(tile + at, span_count), slot, k : k + 1, :]
                    line = shift_layers(jnp.broadcast_to(line, (width, coarse)), velocities[pop][1])
                    keep = (sub == row) & (blocked[velocities[pop][1]] == 0)
                    edges[pop] = jnp.where(keep, line, 0.0)
            density, moment = moments_of(edges)
            density = density + tiles[tile, 10]
            moment = [moment[axis_num] + tiles[tile, 11 + axis_num] for axis_num in range(3)]
            for k, value in enumerate([density] + moment):
                awaited[place, k] = value
            for k, pop in enumerate(incoming):
                new = tiles[tile, 5 + k]
                if edges[pop] is not None:
                    new = new + edges[pop]
                awaited[place, 4 + k] = new
        stacked = jnp.concatenate([plane for group in planes for plane in group], axis=0)
        for place, value in enumerate(refine(stacked, phases, fine)):
            inflow[place] = value.reshape(5, width, fine)

    for copy_out in copies:
        copy_out.wait()


def last_kernel(
    masks,
    star_pre,
    star_main,
    mid_pre,
    mid_main,
    inflow,
    x_low,
    x_high,
    same,
    cross,
    edge_same,
    edge_cross,
    e_same,
    e_cross,
    part_pre,
    part_main,
    out_pre_hbm,
    out_main_hbm,
    kept_rows,
    col_left,
    col_right,
    corner_left,
    corner_right,
    in_low,
    in_high,
    next_pre,
    next_main,
    rim_left,
    rim_right,
    out_pre,
    out_main,
    sent,
):
    rows, width, coarse = star_pre.shape[1:]
    fine = star_main.shape[3]
    pre_lanes, main_lanes = lanes_of(coarse, fine)
    is_first = lax.axis_index("stream") == 0
    is_last = lax.axis_index("stream") == lax.axis_size("stream") - 1
    parity = lax.rem(lax.axis_index("span"), 2)
    ends = (x_low, x_high, [(lanes, masks_of(masks, lanes)) for lanes in (pre_lanes, main_lanes)])

    @pl.when(parity == 0)
    def _():
        build_columns(True, col_left, corner_left, cross, edge_cross, e_cross, *ends)
        build_columns(False, col_right, corner_right, same, edge_same, e_same, *ends)

    @pl.when(parity == 1)
    def _():
        build_columns(True, col_left, corner_left, same, edge_same, e_same, *ends)
        build_columns(False, col_right, corner_right, cross, edge_cross, e_cross, *ends)

    for k in range(5):
        in_low[k] = x_low[k, :, main_lanes]
        in_high[k] = x_high[k, :, main_lanes]

    @pl.when(is_last)
    def _():
        for k in range(5):
            in_high[k] = star_main[backward_x[k], rows - 1]
        for col in (col_left, col_right):
            for k in range(KEPT + 5):
                col[k, 16:17, main_lanes] = col[k, 15:16, main_lanes]

    @pl.when(is_first)
    def _():
        before, own, after = (inflow.at[tile] for tile in range(3))
        for k in range(5):
            in_low[k] = own[k]
            col_left[incoming[k], 7:8, main_lanes] = before[k, width - 1 : width]
            col_right[incoming[k], 7:8, main_lanes] = after[k, 0:1]
        col_left[POPS + 1, 7:8, main_lanes] = before[3, width - 2 : width - 1]
        col_left[KEPT + 2, 7:8, main_lanes] = own[4, 0:1]
        col_right[POPS + 2, 7:8, main_lanes] = after[4, 1:2]
        col_right[KEPT + 1, 7:8, main_lanes] = own[3, width - 1 : width]

    for is_left, col, corner, rim in (
        (True, col_left, corner_left, rim_left),
        (False, col_right, corner_right, rim_right),
    ):
        moving = forward_z if is_left else backward_z
        for lanes in (pre_lanes, main_lanes):
            new = column_values(
                is_left,
                lambda pop, step_x=0: col[pop, 7 - step_x : 23 - step_x, lanes],
                lambda k, step_x: col[POPS + k, 7 - step_x : 23 - step_x, lanes],
                lambda k, step_x: col[KEPT + k, 7 - step_x : 23 - step_x, lanes],
                lambda read, at, step_x: read(at, step_x),
                masks_of(masks, lanes, 16),
            )
            row = lax.broadcasted_iota(jnp.int32, new[0].shape, 0)
            for pop in range(POPS):
                if pop not in backward_x:
                    new[pop] = jnp.where(row == 0, 0.0, new[pop])
                if pop not in incoming:
                    new[pop] = jnp.where(row == rows + 1, 0.0, new[pop])
            density, moment = moments_of(new)
            density = density + corner[0, :, lanes]
            moment = [moment[axis_num] + corner[1 + axis_num, :, lanes] for axis_num in range(3)]
            for at, ends_of in ((4, incoming), (5, backward_x)):
                pop = [pop for pop in moving if pop in ends_of][0]
                new[pop] = new[pop] + corner[at, :, lanes]
            out = relax(new, density, moment, moving)
            for k in range(5):
                rim[k, :, lanes] = out[moving[k]]

    stars = (star_pre, star_main)
    outer = {-1: 0, 0: 1, rows - 1: 2, rows: 3}

    def base_of(domain, lanes):
        def base(pop, x_at):
            if 0 <= x_at < rows:
                return stars[domain][pop, x_at]
            if x_at == -1:
                k = incoming.index(pop)
                return in_low[k] if domain == 1 else x_low[k, :, lanes]
            k = backward_x.index(pop)
            return in_high[k] if domain == 1 else x_high[k, :, lanes]

        return base

    def beside_tile(domain, lanes, x_at):
        star = stars[domain]
        face, moving, back = (
            (x_low, incoming, backward_x) if x_at < 0 else (x_high, backward_x, incoming)
        )
        blocked = masks_of(masks, lanes)
        left = lambda pop, at: col_left[pop, 8 + at : 9 + at, lanes]
        right = lambda pop, at: col_right[pop, 8 + at : 9 + at, lanes]

        def base(pop, at):
            return face[moving.index(pop), :, lanes] if at == x_at else star[pop, at]

        new = moved_row(base, left, right, blocked, x_at, back)
        sub = lax.broadcasted_iota(jnp.int32, new[back[0]].shape, 0)
        for pop in range(POPS):
            if pop in back:
                continue
            step_x, step_y, step_z = velocities[pop]
            if step_z != 0:
                line = (left if step_z == 1 else right)(pop, x_at - step_x)
                line = shift_layers(jnp.broadcast_to(line, sub.shape), step_y)
                keep = (sub == (0 if step_z == 1 else width - 1)) & (blocked[step_y] == 0)
                new[pop] = jnp.where(keep, line, 0.0)
            if pop in moving:
                part = face[5 + moving.index(pop), :, lanes]
                new[pop] = part if new[pop] is None else part + new[pop]
        density, moment = moments_of(new)
        density = density + face[10, :, lanes]
        moment = [moment[0], moment[1] + face[11, :, lanes], moment[2] + face[12, :, lanes]]
        return relax(new, density, moment, moving), moving

    for x_at in outer:
        for domain, lanes in enumerate((pre_lanes, main_lanes)):
            if 0 <= x_at < rows:
                new = moved_row(
                    base_of(domain, lanes),
                    lambda pop, at: col_left[pop, 8 + at : 9 + at, lanes],
                    lambda pop, at: col_right[pop, 8 + at : 9 + at, lanes],
                    masks_of(masks, lanes),
                    x_at,
                )
                out, wanted = collide(new), range(POPS)
            else:
                out, wanted = beside_tile(domain, lanes, x_at)
            for pop in wanted:
                (next_pre, next_main)[domain][pop, outer[x_at]] = out[pop]

    for k in range(5):
        kept_rows[k] = next_main[backward_x[k], 1]

    @pl.when(is_last)
    def _():
        for k in range(5):
            next_main[backward_x[k], 3] = next_main[backward_x[k], 2]
            for rim in (rim_left, rim_right):
                rim[k, rows + 1 : rows + 2, main_lanes] = rim[k, rows : rows + 1, main_lanes]

    def next_of(domain):
        def base(pop, x_at):
            if x_at in outer:
                return (next_pre, next_main)[domain][pop, outer[x_at]]
            return (mid_pre, mid_main)[domain][pop, x_at - 1]

        return base

    copies = []
    for at_end, x_at in enumerate((0, 1, rows - 2, rows - 1)):
        for domain, lanes in enumerate((pre_lanes, main_lanes)):
            new = moved_row(
                next_of(domain),
                lambda pop, at: rim_left[forward_z.index(pop), at + 1 : at + 2, lanes],
                lambda pop, at: rim_right[backward_z.index(pop), at + 1 : at + 2, lanes],
                masks_of(masks, lanes),
                x_at,
            )
            kept = (out_pre, out_main)[domain]
            for pop in range(POPS):
                kept[pop, at_end] = new[pop]
            copy = pltpu.make_async_copy(
                kept.at[:, at_end],
                (out_pre_hbm, out_main_hbm)[domain].at[:, x_at],
                sent.at[domain, at_end],
            )
            copy.start()
            copies.append(copy)
    for copy in copies:
        copy.wait()


def inlet_kernel(layer_phase, masks, awaited, back, kept_rows, main_hbm, out_hbm, ready, sent):
    @pl.when(lax.axis_index("stream") == 0)
    def _():
        width, coarse = awaited.shape[2:]
        fine = masks.shape[2] - coarse
        span_pos, span_count = lax.axis_index("span"), lax.axis_size("span")
        phases, planes = [], []
        for place, offset in enumerate((span_count - 1, 0, 1)):
            phases.append(layer_phase[lax.rem(span_pos + offset, span_count)])
            density = awaited[place, 0] + back[place, 0]
            moment = [
                awaited[place, 1] - back[place, 0],
                awaited[place, 2] + back[place, 1],
                awaited[place, 3] + back[place, 2],
            ]
            new = [None] * POPS
            for k, pop in enumerate(incoming):
                new[pop] = awaited[place, 4 + k]
            out = relax(new, density, moment, incoming)
            planes += [out[pop] for pop in incoming]
        before, own, after = (
            value.reshape(5, width, fine)
            for value in refine(jnp.concatenate(planes, axis=0), phases, fine)
        )

        def base(pop, x_at):
            return own[incoming.index(pop)] if x_at < 0 else kept_rows[backward_x.index(pop)]

        new = moved_row(
            base,
            lambda pop, x_at: before[incoming.index(pop), width - 1 : width],
            lambda pop, x_at: after[incoming.index(pop), 0:1],
            masks_of(masks, slice(coarse, coarse + fine)),
            0,
            incoming,
        )
        copies = []
        for k, pop in enumerate(incoming):
            ready[k] = new[pop]
            copies.append(pltpu.make_async_copy(ready.at[k], out_hbm.at[pop, 0], sent.at[k]))
            copies[-1].start()
        for copy in copies:
            copy.wait()


def f32(*shape):
    return jax.ShapeDtypeStruct(shape, jnp.float32)


def local(pre_pops, main_pops, tile_map, layer_phase, wall_flags):
    span_count = lax.axis_size("span")
    stream_count = lax.axis_size("stream")
    _, rows, width, coarse = pre_pops.shape
    fine = main_pops.shape[3]
    lanes = coarse + fine

    def send(value, step_x, place, only=range(stream_count)):
        moves = []
        for s in range(stream_count):
            if s not in only:
                continue
            for j in range(span_count):
                target = (s + step_x) % stream_count * span_count + place(j) % span_count
                moves.append((s * span_count + j, target))
        return lax.ppermute(value, ("stream", "span"), moves)

    stay = lambda j: j
    sibling = lambda j: j + 1 if j % 2 == 0 else j - 1
    beyond = lambda j: j - 1 if j % 2 == 0 else j + 1
    params = pltpu.CompilerParams(vmem_limit_bytes=VMEM_SMALL)

    whole = pl.BlockSpec(memory_space=pltpu.VMEM)
    outside = pl.BlockSpec(memory_space=pltpu.HBM)
    scalars = pl.BlockSpec(memory_space=pltpu.SMEM)

    in_hbm = lambda value: pltpu.with_memory_space_constraint(value, pltpu.HBM)
    star_pre, star_main, z_same, z_cross = pl.pallas_call(
        first_kernel,
        out_shape=(
            f32(*pre_pops.shape),
            f32(*main_pops.shape),
            f32(KEPT, rows, lanes),
            f32(KEPT, rows, lanes),
        ),
        in_specs=[outside, outside],
        scratch_shapes=[
            pltpu.VMEM(pre_pops.shape, jnp.float32),
            pltpu.VMEM(main_pops.shape, jnp.float32),
            pltpu.SemaphoreType.DMA((2, rows)),
        ],
        compiler_params=pltpu.CompilerParams(vmem_limit_bytes=VMEM_SMALL),
        name="collide_and_pack",
    )(in_hbm(pre_pops), in_hbm(main_pops))
    masks, x_hi, x_lo, plane = pl.pallas_call(
        face_kernel,
        out_shape=(
            f32(3, 8, lanes),
            f32(FACE, width, lanes),
            f32(FACE, width, lanes),
            f32(PLANE, width, coarse),
        ),
        compiler_params=params,
        name="faces",
    )(wall_flags.reshape(1, fine), star_pre, star_main)

    same = send(z_same, 0, sibling)
    cross = send(z_cross, 0, beyond)
    x_low = send(x_hi, 1, stay)
    x_high = send(x_lo, -1, stay)
    tiles = lax.all_gather(plane, "span", axis=0, tiled=False)
    anywhere = pl.BlockSpec(memory_space=pl.ANY)
    all_tiles = [
        pltpu.VMEM((span_count, PLANE, width, coarse), jnp.float32),
        pltpu.SemaphoreType.DMA,
    ]
    e_to_same, e_to_cross = pl.pallas_call(
        corner_kernel,
        out_shape=(f32(2 * SIDE, lanes), f32(2 * SIDE, lanes)),
        in_specs=[whole] * 2 + [anywhere],
        compiler_params=params,
        name="corners",
    )(x_low, x_high, tiles)
    e_same = send(e_to_same, 0, sibling)
    e_cross = send(e_to_cross, 0, beyond)
    back = pl.pallas_call(
        back_kernel,
        out_shape=f32(3, 3, width, coarse),
        in_specs=[scalars, whole, anywhere],
        scratch_shapes=all_tiles,
        compiler_params=params,
        name="behind_plane",
    )(tile_map, masks, tiles)
    back = send(back, -1, stay, (1 % stream_count,))
    half_pre = pltpu.VMEM((POPS, 4, width, coarse), jnp.float32)
    half_main = pltpu.VMEM((POPS, 4, width, fine), jnp.float32)
    mid_pre, mid_main, inflow, awaited, part_pre, part_main = pl.pallas_call(
        middle_kernel,
        out_shape=(
            f32(POPS, rows - 2, width, coarse),
            f32(POPS, rows - 2, width, fine),
            f32(3, 5, width, fine),
            f32(3, 9, width, coarse),
            f32(*pre_pops.shape),
            f32(*main_pops.shape),
        ),
        in_specs=[scalars, scalars] + [whole] * 7 + [anywhere],
        out_specs=[whole] * 4 + [outside] * 2,
        scratch_shapes=[
            pltpu.VMEM((5, rows, lanes), jnp.float32),
            pltpu.VMEM((5, rows, lanes), jnp.float32),
            pltpu.VMEM((5, rows, lanes), jnp.float32),
            pltpu.VMEM((5, rows, lanes), jnp.float32),
            pltpu.VMEM((POPS, rows - 4, width, coarse), jnp.float32),
            pltpu.VMEM((POPS, rows - 4, width, fine), jnp.float32),
        ]
        + all_tiles
        + [pltpu.SemaphoreType.DMA((2, rows - 4))],
        compiler_params=params,
        name="middle_rows",
    )(tile_map, layer_phase, masks, star_pre, star_main, same, cross, z_same, z_cross, tiles)
    out_pre, out_main, kept_rows = pl.pallas_call(
        last_kernel,
        out_shape=(f32(*pre_pops.shape), f32(*main_pops.shape), f32(5, width, fine)),
        in_specs=[whole] * 14 + [outside] * 2,
        out_specs=(outside, outside, whole),
        input_output_aliases={14: 0, 15: 1},
        scratch_shapes=[
            pltpu.VMEM((KEPT + 5, 24, lanes), jnp.float32),
            pltpu.VMEM((KEPT + 5, 24, lanes), jnp.float32),
            pltpu.VMEM((6, 16, lanes), jnp.float32),
            pltpu.VMEM((6, 16, lanes), jnp.float32),
            pltpu.VMEM((5, width, fine), jnp.float32),
            pltpu.VMEM((5, width, fine), jnp.float32),
            half_pre,
            half_main,
            pltpu.VMEM((5, 16, lanes), jnp.float32),
            pltpu.VMEM((5, 16, lanes), jnp.float32),
            half_pre,
            half_main,
            pltpu.SemaphoreType.DMA((2, 4)),
        ],
        compiler_params=pltpu.CompilerParams(vmem_limit_bytes=VMEM_LARGE),
        name="last_rows",
    )(
        masks,
        star_pre,
        star_main,
        mid_pre,
        mid_main,
        inflow,
        x_low,
        x_high,
        same,
        cross,
        z_same,
        z_cross,
        e_same,
        e_cross,
        part_pre,
        part_main,
    )
    out_main = pl.pallas_call(
        inlet_kernel,
        out_shape=f32(*main_pops.shape),
        in_specs=[scalars] + [whole] * 4 + [outside],
        out_specs=outside,
        input_output_aliases={5: 0},
        scratch_shapes=[
            pltpu.VMEM((5, width, fine), jnp.float32),
            pltpu.SemaphoreType.DMA((5,)),
        ],
        compiler_params=params,
        name="inlet_row",
    )(layer_phase, masks, awaited, back, kept_rows, out_main)
    return out_pre, out_main


def solution(mesh):
    return jax.shard_map(
        local,
        mesh=mesh,
        in_specs=(P(None, "stream", "span", None), P(None, "stream", "span", None), P(), P(), P()),
        out_specs=(P(None, "stream", "span", None), P(None, "stream", "span", None)),
        check_vma=False,
    )
```

```python
import jax
import jax.numpy as jnp
from jax import lax
from jax.experimental import pallas as pl
from jax.experimental.pallas import tpu as pltpu
from jax.sharding import PartitionSpec as P

velocities = (
    (0, 0, 0),
    (1, 0, 0),
    (-1, 0, 0),
    (0, 1, 0),
    (0, -1, 0),
    (0, 0, 1),
    (0, 0, -1),
    (1, 1, 0),
    (-1, -1, 0),
    (1, -1, 0),
    (-1, 1, 0),
    (1, 0, 1),
    (-1, 0, -1),
    (1, 0, -1),
    (-1, 0, 1),
    (0, 1, 1),
    (0, -1, -1),
    (0, 1, -1),
    (0, -1, 1),
)
opposite = (0, 2, 1, 4, 3, 6, 5, 8, 7, 10, 9, 12, 11, 14, 13, 16, 15, 18, 17)
pairs = tuple((k, k + 1) for k in range(1, 19, 2))
incoming = (1, 7, 9, 11, 13)
backward_x = (2, 8, 10, 12, 14)
forward_z = (5, 11, 14, 15, 18)
backward_z = (6, 12, 13, 16, 17)
POPS = 19
PLANE = 16
FACE = 14
SIDE = 16
stays_x = tuple(k for k in range(POPS) if velocities[k][0] == 0)
KEPT = POPS + 5
VMEM_SMALL = 10 * 1024 * 1024
VMEM_LARGE = 20 * 1024 * 1024


def moments_of(pops):
    density = None
    moment = [None, None, None]

    def add(total, value):
        return value if total is None else total + value

    for group, weight in ((range(1, 7), 1.0 / 18.0), (range(7, POPS), 1.0 / 36.0)):
        part = None
        parts = [None, None, None]
        for a, b in ((k, k + 1) for k in group[::2]):
            if pops[a] is None and pops[b] is None:
                continue
            if pops[b] is None:
                both, diff = pops[a], pops[a]
            elif pops[a] is None:
                both, diff = pops[b], -pops[b]
            else:
                both, diff = pops[a] + pops[b], pops[a] - pops[b]
            part = add(part, both)
            for axis_num, step in enumerate(velocities[a]):
                if step != 0:
                    parts[axis_num] = add(parts[axis_num], diff if step == 1 else -diff)
        if part is not None:
            density = add(density, part * weight)
        for axis_num in range(3):
            if parts[axis_num] is not None:
                moment[axis_num] = add(moment[axis_num], parts[axis_num] * weight)
    if pops[0] is not None:
        density = add(density, pops[0] * (1.0 / 3.0))
    return density, moment


def relax(pops, density, moment, wanted):
    inverse = 1.0 / density
    speed = [component * inverse for component in moment]
    kinetic = moment[0] * speed[0] + moment[1] * speed[1] + moment[2] * speed[2]
    base = 1.25 * density - 1.875 * kinetic
    result = [None] * POPS
    if 0 in wanted:
        result[0] = base - 0.25 * pops[0]
    for a, b in pairs:
        if a not in wanted and b not in wanted:
            continue
        flux = None
        along = None
        for axis_num, step in enumerate(velocities[a]):
            if step == 0:
                continue
            if flux is None:
                flux, along = moment[axis_num], speed[axis_num]
            elif step == 1:
                flux, along = flux + moment[axis_num], along + speed[axis_num]
            else:
                flux, along = flux - moment[axis_num], along - speed[axis_num]
        even = base + 5.625 * (flux * along)
        odd = 3.75 * flux
        if a in wanted:
            result[a] = even + odd - 0.25 * pops[a]
        if b in wanted:
            result[b] = even - odd - 0.25 * pops[b]
    return result


def collide(pops, wanted=range(POPS)):
    density, moment = moments_of(pops)
    return relax(pops, density, moment, wanted)


def shift_layers(value, step_y):
    if step_y == 0:
        return value
    size = value.shape[-1]
    return pltpu.roll(value, step_y % size, value.ndim - 1)


def moved_row(base, left, right, masks, x_at, wanted=range(POPS)):
    result = []
    sub = None
    for which_pop in range(POPS):
        if which_pop not in wanted:
            result.append(None)
            continue
        step_x, step_y, step_z = velocities[which_pop]
        source = base(which_pop, x_at - step_x)
        if step_z != 0 and sub is None:
            sub = lax.broadcasted_iota(jnp.int32, source.shape, 0)
        width = source.shape[0]
        if step_z == 1:
            source = jnp.where(
                sub == 0, left(which_pop, x_at - step_x), pltpu.roll(source, 1, 0)
            )
        elif step_z == -1:
            source = jnp.where(
                sub == width - 1,
                right(which_pop, x_at - step_x),
                pltpu.roll(source, width - 1, 0),
            )
        source = shift_layers(source, step_y)
        result.append(
            jnp.where(masks[step_y] != 0, base(opposite[which_pop], x_at), source)
        )
    return result


def fill_masks(walls, masks):
    fine = walls.shape[1]
    coarse = masks.shape[2] - fine

    def fill(solid, lanes):
        layers = solid.shape[1]
        lane = lax.broadcasted_iota(jnp.int32, solid.shape, 1)
        masks[0, :, lanes] = solid
        masks[1, :, lanes] = jnp.where(lane == 0, 1.0, pltpu.roll(solid, 1, 1))
        masks[2, :, lanes] = jnp.where(lane == layers - 1, 1.0, pltpu.roll(solid, layers - 1, 1))

    solid = jnp.broadcast_to(jnp.where(walls[...] > 0, 1.0, 0.0), (8, fine))
    fine_at = lax.broadcasted_iota(jnp.int32, (fine, coarse), 0)
    coarse_at = lax.broadcasted_iota(jnp.int32, (fine, coarse), 1)
    halves = jnp.where(lax.shift_right_logical(fine_at, 1) == coarse_at, 1.0, 0.0)
    hits = jnp.dot(solid, halves, preferred_element_type=jnp.float32)
    fill(jnp.where(hits > 0.5, 1.0, 0.0), slice(0, coarse))
    fill(solid, slice(coarse, coarse + fine))


def first_kernel(
    pre_hbm,
    main_hbm,
    star_pre,
    star_main,
    z_same,
    z_cross,
    pre,
    main,
    arrived,
):
    rows = pre.shape[1]
    coarse = pre.shape[3]
    parity = lax.rem(lax.axis_index("span"), 2)
    domains = ((pre, star_pre, slice(0, coarse)), (main, star_main, slice(coarse, None)))
    copies = [
        [
            pltpu.make_async_copy(source.at[:, x_at], target.at[:, x_at], arrived.at[at, x_at])
            for at, (source, target) in enumerate(((pre_hbm, pre), (main_hbm, main)))
        ]
        for x_at in range(rows)
    ]
    for row in copies:
        for copy in row:
            copy.start()
    for x_at in range(rows):
        for copy in copies[x_at]:
            copy.wait()
        for pops, star, lanes in domains:
            out = collide([pops[which_pop, x_at] for which_pop in range(POPS)])
            for which_pop in range(POPS):
                star[which_pop, x_at] = out[which_pop]

    def edges(hi, lo):
        for _, star, lanes in domains:
            width = star.shape[2]
            for which_pop in range(POPS):
                hi[which_pop, :, lanes] = star[which_pop, :, width - 1, :]
                lo[which_pop, :, lanes] = star[which_pop, :, 0, :]
            for k in range(5):
                hi[POPS + k, :, lanes] = star[forward_z[k], :, width - 2, :]
                lo[POPS + k, :, lanes] = star[backward_z[k], :, 1, :]

    @pl.when(parity == 0)
    def _():
        edges(z_same, z_cross)

    @pl.when(parity == 1)
    def _():
        edges(z_cross, z_same)


def edge_lines(pops, moving, rim, inner):
    return [(pop, rim) for pop in pops if pop in stays_x] + [
        (pop, inner) for pop in pops if pop in moving
    ]


def fill_face(star, lanes, blocked, at_top, face):
    last = star.shape[1] - 1
    moving = incoming if at_top else backward_x
    rim = last if at_top else 0
    none = lambda pop, x_at: 0.0
    base = lambda pop, x_at: star[pop, x_at]
    new = moved_row(base, none, none, blocked, rim, moving + stays_x)
    for k, pop in enumerate(moving):
        face[k, :, lanes] = star[pop, rim]
        face[5 + k, :, lanes] = new[pop]
        new[pop] = None
    density, moment = moments_of(new)
    face[10, :, lanes] = density
    face[11, :, lanes] = moment[1]
    face[12, :, lanes] = moment[2]
    inner = rim - 1 if at_top else rim + 1
    for first, pops, z_at in ((0, backward_z, 0), (4, forward_z, star.shape[2] - 1)):
        for k, (pop, x_at) in enumerate(edge_lines(pops, moving, rim, inner)):
            row = first + k
            face[13, row : row + 1, lanes] = star[pop, x_at, z_at : z_at + 1, :]


def face_kernel(walls, star_pre, star_main, masks, x_hi, x_lo, plane):
    coarse = star_pre.shape[3]
    fill_masks(walls, masks)
    for star, lanes in zip((star_pre, star_main), lanes_of(coarse, star_main.shape[3])):
        blocked = masks_of(masks, lanes)
        fill_face(star, lanes, blocked, True, x_hi)
        fill_face(star, lanes, blocked, False, x_lo)
    fill_plane(star_pre, masks_of(masks, slice(0, coarse)), plane)


def fill_plane(star, blocked, plane):
    width, coarse = plane.shape[1:]
    last = star.shape[1] - 1
    zero = jnp.zeros((width, coarse), jnp.float32)
    stream_pos = lax.axis_index("stream")

    @pl.when(stream_pos != 1)
    def _():
        base = lambda pop, x_at: zero if x_at > last else star[pop, x_at]
        none = lambda pop, x_at: 0.0
        new = moved_row(base, none, none, blocked, last)
        density, moment = moments_of(new)
        for k, pop in enumerate(incoming):
            plane[k] = star[pop, last]
            plane[5 + k] = new[pop]
        plane[10] = density
        for axis_num in range(3):
            plane[11 + axis_num] = moment[axis_num]
        plane[14] = zero
        plane[15] = zero
        for k in range(5):
            hi, lo = forward_z[k], backward_z[k]
            plane[14, k : k + 1, :] = base(hi, last - velocities[hi][0])[width - 1 : width]
            plane[15, k : k + 1, :] = base(lo, last - velocities[lo][0])[0:1]

    @pl.when(stream_pos == 1)
    def _():
        none = lambda pop, x_at: 0.0
        back = moved_row(
            lambda pop, x_at: star[pop, x_at] if pop in backward_x else zero,
            none,
            none,
            blocked,
            -1,
            backward_x,
        )
        density, moment = moments_of(back)
        for k, value in enumerate([density] + moment):
            plane[k] = value
        for k in range(4, PLANE):
            plane[k] = zero
        plane[14, 1:2, :] = star[14, 0, width - 1 : width, :]
        plane[15, 1:2, :] = star[12, 0, 0:1, :]


def column_values(is_left, first, second, inner, shift, blocked):
    inward, outward = (forward_z, backward_z) if is_left else (backward_z, forward_z)
    result = []
    for pop in range(POPS):
        step_x, step_y, _ = velocities[pop]
        if pop in inward:
            source = shift(second, inward.index(pop), step_x)
        elif pop in outward:
            source = shift(inner, outward.index(pop), step_x)
        else:
            source = shift(first, pop, step_x)
        result.append(
            jnp.where(blocked[step_y] != 0, first(opposite[pop]), shift_layers(source, step_y))
        )
    return result


def turned(read, at, step_x):
    value = read(at)
    return value if step_x == 0 else pltpu.roll(value, step_x % value.shape[0], 0)


def only(pops, values):
    return [values[pop] if pop in pops else None for pop in range(POPS)]


def corner_kernel(x_low, x_high, tiles, e_same, e_cross):
    def lines(is_left, target):
        inward = forward_z if is_left else backward_z
        edge, second, first = (7, 6, 4) if is_left else (0, 1, 0)
        for start, moving, face in ((0, incoming, x_low), (SIDE, backward_x, x_high)):
            turning = moving.index([pop for pop in moving if pop in inward][0])
            new = [None] * POPS
            for k, pop in enumerate(moving):
                new[pop] = face[5 + k]
            density, moment = moments_of(new)
            sums = [
                density + face[10],
                moment[0],
                moment[1] + face[11],
                moment[2] + face[12],
                face[5 + turning],
            ]
            found = [face[k, edge : edge + 1, :] for k in range(5)]
            found += [face[13, first + k : first + k + 1, :] for k in range(4)]
            found += [face[turning, second : second + 1, :]]
            found += [value[edge : edge + 1] for value in sums]
            for k, line in enumerate(found):
                target[start + k : start + k + 1, :] = line

    parity = lax.rem(lax.axis_index("span"), 2)

    @pl.when(parity == 0)
    def _():
        lines(True, e_same)
        lines(False, e_cross)

    @pl.when(parity == 1)
    def _():
        lines(False, e_same)
        lines(True, e_cross)


def back_kernel(tile_map, masks, tiles_hbm, back, tiles, arrived):
    @pl.when(lax.axis_index("stream") == 1)
    def _():
        copy = pltpu.make_async_copy(tiles_hbm, tiles, arrived)
        copy.start()
        copy.wait()
        width, coarse = tiles.shape[2:]
        sub = lax.broadcasted_iota(jnp.int32, (width, coarse), 0)
        open_layers = masks[0, :, :coarse] == 0
        for at, number in enumerate(neighbours(tile_map)):
            edges = [None] * POPS
            for pop, offset, row, slot in ((14, -1, 0, 14), (12, 1, width - 1, 15)):
                line = tile_at(tiles, number, (slot,), offset)[0][1:2]
                line = jnp.broadcast_to(line, (width, coarse))
                edges[pop] = jnp.where((sub == row) & open_layers, line, 0.0)
            density, moment = moments_of(edges)
            sums = tile_at(tiles, number, (0, 2, 3))
            back[at, 0] = sums[0] + density
            back[at, 1] = sums[1]
            back[at, 2] = sums[2] + moment[2]


def build_columns(is_left, col, corner, halo, edge, lines, x_low, x_high, masks):
    inward, outward = (forward_z, backward_z) if is_left else (backward_z, forward_z)
    rim, first = (0, 0) if is_left else (7, 4)
    for k in range(KEPT):
        col[k, 8:16, :] = halo[k]
    for k in range(5):
        col[KEPT + k, 8:16, :] = edge[outward[k]]
    corner[...] = jnp.zeros(corner.shape, jnp.float32)
    for moving, face, start, near, beyond, row in (
        (incoming, x_low, 0, 7, 6, 0),
        (backward_x, x_high, SIDE, 16, 17, 9),
    ):
        line = lambda k: lines[start + k : start + k + 1, :]
        for k in range(5):
            col[moving[k], near : near + 1, :] = line(k)
        for k, pop in enumerate([pop for pop in inward if pop in stays_x]):
            col[pop, near : near + 1, :] = line(5 + k)
        turning = [pop for pop in moving if pop in inward][0]
        leaving = [pop for pop in moving if pop in outward][0]
        col[turning, beyond : beyond + 1, :] = line(8)
        at = POPS + inward.index(turning)
        col[at, near : near + 1, :] = line(9)
        at = KEPT + outward.index(leaving)
        col[at, near : near + 1, :] = face[moving.index(leaving), rim : rim + 1, :]
        for k in range(4):
            corner[k, row : row + 1, :] = line(10 + k)
        at = 4 if moving is incoming else 5
        corner[at, row : row + 1, :] = line(14)
        for lanes, blocked in masks:
            missing = [None] * POPS
            for k, (pop, _) in enumerate(edge_lines(outward, moving, 0, 0)):
                step_y = velocities[pop][1]
                value = face[13, first + k : first + k + 1, lanes]
                value = shift_layers(jnp.broadcast_to(value, blocked[0].shape), step_y)
                missing[pop] = jnp.where(blocked[step_y] != 0, 0.0, value)
            density, moment = moments_of(missing)
            for k, value in enumerate([density] + moment):
                corner[k, row : row + 1, lanes] += value[:1]


def entry_at(row, at):
    lane = lax.broadcasted_iota(jnp.int32, row.shape, 1)
    return jnp.sum(jnp.where(lane == at, row[...].astype(jnp.float32), 0.0), axis=1, keepdims=True)


def neighbours(row):
    count = row.shape[1]
    position = lax.axis_index("span")
    return [entry_at(row, lax.rem(position + step, count)) for step in (count - 1, 0, 1)]


def tile_at(tiles, number, slots, offset=0):
    count = tiles.shape[0]
    found = [tiles[offset % count, slot] for slot in slots]
    for tile in range(1, count):
        here = jnp.broadcast_to(number, found[0].shape) == float(tile)
        found = [
            jnp.where(here, tiles[(tile + offset) % count, slot], value)
            for slot, value in zip(slots, found)
        ]
    return found


def refine(coarse, phases, fine_len):
    coarse_len = coarse.shape[1]
    count = coarse.shape[0] // 3
    rows = lax.broadcasted_iota(jnp.int32, (coarse_len, fine_len), 0)
    fine = lax.broadcasted_iota(jnp.int32, (coarse_len, fine_len), 1)
    matrices = []
    for phase in (0, 1):
        position = fine + phase
        lower = lax.shift_right_arithmetic(position - 1, 1)
        upper_wt = jnp.where(position % 2 == 0, 0.75, 0.25)
        low_idx = jnp.clip(lower, 0, coarse_len - 1)
        high_idx = jnp.clip(lower + 1, 0, coarse_len - 1)
        matrix = jnp.where(rows == low_idx, 1.0 - upper_wt, 0.0) + jnp.where(
            rows == high_idx, upper_wt, 0.0
        )
        matrices.append(matrix.astype(jnp.bfloat16))
    parts = []
    rest = coarse
    for _ in range(3):
        parts.append(rest.astype(jnp.bfloat16))
        rest = rest - parts[-1].astype(jnp.float32)
    outs = []
    for matrix in matrices:
        total = None
        for part in reversed(parts):
            product = jnp.dot(part, matrix, preferred_element_type=jnp.float32)
            total = product if total is None else total + product
        outs.append(total)
    return [
        jnp.where(
            jnp.broadcast_to(phases[tile], (count, fine_len)) > 0.5,
            outs[1][tile * count : (tile + 1) * count],
            outs[0][tile * count : (tile + 1) * count],
        )
        for tile in range(3)
    ]


def lanes_of(coarse, fine):
    return slice(0, coarse), slice(coarse, coarse + fine)


def masks_of(masks, lanes, height=8):
    values = {step: masks[step % 3, :, lanes] for step in (0, 1, -1)}
    if height == 8:
        return values
    return {
        step: jnp.broadcast_to(value[:1], (height, value.shape[1]))
        for step, value in values.items()
    }


def middle_kernel(
    tile_map,
    layer_phase,
    masks,
    star_pre,
    star_main,
    same,
    cross,
    edge_same,
    edge_cross,
    tiles_hbm,
    mid_pre,
    mid_main,
    inflow,
    awaited,
    out_pre_hbm,
    out_main_hbm,
    ghost_left,
    ghost_right,
    rim_left,
    rim_right,
    out_pre,
    out_main,
    tiles,
    arrived,
    sent,
):
    rows, width, coarse = star_pre.shape[1:]
    fine = star_main.shape[3]
    parity = lax.rem(lax.axis_index("span"), 2)

    on_inlet = lax.axis_index("stream") == 0
    copy = pltpu.make_async_copy(tiles_hbm, tiles, arrived)

    @pl.when(on_inlet)
    def _():
        copy.start()

    def ghosts(is_left, ghost, halo, edge, rim):
        inward, outward = (forward_z, backward_z) if is_left else (backward_z, forward_z)
        for k in range(5):
            ghost[k] = halo[inward[k]]
        for lanes in lanes_of(coarse, fine):
            new = column_values(
                is_left,
                lambda pop: halo[pop, :, lanes],
                lambda k: halo[POPS + k, :, lanes],
                lambda k: edge[outward[k], :, lanes],
                turned,
                masks_of(masks, lanes),
            )
            out = collide(new, inward)
            for k in range(5):
                rim[k, :, lanes] = out[inward[k]]

    @pl.when(parity == 0)
    def _():
        ghosts(True, ghost_left, cross, edge_cross, rim_left)
        ghosts(False, ghost_right, same, edge_same, rim_right)

    @pl.when(parity == 1)
    def _():
        ghosts(True, ghost_left, same, edge_same, rim_left)
        ghosts(False, ghost_right, cross, edge_cross, rim_right)

    stars = (star_pre, star_main)
    for x_at in range(1, rows - 1):
        for domain, lanes in enumerate(lanes_of(coarse, fine)):
            new = moved_row(
                lambda pop, at: stars[domain][pop, at],
                lambda pop, at: ghost_left[forward_z.index(pop), at : at + 1, lanes],
                lambda pop, at: ghost_right[backward_z.index(pop), at : at + 1, lanes],
                masks_of(masks, lanes),
                x_at,
            )
            out = collide(new)
            for pop in range(POPS):
                (mid_pre, mid_main)[domain][pop, x_at - 1] = out[pop]

    copies = []
    for x_at in range(2, rows - 2):
        for domain, lanes in enumerate(lanes_of(coarse, fine)):
            new = moved_row(
                lambda pop, at: (mid_pre, mid_main)[domain][pop, at - 1],
                lambda pop, at: rim_left[forward_z.index(pop), at : at + 1, lanes],
                lambda pop, at: rim_right[backward_z.index(pop), at : at + 1, lanes],
                masks_of(masks, lanes),
                x_at,
            )
            kept = (out_pre, out_main)[domain]
            for pop in range(POPS):
                kept[pop, x_at - 2] = new[pop]
            copies.append(
                pltpu.make_async_copy(
                    kept.at[:, x_at - 2],
                    (out_pre_hbm, out_main_hbm)[domain].at[:, x_at],
                    sent.at[domain, x_at - 2],
                )
            )
            copies[-1].start()

    @pl.when(on_inlet)
    def _():
        copy.wait()
        planes = []
        blocked = masks_of(masks, slice(0, coarse))
        sub = lax.broadcasted_iota(jnp.int32, (width, coarse), 0)
        for place, number in enumerate(neighbours(tile_map)):
            found = tile_at(tiles, number, range(14))
            planes += found[:5]
            edges = [None] * POPS
            for pops, offset, row, slot in (
                (forward_z, -1, 0, 14),
                (backward_z, 1, width - 1, 15),
            ):
                lines = tile_at(tiles, number, (slot,), offset)[0]
                for k, pop in enumerate(pops):
                    line = jnp.broadcast_to(lines[k : k + 1], (width, coarse))
                    line = shift_layers(line, velocities[pop][1])
                    keep = (sub == row) & (blocked[velocities[pop][1]] == 0)
                    edges[pop] = jnp.where(keep, line, 0.0)
            density, moment = moments_of(edges)
            for k, value in enumerate([density] + moment):
                awaited[place, k] = found[10 + k] + value
            for k, pop in enumerate(incoming):
                new = found[5 + k]
                awaited[place, 4 + k] = new if edges[pop] is None else new + edges[pop]
        refined = refine(jnp.concatenate(planes, axis=0), neighbours(layer_phase), fine)
        for place, value in enumerate(refined):
            inflow[place] = value.reshape(5, width, fine)

    for copy_out in copies:
        copy_out.wait()


def last_kernel(
    masks,
    star_pre,
    star_main,
    mid_pre,
    mid_main,
    inflow,
    x_low,
    x_high,
    same,
    cross,
    edge_same,
    edge_cross,
    e_same,
    e_cross,
    part_pre,
    part_main,
    out_pre_hbm,
    out_main_hbm,
    kept_rows,
    col_left,
    col_right,
    corner_left,
    corner_right,
    in_low,
    in_high,
    next_pre,
    next_main,
    rim_left,
    rim_right,
    out_pre,
    out_main,
    sent,
):
    rows, width, coarse = star_pre.shape[1:]
    fine = star_main.shape[3]
    pre_lanes, main_lanes = lanes_of(coarse, fine)
    is_first = lax.axis_index("stream") == 0
    is_last = lax.axis_index("stream") == lax.axis_size("stream") - 1
    parity = lax.rem(lax.axis_index("span"), 2)
    ends = (x_low, x_high, [(lanes, masks_of(masks, lanes)) for lanes in (pre_lanes, main_lanes)])

    @pl.when(parity == 0)
    def _():
        build_columns(True, col_left, corner_left, cross, edge_cross, e_cross, *ends)
        build_columns(False, col_right, corner_right, same, edge_same, e_same, *ends)

    @pl.when(parity == 1)
    def _():
        build_columns(True, col_left, corner_left, same, edge_same, e_same, *ends)
        build_columns(False, col_right, corner_right, cross, edge_cross, e_cross, *ends)

    for k in range(5):
        in_low[k] = x_low[k, :, main_lanes]
        in_high[k] = x_high[k, :, main_lanes]

    @pl.when(is_last)
    def _():
        for k in range(5):
            in_high[k] = star_main[backward_x[k], rows - 1]
        for col in (col_left, col_right):
            for k in range(KEPT + 5):
                col[k, 16:17, main_lanes] = col[k, 15:16, main_lanes]

    @pl.when(is_first)
    def _():
        before, own, after = (inflow.at[tile] for tile in range(3))
        for k in range(5):
            in_low[k] = own[k]
            col_left[incoming[k], 7:8, main_lanes] = before[k, width - 1 : width]
            col_right[incoming[k], 7:8, main_lanes] = after[k, 0:1]
        col_left[POPS + 1, 7:8, main_lanes] = before[3, width - 2 : width - 1]
        col_left[KEPT + 2, 7:8, main_lanes] = own[4, 0:1]
        col_right[POPS + 2, 7:8, main_lanes] = after[4, 1:2]
        col_right[KEPT + 1, 7:8, main_lanes] = own[3, width - 1 : width]

    for is_left, col, corner, rim in (
        (True, col_left, corner_left, rim_left),
        (False, col_right, corner_right, rim_right),
    ):
        moving = forward_z if is_left else backward_z
        for lanes in (pre_lanes, main_lanes):
            new = column_values(
                is_left,
                lambda pop, step_x=0: col[pop, 7 - step_x : 23 - step_x, lanes],
                lambda k, step_x: col[POPS + k, 7 - step_x : 23 - step_x, lanes],
                lambda k, step_x: col[KEPT + k, 7 - step_x : 23 - step_x, lanes],
                lambda read, at, step_x: read(at, step_x),
                masks_of(masks, lanes, 16),
            )
            row = lax.broadcasted_iota(jnp.int32, new[0].shape, 0)
            for pop in range(POPS):
                if pop not in backward_x:
                    new[pop] = jnp.where(row == 0, 0.0, new[pop])
                if pop not in incoming:
                    new[pop] = jnp.where(row == rows + 1, 0.0, new[pop])
            density, moment = moments_of(new)
            density = density + corner[0, :, lanes]
            moment = [moment[axis_num] + corner[1 + axis_num, :, lanes] for axis_num in range(3)]
            for at, ends_of in ((4, incoming), (5, backward_x)):
                pop = [pop for pop in moving if pop in ends_of][0]
                new[pop] = new[pop] + corner[at, :, lanes]
            out = relax(new, density, moment, moving)
            for k in range(5):
                rim[k, :, lanes] = out[moving[k]]

    stars = (star_pre, star_main)
    outer = {-1: 0, 0: 1, rows - 1: 2, rows: 3}

    def base_of(domain, lanes):
        def base(pop, x_at):
            if 0 <= x_at < rows:
                return stars[domain][pop, x_at]
            if x_at == -1:
                k = incoming.index(pop)
                return in_low[k] if domain == 1 else x_low[k, :, lanes]
            k = backward_x.index(pop)
            return in_high[k] if domain == 1 else x_high[k, :, lanes]

        return base

    def beside_tile(domain, lanes, x_at):
        star = stars[domain]
        face, moving, back = (
            (x_low, incoming, backward_x) if x_at < 0 else (x_high, backward_x, incoming)
        )
        blocked = masks_of(masks, lanes)
        left = lambda pop, at: col_left[pop, 8 + at : 9 + at, lanes]
        right = lambda pop, at: col_right[pop, 8 + at : 9 + at, lanes]

        def base(pop, at):
            return face[moving.index(pop), :, lanes] if at == x_at else star[pop, at]

        new = moved_row(base, left, right, blocked, x_at, back)
        sub = lax.broadcasted_iota(jnp.int32, new[back[0]].shape, 0)
        for pop in range(POPS):
            if pop in back:
                continue
            step_x, step_y, step_z = velocities[pop]
            if step_z != 0:
                line = (left if step_z == 1 else right)(pop, x_at - step_x)
                line = shift_layers(jnp.broadcast_to(line, sub.shape), step_y)
                keep = (sub == (0 if step_z == 1 else width - 1)) & (blocked[step_y] == 0)
                new[pop] = jnp.where(keep, line, 0.0)
            if pop in moving:
                part = face[5 + moving.index(pop), :, lanes]
                new[pop] = part if new[pop] is None else part + new[pop]
        density, moment = moments_of(new)
        density = density + face[10, :, lanes]
        moment = [moment[0], moment[1] + face[11, :, lanes], moment[2] + face[12, :, lanes]]
        return relax(new, density, moment, moving), moving

    for x_at in outer:
        for domain, lanes in enumerate((pre_lanes, main_lanes)):
            if 0 <= x_at < rows:
                new = moved_row(
                    base_of(domain, lanes),
                    lambda pop, at: col_left[pop, 8 + at : 9 + at, lanes],
                    lambda pop, at: col_right[pop, 8 + at : 9 + at, lanes],
                    masks_of(masks, lanes),
                    x_at,
                )
                out, wanted = collide(new), range(POPS)
            else:
                out, wanted = beside_tile(domain, lanes, x_at)
            for pop in wanted:
                (next_pre, next_main)[domain][pop, outer[x_at]] = out[pop]

    for k in range(5):
        kept_rows[k] = next_main[backward_x[k], 1]

    @pl.when(is_last)
    def _():
        for k in range(5):
            next_main[backward_x[k], 3] = next_main[backward_x[k], 2]
            for rim in (rim_left, rim_right):
                rim[k, rows + 1 : rows + 2, main_lanes] = rim[k, rows : rows + 1, main_lanes]

    def next_of(domain):
        def base(pop, x_at):
            if x_at in outer:
                return (next_pre, next_main)[domain][pop, outer[x_at]]
            return (mid_pre, mid_main)[domain][pop, x_at - 1]

        return base

    copies = []
    for at_end, x_at in enumerate((0, 1, rows - 2, rows - 1)):
        for domain, lanes in enumerate((pre_lanes, main_lanes)):
            new = moved_row(
                next_of(domain),
                lambda pop, at: rim_left[forward_z.index(pop), at + 1 : at + 2, lanes],
                lambda pop, at: rim_right[backward_z.index(pop), at + 1 : at + 2, lanes],
                masks_of(masks, lanes),
                x_at,
            )
            kept = (out_pre, out_main)[domain]
            for pop in range(POPS):
                kept[pop, at_end] = new[pop]
            copy = pltpu.make_async_copy(
                kept.at[:, at_end],
                (out_pre_hbm, out_main_hbm)[domain].at[:, x_at],
                sent.at[domain, at_end],
            )
            copy.start()
            copies.append(copy)
    for copy in copies:
        copy.wait()


def inlet_kernel(layer_phase, masks, awaited, back, kept_rows, main_hbm, out_hbm, ready, sent):
    @pl.when(lax.axis_index("stream") == 0)
    def _():
        width, coarse = awaited.shape[2:]
        fine = masks.shape[2] - coarse
        planes = []
        for place in range(3):
            density = awaited[place, 0] + back[place, 0]
            moment = [
                awaited[place, 1] - back[place, 0],
                awaited[place, 2] + back[place, 1],
                awaited[place, 3] + back[place, 2],
            ]
            new = [None] * POPS
            for k, pop in enumerate(incoming):
                new[pop] = awaited[place, 4 + k]
            out = relax(new, density, moment, incoming)
            planes += [out[pop] for pop in incoming]
        before, own, after = (
            value.reshape(5, width, fine)
            for value in refine(jnp.concatenate(planes, axis=0), neighbours(layer_phase), fine)
        )

        def base(pop, x_at):
            return own[incoming.index(pop)] if x_at < 0 else kept_rows[backward_x.index(pop)]

        new = moved_row(
            base,
            lambda pop, x_at: before[incoming.index(pop), width - 1 : width],
            lambda pop, x_at: after[incoming.index(pop), 0:1],
            masks_of(masks, slice(coarse, coarse + fine)),
            0,
            incoming,
        )
        copies = []
        for k, pop in enumerate(incoming):
            ready[k] = new[pop]
            copies.append(pltpu.make_async_copy(ready.at[k], out_hbm.at[pop, 0], sent.at[k]))
            copies[-1].start()
        for copy in copies:
            copy.wait()


def f32(*shape):
    return jax.ShapeDtypeStruct(shape, jnp.float32)


def local(pre_pops, main_pops, tile_map, layer_phase, wall_flags):
    span_count = lax.axis_size("span")
    stream_count = lax.axis_size("stream")
    _, rows, width, coarse = pre_pops.shape
    fine = main_pops.shape[3]
    lanes = coarse + fine

    def send(value, step_x, place, only=range(stream_count)):
        moves = []
        for s in range(stream_count):
            if s not in only:
                continue
            for j in range(span_count):
                target = (s + step_x) % stream_count * span_count + place(j) % span_count
                moves.append((s * span_count + j, target))
        return lax.ppermute(value, ("stream", "span"), moves)

    stay = lambda j: j
    sibling = lambda j: j + 1 if j % 2 == 0 else j - 1
    beyond = lambda j: j - 1 if j % 2 == 0 else j + 1
    params = pltpu.CompilerParams(vmem_limit_bytes=VMEM_SMALL)

    whole = pl.BlockSpec(memory_space=pltpu.VMEM)
    outside = pl.BlockSpec(memory_space=pltpu.HBM)
    tile_row, phase_row = (row.reshape(1, span_count) for row in (tile_map, layer_phase))

    in_hbm = lambda value: pltpu.with_memory_space_constraint(value, pltpu.HBM)
    star_pre, star_main, z_same, z_cross = pl.pallas_call(
        first_kernel,
        out_shape=(
            f32(*pre_pops.shape),
            f32(*main_pops.shape),
            f32(KEPT, rows, lanes),
            f32(KEPT, rows, lanes),
        ),
        in_specs=[outside, outside],
        scratch_shapes=[
            pltpu.VMEM(pre_pops.shape, jnp.float32),
            pltpu.VMEM(main_pops.shape, jnp.float32),
            pltpu.SemaphoreType.DMA((2, rows)),
        ],
        compiler_params=pltpu.CompilerParams(vmem_limit_bytes=VMEM_SMALL),
        name="collide_and_pack",
    )(in_hbm(pre_pops), in_hbm(main_pops))
    masks, x_hi, x_lo, plane = pl.pallas_call(
        face_kernel,
        out_shape=(
            f32(3, 8, lanes),
            f32(FACE, width, lanes),
            f32(FACE, width, lanes),
            f32(PLANE, width, coarse),
        ),
        compiler_params=params,
        name="faces",
    )(wall_flags.reshape(1, fine), star_pre, star_main)

    same = send(z_same, 0, sibling)
    cross = send(z_cross, 0, beyond)
    x_low = send(x_hi, 1, stay)
    x_high = send(x_lo, -1, stay)
    tiles = lax.all_gather(plane, "span", axis=0, tiled=False)
    anywhere = pl.BlockSpec(memory_space=pl.ANY)
    all_tiles = [
        pltpu.VMEM((span_count, PLANE, width, coarse), jnp.float32),
        pltpu.SemaphoreType.DMA,
    ]
    e_to_same, e_to_cross = pl.pallas_call(
        corner_kernel,
        out_shape=(f32(2 * SIDE, lanes), f32(2 * SIDE, lanes)),
        in_specs=[whole] * 2 + [anywhere],
        compiler_params=params,
        name="corners",
    )(x_low, x_high, tiles)
    e_same = send(e_to_same, 0, sibling)
    e_cross = send(e_to_cross, 0, beyond)
    back = pl.pallas_call(
        back_kernel,
        out_shape=f32(3, 3, width, coarse),
        in_specs=[whole, whole, anywhere],
        scratch_shapes=all_tiles,
        compiler_params=params,
        name="behind_plane",
    )(tile_row, masks, tiles)
    back = send(back, -1, stay, (1 % stream_count,))
    half_pre = pltpu.VMEM((POPS, 4, width, coarse), jnp.float32)
    half_main = pltpu.VMEM((POPS, 4, width, fine), jnp.float32)
    mid_pre, mid_main, inflow, awaited, part_pre, part_main = pl.pallas_call(
        middle_kernel,
        out_shape=(
            f32(POPS, rows - 2, width, coarse),
            f32(POPS, rows - 2, width, fine),
            f32(3, 5, width, fine),
            f32(3, 9, width, coarse),
            f32(*pre_pops.shape),
            f32(*main_pops.shape),
        ),
        in_specs=[whole] * 9 + [anywhere],
        out_specs=[whole] * 4 + [outside] * 2,
        scratch_shapes=[
            pltpu.VMEM((5, rows, lanes), jnp.float32),
            pltpu.VMEM((5, rows, lanes), jnp.float32),
            pltpu.VMEM((5, rows, lanes), jnp.float32),
            pltpu.VMEM((5, rows, lanes), jnp.float32),
            pltpu.VMEM((POPS, rows - 4, width, coarse), jnp.float32),
            pltpu.VMEM((POPS, rows - 4, width, fine), jnp.float32),
        ]
        + all_tiles
        + [pltpu.SemaphoreType.DMA((2, rows - 4))],
        compiler_params=params,
        name="middle_rows",
    )(tile_row, phase_row, masks, star_pre, star_main, same, cross, z_same, z_cross, tiles)
    out_pre, out_main, kept_rows = pl.pallas_call(
        last_kernel,
        out_shape=(f32(*pre_pops.shape), f32(*main_pops.shape), f32(5, width, fine)),
        in_specs=[whole] * 14 + [outside] * 2,
        out_specs=(outside, outside, whole),
        input_output_aliases={14: 0, 15: 1},
        scratch_shapes=[
            pltpu.VMEM((KEPT + 5, 24, lanes), jnp.float32),
            pltpu.VMEM((KEPT + 5, 24, lanes), jnp.float32),
            pltpu.VMEM((6, 16, lanes), jnp.float32),
            pltpu.VMEM((6, 16, lanes), jnp.float32),
            pltpu.VMEM((5, width, fine), jnp.float32),
            pltpu.VMEM((5, width, fine), jnp.float32),
            half_pre,
            half_main,
            pltpu.VMEM((5, 16, lanes), jnp.float32),
            pltpu.VMEM((5, 16, lanes), jnp.float32),
            half_pre,
            half_main,
            pltpu.SemaphoreType.DMA((2, 4)),
        ],
        compiler_params=pltpu.CompilerParams(vmem_limit_bytes=VMEM_LARGE),
        name="last_rows",
    )(
        masks,
        star_pre,
        star_main,
        mid_pre,
        mid_main,
        inflow,
        x_low,
        x_high,
        same,
        cross,
        z_same,
        z_cross,
        e_same,
        e_cross,
        part_pre,
        part_main,
    )
    out_main = pl.pallas_call(
        inlet_kernel,
        out_shape=f32(*main_pops.shape),
        in_specs=[whole] * 5 + [outside],
        out_specs=outside,
        input_output_aliases={5: 0},
        scratch_shapes=[
            pltpu.VMEM((5, width, fine), jnp.float32),
            pltpu.SemaphoreType.DMA((5,)),
        ],
        compiler_params=params,
        name="inlet_row",
    )(phase_row, masks, awaited, back, kept_rows, out_main)
    return out_pre, out_main


def solution(mesh):
    return jax.shard_map(
        local,
        mesh=mesh,
        in_specs=(P(None, "stream", "span", None), P(None, "stream", "span", None), P(), P(), P()),
        out_specs=(P(None, "stream", "span", None), P(None, "stream", "span", None)),
        check_vma=False,
    )
```

```python
import jax
import jax.numpy as jnp
from jax import lax
from jax.experimental import pallas as pl
from jax.experimental.pallas import tpu as pltpu
from jax.sharding import PartitionSpec as P

velocities = (
    (0, 0, 0),
    (1, 0, 0),
    (-1, 0, 0),
    (0, 1, 0),
    (0, -1, 0),
    (0, 0, 1),
    (0, 0, -1),
    (1, 1, 0),
    (-1, -1, 0),
    (1, -1, 0),
    (-1, 1, 0),
    (1, 0, 1),
    (-1, 0, -1),
    (1, 0, -1),
    (-1, 0, 1),
    (0, 1, 1),
    (0, -1, -1),
    (0, 1, -1),
    (0, -1, 1),
)
opposite = (0, 2, 1, 4, 3, 6, 5, 8, 7, 10, 9, 12, 11, 14, 13, 16, 15, 18, 17)
pairs = tuple((k, k + 1) for k in range(1, 19, 2))
incoming = (1, 7, 9, 11, 13)
backward_x = (2, 8, 10, 12, 14)
forward_z = (5, 11, 14, 15, 18)
backward_z = (6, 12, 13, 16, 17)
POPS = 19
PLANE = 16
FACE = 14
SIDE = 16
stays_x = tuple(k for k in range(POPS) if velocities[k][0] == 0)
KEPT = POPS + 5
VMEM_SMALL = 10 * 1024 * 1024
VMEM_LARGE = 20 * 1024 * 1024


def moments_of(pops):
    density = None
    moment = [None, None, None]

    def add(total, value):
        return value if total is None else total + value

    for group, weight in ((range(1, 7), 1.0 / 18.0), (range(7, POPS), 1.0 / 36.0)):
        part = None
        parts = [None, None, None]
        for a, b in ((k, k + 1) for k in group[::2]):
            if pops[a] is None and pops[b] is None:
                continue
            if pops[b] is None:
                both, diff = pops[a], pops[a]
            elif pops[a] is None:
                both, diff = pops[b], -pops[b]
            else:
                both, diff = pops[a] + pops[b], pops[a] - pops[b]
            part = add(part, both)
            for axis_num, step in enumerate(velocities[a]):
                if step != 0:
                    parts[axis_num] = add(parts[axis_num], diff if step == 1 else -diff)
        if part is not None:
            density = add(density, part * weight)
        for axis_num in range(3):
            if parts[axis_num] is not None:
                moment[axis_num] = add(moment[axis_num], parts[axis_num] * weight)
    if pops[0] is not None:
        density = add(density, pops[0] * (1.0 / 3.0))
    return density, moment


def relax(pops, density, moment, wanted):
    inverse = 1.0 / density
    speed = [component * inverse for component in moment]
    kinetic = moment[0] * speed[0] + moment[1] * speed[1] + moment[2] * speed[2]
    base = 1.25 * density - 1.875 * kinetic
    result = [None] * POPS
    if 0 in wanted:
        result[0] = base - 0.25 * pops[0]
    for a, b in pairs:
        if a not in wanted and b not in wanted:
            continue
        flux = None
        along = None
        for axis_num, step in enumerate(velocities[a]):
            if step == 0:
                continue
            if flux is None:
                flux, along = moment[axis_num], speed[axis_num]
            elif step == 1:
                flux, along = flux + moment[axis_num], along + speed[axis_num]
            else:
                flux, along = flux - moment[axis_num], along - speed[axis_num]
        even = base + 5.625 * (flux * along)
        odd = 3.75 * flux
        if a in wanted:
            result[a] = even + odd - 0.25 * pops[a]
        if b in wanted:
            result[b] = even - odd - 0.25 * pops[b]
    return result


def collide(pops, wanted=range(POPS)):
    density, moment = moments_of(pops)
    return relax(pops, density, moment, wanted)


def shift_layers(value, step_y):
    if step_y == 0:
        return value
    size = value.shape[-1]
    return pltpu.roll(value, step_y % size, value.ndim - 1)


def moved_row(base, left, right, masks, x_at, wanted=range(POPS)):
    result = []
    sub = None
    for which_pop in range(POPS):
        if which_pop not in wanted:
            result.append(None)
            continue
        step_x, step_y, step_z = velocities[which_pop]
        source = base(which_pop, x_at - step_x)
        if step_z != 0 and sub is None:
            sub = lax.broadcasted_iota(jnp.int32, source.shape, 0)
        width = source.shape[0]
        if step_z == 1:
            source = jnp.where(
                sub == 0, left(which_pop, x_at - step_x), pltpu.roll(source, 1, 0)
            )
        elif step_z == -1:
            source = jnp.where(
                sub == width - 1,
                right(which_pop, x_at - step_x),
                pltpu.roll(source, width - 1, 0),
            )
        source = shift_layers(source, step_y)
        result.append(
            jnp.where(masks[step_y] != 0, base(opposite[which_pop], x_at), source)
        )
    return result


def fill_masks(walls, masks):
    fine = walls.shape[1]
    coarse = masks.shape[2] - fine

    def fill(solid, lanes):
        layers = solid.shape[1]
        lane = lax.broadcasted_iota(jnp.int32, solid.shape, 1)
        masks[0, :, lanes] = solid
        masks[1, :, lanes] = jnp.where(lane == 0, 1.0, pltpu.roll(solid, 1, 1))
        masks[2, :, lanes] = jnp.where(lane == layers - 1, 1.0, pltpu.roll(solid, layers - 1, 1))

    solid = jnp.broadcast_to(jnp.where(walls[...] > 0, 1.0, 0.0), (8, fine))
    fine_at = lax.broadcasted_iota(jnp.int32, (fine, coarse), 0)
    coarse_at = lax.broadcasted_iota(jnp.int32, (fine, coarse), 1)
    halves = jnp.where(lax.shift_right_logical(fine_at, 1) == coarse_at, 1.0, 0.0)
    hits = jnp.dot(solid, halves, preferred_element_type=jnp.float32)
    fill(jnp.where(hits > 0.5, 1.0, 0.0), slice(0, coarse))
    fill(solid, slice(coarse, coarse + fine))


def first_kernel(
    pre_hbm,
    main_hbm,
    star_pre,
    star_main,
    z_same,
    z_cross,
    pre,
    main,
    arrived,
):
    rows = pre.shape[1]
    coarse = pre.shape[3]
    parity = lax.rem(lax.axis_index("span"), 2)
    domains = ((pre, star_pre, slice(0, coarse)), (main, star_main, slice(coarse, None)))
    copies = [
        [
            pltpu.make_async_copy(source.at[:, x_at], target.at[:, x_at], arrived.at[at, x_at])
            for at, (source, target) in enumerate(((pre_hbm, pre), (main_hbm, main)))
        ]
        for x_at in range(rows)
    ]
    for row in copies:
        for copy in row:
            copy.start()
    for x_at in range(rows):
        for copy in copies[x_at]:
            copy.wait()
        for pops, star, lanes in domains:
            out = collide([pops[which_pop, x_at] for which_pop in range(POPS)])
            for which_pop in range(POPS):
                star[which_pop, x_at] = out[which_pop]

    def edges(hi, lo):
        for _, star, lanes in domains:
            width = star.shape[2]
            for which_pop in range(POPS):
                hi[which_pop, :, lanes] = star[which_pop, :, width - 1, :]
                lo[which_pop, :, lanes] = star[which_pop, :, 0, :]
            for k in range(5):
                hi[POPS + k, :, lanes] = star[forward_z[k], :, width - 2, :]
                lo[POPS + k, :, lanes] = star[backward_z[k], :, 1, :]

    @pl.when(parity == 0)
    def _():
        edges(z_same, z_cross)

    @pl.when(parity == 1)
    def _():
        edges(z_cross, z_same)


def edge_lines(pops, moving, rim, inner):
    return [(pop, rim) for pop in pops if pop in stays_x] + [
        (pop, inner) for pop in pops if pop in moving
    ]


def fill_face(star, lanes, blocked, at_top, face):
    last = star.shape[1] - 1
    moving = incoming if at_top else backward_x
    rim = last if at_top else 0
    none = lambda pop, x_at: 0.0
    base = lambda pop, x_at: star[pop, x_at]
    new = moved_row(base, none, none, blocked, rim, moving + stays_x)
    for k, pop in enumerate(moving):
        face[k, :, lanes] = star[pop, rim]
        face[5 + k, :, lanes] = new[pop]
        new[pop] = None
    density, moment = moments_of(new)
    face[10, :, lanes] = density
    face[11, :, lanes] = moment[1]
    face[12, :, lanes] = moment[2]
    inner = rim - 1 if at_top else rim + 1
    for first, pops, z_at in ((0, backward_z, 0), (4, forward_z, star.shape[2] - 1)):
        for k, (pop, x_at) in enumerate(edge_lines(pops, moving, rim, inner)):
            row = first + k
            face[13, row : row + 1, lanes] = star[pop, x_at, z_at : z_at + 1, :]


def face_kernel(walls, star_pre, star_main, masks, x_hi, x_lo, plane):
    coarse = star_pre.shape[3]
    fill_masks(walls, masks)
    for star, lanes in zip((star_pre, star_main), lanes_of(coarse, star_main.shape[3])):
        blocked = masks_of(masks, lanes)
        fill_face(star, lanes, blocked, True, x_hi)
        fill_face(star, lanes, blocked, False, x_lo)
    fill_plane(star_pre, masks_of(masks, slice(0, coarse)), plane)


def fill_plane(star, blocked, plane):
    width, coarse = plane.shape[1:]
    last = star.shape[1] - 1
    zero = jnp.zeros((width, coarse), jnp.float32)
    stream_pos = lax.axis_index("stream")

    @pl.when(stream_pos != 1)
    def _():
        base = lambda pop, x_at: zero if x_at > last else star[pop, x_at]
        none = lambda pop, x_at: 0.0
        new = moved_row(base, none, none, blocked, last)
        density, moment = moments_of(new)
        for k, pop in enumerate(incoming):
            plane[k] = star[pop, last]
            plane[5 + k] = new[pop]
        plane[10] = density
        for axis_num in range(3):
            plane[11 + axis_num] = moment[axis_num]
        plane[14] = zero
        plane[15] = zero
        for k in range(5):
            hi, lo = forward_z[k], backward_z[k]
            plane[14, k : k + 1, :] = base(hi, last - velocities[hi][0])[width - 1 : width]
            plane[15, k : k + 1, :] = base(lo, last - velocities[lo][0])[0:1]

    @pl.when(stream_pos == 1)
    def _():
        none = lambda pop, x_at: 0.0
        back = moved_row(
            lambda pop, x_at: star[pop, x_at] if pop in backward_x else zero,
            none,
            none,
            blocked,
            -1,
            backward_x,
        )
        density, moment = moments_of(back)
        for k, value in enumerate([density] + moment):
            plane[k] = value
        for k in range(4, PLANE):
            plane[k] = zero
        plane[14, 1:2, :] = star[14, 0, width - 1 : width, :]
        plane[15, 1:2, :] = star[12, 0, 0:1, :]


def column_values(is_left, first, second, inner, shift, blocked):
    inward, outward = (forward_z, backward_z) if is_left else (backward_z, forward_z)
    result = []
    for pop in range(POPS):
        step_x, step_y, _ = velocities[pop]
        if pop in inward:
            source = shift(second, inward.index(pop), step_x)
        elif pop in outward:
            source = shift(inner, outward.index(pop), step_x)
        else:
            source = shift(first, pop, step_x)
        result.append(
            jnp.where(blocked[step_y] != 0, first(opposite[pop]), shift_layers(source, step_y))
        )
    return result


def turned(read, at, step_x):
    value = read(at)
    return value if step_x == 0 else pltpu.roll(value, step_x % value.shape[0], 0)


def only(pops, values):
    return [values[pop] if pop in pops else None for pop in range(POPS)]


def corner_kernel(x_high, x_low, tiles, e_same, e_cross):
    def lines(is_left, target):
        inward = forward_z if is_left else backward_z
        edge, second, first = (7, 6, 4) if is_left else (0, 1, 0)
        for start, moving, face in ((0, incoming, x_low), (SIDE, backward_x, x_high)):
            turning = moving.index([pop for pop in moving if pop in inward][0])
            new = [None] * POPS
            for k, pop in enumerate(moving):
                new[pop] = face[5 + k]
            density, moment = moments_of(new)
            sums = [
                density + face[10],
                moment[0],
                moment[1] + face[11],
                moment[2] + face[12],
                face[5 + turning],
            ]
            found = [face[k, edge : edge + 1, :] for k in range(5)]
            found += [face[13, first + k : first + k + 1, :] for k in range(4)]
            found += [face[turning, second : second + 1, :]]
            found += [value[edge : edge + 1] for value in sums]
            for k, line in enumerate(found):
                target[start + k : start + k + 1, :] = line

    parity = lax.rem(lax.axis_index("span"), 2)

    @pl.when(parity == 0)
    def _():
        lines(True, e_same)
        lines(False, e_cross)

    @pl.when(parity == 1)
    def _():
        lines(False, e_same)
        lines(True, e_cross)


def back_kernel(tile_map, masks, tiles_hbm, back, tiles, arrived):
    @pl.when(lax.axis_index("stream") == 1)
    def _():
        copy = pltpu.make_async_copy(tiles_hbm, tiles, arrived)
        copy.start()
        copy.wait()
        width, coarse = tiles.shape[2:]
        sub = lax.broadcasted_iota(jnp.int32, (width, coarse), 0)
        open_layers = masks[0, :, :coarse] == 0
        for at, number in enumerate(neighbours(tile_map)):
            edges = [None] * POPS
            for pop, offset, row, slot in ((14, -1, 0, 14), (12, 1, width - 1, 15)):
                line = tile_at(tiles, number, (slot,), offset)[0][1:2]
                line = jnp.broadcast_to(line, (width, coarse))
                edges[pop] = jnp.where((sub == row) & open_layers, line, 0.0)
            density, moment = moments_of(edges)
            sums = tile_at(tiles, number, (0, 2, 3))
            back[at, 0] = sums[0] + density
            back[at, 1] = sums[1]
            back[at, 2] = sums[2] + moment[2]


def build_columns(is_left, col, corner, halo, edge, lines, x_low, x_high, masks):
    inward, outward = (forward_z, backward_z) if is_left else (backward_z, forward_z)
    rim, first = (0, 0) if is_left else (7, 4)
    for k in range(KEPT):
        col[k, 8:16, :] = halo[k]
    for k in range(5):
        col[KEPT + k, 8:16, :] = edge[outward[k]]
    corner[...] = jnp.zeros(corner.shape, jnp.float32)
    for moving, face, start, near, beyond, row in (
        (incoming, x_low, 0, 7, 6, 0),
        (backward_x, x_high, SIDE, 16, 17, 9),
    ):
        line = lambda k: lines[start + k : start + k + 1, :]
        for k in range(5):
            col[moving[k], near : near + 1, :] = line(k)
        for k, pop in enumerate([pop for pop in inward if pop in stays_x]):
            col[pop, near : near + 1, :] = line(5 + k)
        turning = [pop for pop in moving if pop in inward][0]
        leaving = [pop for pop in moving if pop in outward][0]
        col[turning, beyond : beyond + 1, :] = line(8)
        at = POPS + inward.index(turning)
        col[at, near : near + 1, :] = line(9)
        at = KEPT + outward.index(leaving)
        col[at, near : near + 1, :] = face[moving.index(leaving), rim : rim + 1, :]
        for k in range(4):
            corner[k, row : row + 1, :] = line(10 + k)
        at = 4 if moving is incoming else 5
        corner[at, row : row + 1, :] = line(14)
        for lanes, blocked in masks:
            missing = [None] * POPS
            for k, (pop, _) in enumerate(edge_lines(outward, moving, 0, 0)):
                step_y = velocities[pop][1]
                value = face[13, first + k : first + k + 1, lanes]
                value = shift_layers(jnp.broadcast_to(value, blocked[0].shape), step_y)
                missing[pop] = jnp.where(blocked[step_y] != 0, 0.0, value)
            density, moment = moments_of(missing)
            for k, value in enumerate([density] + moment):
                corner[k, row : row + 1, lanes] += value[:1]


def entry_at(row, at):
    lane = lax.broadcasted_iota(jnp.int32, row.shape, 1)
    return jnp.sum(jnp.where(lane == at, row[...].astype(jnp.float32), 0.0), axis=1, keepdims=True)


def neighbours(row):
    count = row.shape[1]
    position = lax.axis_index("span")
    return [entry_at(row, lax.rem(position + step, count)) for step in (count - 1, 0, 1)]


def tile_at(tiles, number, slots, offset=0):
    count = tiles.shape[0]
    found = [tiles[offset % count, slot] for slot in slots]
    for tile in range(1, count):
        here = jnp.broadcast_to(number, found[0].shape) == float(tile)
        found = [
            jnp.where(here, tiles[(tile + offset) % count, slot], value)
            for slot, value in zip(slots, found)
        ]
    return found


def fill_matrices(layer_phase, matrices):
    shape = matrices.shape[1:]
    rows = lax.broadcasted_iota(jnp.int32, shape, 0)
    fine = lax.broadcasted_iota(jnp.int32, shape, 1)
    choices = []
    for phase in (0, 1):
        position = fine + phase
        lower = lax.shift_right_arithmetic(position - 1, 1)
        upper_wt = jnp.where(position % 2 == 0, 0.75, 0.25)
        low_idx = jnp.clip(lower, 0, shape[0] - 1)
        high_idx = jnp.clip(lower + 1, 0, shape[0] - 1)
        choices.append(
            jnp.where(rows == low_idx, 1.0 - upper_wt, 0.0)
            + jnp.where(rows == high_idx, upper_wt, 0.0)
        )
    for tile, phase in enumerate(neighbours(layer_phase)):
        chosen = jnp.where(jnp.broadcast_to(phase, shape) > 0.5, choices[1], choices[0])
        matrices[tile] = chosen.astype(jnp.bfloat16)


def refine(planes, matrices):
    refined = []
    for tile, group in enumerate(planes):
        parts = []
        rest = jnp.concatenate(group, axis=0)
        for _ in range(3):
            parts.append(rest.astype(jnp.bfloat16))
            rest = rest - parts[-1].astype(jnp.float32)
        total = None
        for part in reversed(parts):
            product = jnp.dot(part, matrices[tile], preferred_element_type=jnp.float32)
            total = product if total is None else total + product
        refined.append(total.reshape(len(group), group[0].shape[0], total.shape[1]))
    return refined


def lanes_of(coarse, fine):
    return slice(0, coarse), slice(coarse, coarse + fine)


def masks_of(masks, lanes, height=8):
    values = {step: masks[step % 3, :, lanes] for step in (0, 1, -1)}
    if height == 8:
        return values
    return {
        step: jnp.broadcast_to(value[:1], (height, value.shape[1]))
        for step, value in values.items()
    }


def middle_kernel(
    tile_map,
    layer_phase,
    masks,
    star_pre,
    star_main,
    cross,
    same,
    edge_same,
    edge_cross,
    tiles_hbm,
    mid_pre,
    mid_main,
    inflow,
    awaited,
    matrices,
    out_pre_hbm,
    out_main_hbm,
    ghost_left,
    ghost_right,
    rim_left,
    rim_right,
    out_pre,
    out_main,
    tiles,
    arrived,
    sent,
):
    rows, width, coarse = star_pre.shape[1:]
    fine = star_main.shape[3]
    parity = lax.rem(lax.axis_index("span"), 2)

    on_inlet = lax.axis_index("stream") == 0
    copy = pltpu.make_async_copy(tiles_hbm, tiles, arrived)

    @pl.when(on_inlet)
    def _():
        copy.start()

    def ghosts(is_left, ghost, halo, edge, rim):
        inward, outward = (forward_z, backward_z) if is_left else (backward_z, forward_z)
        for k in range(5):
            ghost[k] = halo[inward[k]]
        for lanes in lanes_of(coarse, fine):
            new = column_values(
                is_left,
                lambda pop: halo[pop, :, lanes],
                lambda k: halo[POPS + k, :, lanes],
                lambda k: edge[outward[k], :, lanes],
                turned,
                masks_of(masks, lanes),
            )
            out = collide(new, inward)
            for k in range(5):
                rim[k, :, lanes] = out[inward[k]]

    @pl.when(parity == 0)
    def _():
        ghosts(True, ghost_left, cross, edge_cross, rim_left)
        ghosts(False, ghost_right, same, edge_same, rim_right)

    @pl.when(parity == 1)
    def _():
        ghosts(True, ghost_left, same, edge_same, rim_left)
        ghosts(False, ghost_right, cross, edge_cross, rim_right)

    stars = (star_pre, star_main)

    def first_step(x_at):
        for domain, lanes in enumerate(lanes_of(coarse, fine)):
            new = moved_row(
                lambda pop, at: stars[domain][pop, at],
                lambda pop, at: ghost_left[forward_z.index(pop), at : at + 1, lanes],
                lambda pop, at: ghost_right[backward_z.index(pop), at : at + 1, lanes],
                masks_of(masks, lanes),
                x_at,
            )
            out = collide(new)
            for pop in range(POPS):
                (mid_pre, mid_main)[domain][pop, x_at - 1] = out[pop]

    copies = []

    def second_step(x_at):
        for domain, lanes in enumerate(lanes_of(coarse, fine)):
            new = moved_row(
                lambda pop, at: (mid_pre, mid_main)[domain][pop, at - 1],
                lambda pop, at: rim_left[forward_z.index(pop), at : at + 1, lanes],
                lambda pop, at: rim_right[backward_z.index(pop), at : at + 1, lanes],
                masks_of(masks, lanes),
                x_at,
            )
            kept = (out_pre, out_main)[domain]
            for pop in range(POPS):
                kept[pop, x_at - 2] = new[pop]
            copies.append(
                pltpu.make_async_copy(
                    kept.at[:, x_at - 2],
                    (out_pre_hbm, out_main_hbm)[domain].at[:, x_at],
                    sent.at[domain, x_at - 2],
                )
            )
            copies[-1].start()

    for x_at in range(1, rows - 1):
        first_step(x_at)
        if x_at >= 3:
            second_step(x_at - 1)

    @pl.when(on_inlet)
    def _():
        copy.wait()
        planes = []
        blocked = masks_of(masks, slice(0, coarse))
        sub = lax.broadcasted_iota(jnp.int32, (width, coarse), 0)
        for place, number in enumerate(neighbours(tile_map)):
            found = tile_at(tiles, number, range(14))
            planes.append(found[:5])
            edges = [None] * POPS
            for pops, offset, row, slot in (
                (forward_z, -1, 0, 14),
                (backward_z, 1, width - 1, 15),
            ):
                lines = tile_at(tiles, number, (slot,), offset)[0]
                for k, pop in enumerate(pops):
                    line = jnp.broadcast_to(lines[k : k + 1], (width, coarse))
                    line = shift_layers(line, velocities[pop][1])
                    keep = (sub == row) & (blocked[velocities[pop][1]] == 0)
                    edges[pop] = jnp.where(keep, line, 0.0)
            density, moment = moments_of(edges)
            for k, value in enumerate([density] + moment):
                awaited[place, k] = found[10 + k] + value
            for k, pop in enumerate(incoming):
                new = found[5 + k]
                awaited[place, 4 + k] = new if edges[pop] is None else new + edges[pop]
        fill_matrices(layer_phase, matrices)
        for place, value in enumerate(refine(planes, matrices)):
            inflow[place] = value

    for copy_out in copies:
        copy_out.wait()


def last_kernel(
    masks,
    star_pre,
    star_main,
    mid_pre,
    mid_main,
    inflow,
    x_high,
    x_low,
    cross,
    same,
    edge_same,
    edge_cross,
    e_cross,
    e_same,
    part_pre,
    part_main,
    out_pre_hbm,
    out_main_hbm,
    kept_rows,
    col_left,
    col_right,
    corner_left,
    corner_right,
    in_low,
    in_high,
    next_pre,
    next_main,
    rim_left,
    rim_right,
    out_pre,
    out_main,
    sent,
):
    rows, width, coarse = star_pre.shape[1:]
    fine = star_main.shape[3]
    pre_lanes, main_lanes = lanes_of(coarse, fine)
    is_first = lax.axis_index("stream") == 0
    is_last = lax.axis_index("stream") == lax.axis_size("stream") - 1
    parity = lax.rem(lax.axis_index("span"), 2)
    ends = (x_low, x_high, [(lanes, masks_of(masks, lanes)) for lanes in (pre_lanes, main_lanes)])

    @pl.when(parity == 0)
    def _():
        build_columns(True, col_left, corner_left, cross, edge_cross, e_cross, *ends)
        build_columns(False, col_right, corner_right, same, edge_same, e_same, *ends)

    @pl.when(parity == 1)
    def _():
        build_columns(True, col_left, corner_left, same, edge_same, e_same, *ends)
        build_columns(False, col_right, corner_right, cross, edge_cross, e_cross, *ends)

    for k in range(5):
        in_low[k] = x_low[k, :, main_lanes]
        in_high[k] = x_high[k, :, main_lanes]

    @pl.when(is_last)
    def _():
        for k in range(5):
            in_high[k] = star_main[backward_x[k], rows - 1]
        for col in (col_left, col_right):
            for k in range(KEPT + 5):
                col[k, 16:17, main_lanes] = col[k, 15:16, main_lanes]

    @pl.when(is_first)
    def _():
        before, own, after = (inflow.at[tile] for tile in range(3))
        for k in range(5):
            in_low[k] = own[k]
            col_left[incoming[k], 7:8, main_lanes] = before[k, width - 1 : width]
            col_right[incoming[k], 7:8, main_lanes] = after[k, 0:1]
        col_left[POPS + 1, 7:8, main_lanes] = before[3, width - 2 : width - 1]
        col_left[KEPT + 2, 7:8, main_lanes] = own[4, 0:1]
        col_right[POPS + 2, 7:8, main_lanes] = after[4, 1:2]
        col_right[KEPT + 1, 7:8, main_lanes] = own[3, width - 1 : width]

    for is_left, col, corner, rim in (
        (True, col_left, corner_left, rim_left),
        (False, col_right, corner_right, rim_right),
    ):
        moving = forward_z if is_left else backward_z
        for lanes in (pre_lanes, main_lanes):
            new = column_values(
                is_left,
                lambda pop, step_x=0: col[pop, 7 - step_x : 23 - step_x, lanes],
                lambda k, step_x: col[POPS + k, 7 - step_x : 23 - step_x, lanes],
                lambda k, step_x: col[KEPT + k, 7 - step_x : 23 - step_x, lanes],
                lambda read, at, step_x: read(at, step_x),
                masks_of(masks, lanes, 16),
            )
            row = lax.broadcasted_iota(jnp.int32, new[0].shape, 0)
            for pop in range(POPS):
                if pop not in backward_x:
                    new[pop] = jnp.where(row == 0, 0.0, new[pop])
                if pop not in incoming:
                    new[pop] = jnp.where(row == rows + 1, 0.0, new[pop])
            density, moment = moments_of(new)
            density = density + corner[0, :, lanes]
            moment = [moment[axis_num] + corner[1 + axis_num, :, lanes] for axis_num in range(3)]
            for at, ends_of in ((4, incoming), (5, backward_x)):
                pop = [pop for pop in moving if pop in ends_of][0]
                new[pop] = new[pop] + corner[at, :, lanes]
            out = relax(new, density, moment, moving)
            for k in range(5):
                rim[k, :, lanes] = out[moving[k]]

    stars = (star_pre, star_main)
    outer = {-1: 0, 0: 1, rows - 1: 2, rows: 3}

    def base_of(domain, lanes):
        def base(pop, x_at):
            if 0 <= x_at < rows:
                return stars[domain][pop, x_at]
            if x_at == -1:
                k = incoming.index(pop)
                return in_low[k] if domain == 1 else x_low[k, :, lanes]
            k = backward_x.index(pop)
            return in_high[k] if domain == 1 else x_high[k, :, lanes]

        return base

    def beside_tile(domain, lanes, x_at):
        star = stars[domain]
        face, moving, back = (
            (x_low, incoming, backward_x) if x_at < 0 else (x_high, backward_x, incoming)
        )
        blocked = masks_of(masks, lanes)
        left = lambda pop, at: col_left[pop, 8 + at : 9 + at, lanes]
        right = lambda pop, at: col_right[pop, 8 + at : 9 + at, lanes]

        def base(pop, at):
            return face[moving.index(pop), :, lanes] if at == x_at else star[pop, at]

        new = moved_row(base, left, right, blocked, x_at, back)
        sub = lax.broadcasted_iota(jnp.int32, new[back[0]].shape, 0)
        for pop in range(POPS):
            if pop in back:
                continue
            step_x, step_y, step_z = velocities[pop]
            if step_z != 0:
                line = (left if step_z == 1 else right)(pop, x_at - step_x)
                line = shift_layers(jnp.broadcast_to(line, sub.shape), step_y)
                keep = (sub == (0 if step_z == 1 else width - 1)) & (blocked[step_y] == 0)
                new[pop] = jnp.where(keep, line, 0.0)
            if pop in moving:
                part = face[5 + moving.index(pop), :, lanes]
                new[pop] = part if new[pop] is None else part + new[pop]
        density, moment = moments_of(new)
        density = density + face[10, :, lanes]
        moment = [moment[0], moment[1] + face[11, :, lanes], moment[2] + face[12, :, lanes]]
        return relax(new, density, moment, moving), moving

    def next_of(domain):
        def base(pop, x_at):
            if x_at in outer:
                return (next_pre, next_main)[domain][pop, outer[x_at]]
            return (mid_pre, mid_main)[domain][pop, x_at - 1]

        return base

    def end_row(x_at):
        for domain, lanes in enumerate((pre_lanes, main_lanes)):
            if 0 <= x_at < rows:
                new = moved_row(
                    base_of(domain, lanes),
                    lambda pop, at: col_left[pop, 8 + at : 9 + at, lanes],
                    lambda pop, at: col_right[pop, 8 + at : 9 + at, lanes],
                    masks_of(masks, lanes),
                    x_at,
                )
                out, wanted = collide(new), range(POPS)
            else:
                out, wanted = beside_tile(domain, lanes, x_at)
            for pop in wanted:
                (next_pre, next_main)[domain][pop, outer[x_at]] = out[pop]

    copies = []

    def second_step(at_end, x_at):
        for domain, lanes in enumerate((pre_lanes, main_lanes)):
            new = moved_row(
                next_of(domain),
                lambda pop, at: rim_left[forward_z.index(pop), at + 1 : at + 2, lanes],
                lambda pop, at: rim_right[backward_z.index(pop), at + 1 : at + 2, lanes],
                masks_of(masks, lanes),
                x_at,
            )
            kept = (out_pre, out_main)[domain]
            for pop in range(POPS):
                kept[pop, at_end] = new[pop]
            copies.append(
                pltpu.make_async_copy(
                    kept.at[:, at_end],
                    (out_pre_hbm, out_main_hbm)[domain].at[:, x_at],
                    sent.at[domain, at_end],
                )
            )
            copies[-1].start()

    end_row(0)
    for k in range(5):
        kept_rows[k] = next_main[backward_x[k], 1]
    second_step(0, 1)
    end_row(-1)
    second_step(1, 0)
    end_row(rows - 1)
    second_step(2, rows - 2)
    end_row(rows)

    @pl.when(is_last)
    def _():
        for k in range(5):
            next_main[backward_x[k], 3] = next_main[backward_x[k], 2]
            for rim in (rim_left, rim_right):
                rim[k, rows + 1 : rows + 2, main_lanes] = rim[k, rows : rows + 1, main_lanes]

    second_step(3, rows - 1)
    for copy in copies:
        copy.wait()


def inlet_kernel(matrices, masks, awaited, back, kept_rows, main_hbm, out_hbm, ready, sent):
    @pl.when(lax.axis_index("stream") == 0)
    def _():
        width, coarse = awaited.shape[2:]
        fine = masks.shape[2] - coarse
        planes = []
        for place in range(3):
            density = awaited[place, 0] + back[place, 0]
            moment = [
                awaited[place, 1] - back[place, 0],
                awaited[place, 2] + back[place, 1],
                awaited[place, 3] + back[place, 2],
            ]
            new = [None] * POPS
            for k, pop in enumerate(incoming):
                new[pop] = awaited[place, 4 + k]
            out = relax(new, density, moment, incoming)
            planes.append([out[pop] for pop in incoming])
        before, own, after = refine(planes, matrices)

        def base(pop, x_at):
            return own[incoming.index(pop)] if x_at < 0 else kept_rows[backward_x.index(pop)]

        new = moved_row(
            base,
            lambda pop, x_at: before[incoming.index(pop), width - 1 : width],
            lambda pop, x_at: after[incoming.index(pop), 0:1],
            masks_of(masks, slice(coarse, coarse + fine)),
            0,
            incoming,
        )
        copies = []
        for k, pop in enumerate(incoming):
            ready[k] = new[pop]
            copies.append(pltpu.make_async_copy(ready.at[k], out_hbm.at[pop, 0], sent.at[k]))
            copies[-1].start()
        for copy in copies:
            copy.wait()


def f32(*shape):
    return jax.ShapeDtypeStruct(shape, jnp.float32)


def local(pre_pops, main_pops, tile_map, layer_phase, wall_flags):
    span_count = lax.axis_size("span")
    stream_count = lax.axis_size("stream")
    _, rows, width, coarse = pre_pops.shape
    fine = main_pops.shape[3]
    lanes = coarse + fine

    def send(value, step_x, place, only=range(stream_count)):
        moves = []
        for s in range(stream_count):
            if s not in only:
                continue
            for j in range(span_count):
                target = (s + step_x) % stream_count * span_count + place(j) % span_count
                moves.append((s * span_count + j, target))
        return lax.ppermute(value, ("stream", "span"), moves)

    def swap_in_pairs(value):
        moves = []
        for s in range(stream_count):
            other = min(s ^ 1, stream_count - 1)
            moves += [(s * span_count + j, other * span_count + j) for j in range(span_count)]
        return lax.ppermute(value, ("stream", "span"), moves)

    stay = lambda j: j
    sibling = lambda j: j + 1 if j % 2 == 0 else j - 1
    beyond = lambda j: j - 1 if j % 2 == 0 else j + 1
    params = pltpu.CompilerParams(vmem_limit_bytes=VMEM_SMALL)

    whole = pl.BlockSpec(memory_space=pltpu.VMEM)
    outside = pl.BlockSpec(memory_space=pltpu.HBM)
    tile_row, phase_row = (row.reshape(1, span_count) for row in (tile_map, layer_phase))

    in_hbm = lambda value: pltpu.with_memory_space_constraint(value, pltpu.HBM)
    star_pre, star_main, z_same, z_cross = pl.pallas_call(
        first_kernel,
        out_shape=(
            f32(*pre_pops.shape),
            f32(*main_pops.shape),
            f32(KEPT, rows, lanes),
            f32(KEPT, rows, lanes),
        ),
        in_specs=[outside, outside],
        scratch_shapes=[
            pltpu.VMEM(pre_pops.shape, jnp.float32),
            pltpu.VMEM(main_pops.shape, jnp.float32),
            pltpu.SemaphoreType.DMA((2, rows)),
        ],
        compiler_params=pltpu.CompilerParams(vmem_limit_bytes=VMEM_SMALL),
        name="collide_and_pack",
    )(in_hbm(pre_pops), in_hbm(main_pops))
    masks, x_hi, x_lo, plane = pl.pallas_call(
        face_kernel,
        out_shape=(
            f32(3, 8, lanes),
            f32(FACE, width, lanes),
            f32(FACE, width, lanes),
            f32(PLANE, width, coarse),
        ),
        compiler_params=params,
        name="faces",
    )(wall_flags.reshape(1, fine), star_pre, star_main)

    same = send(z_same, 0, sibling)
    cross = send(z_cross, 0, beyond)
    x_low = send(x_hi, 1, stay)
    x_high = send(x_lo, -1, stay)
    tiles = lax.all_gather(plane, "span", axis=0, tiled=False)
    anywhere = pl.BlockSpec(memory_space=pl.ANY)
    all_tiles = [
        pltpu.VMEM((span_count, PLANE, width, coarse), jnp.float32),
        pltpu.SemaphoreType.DMA,
    ]
    e_to_same, e_to_cross = pl.pallas_call(
        corner_kernel,
        out_shape=(f32(2 * SIDE, lanes), f32(2 * SIDE, lanes)),
        in_specs=[whole] * 2 + [anywhere],
        compiler_params=params,
        name="corners",
    )(x_high, x_low, tiles)
    e_same = send(e_to_same, 0, sibling)
    e_cross = send(e_to_cross, 0, beyond)
    back = pl.pallas_call(
        back_kernel,
        out_shape=f32(3, 3, width, coarse),
        in_specs=[whole, whole, anywhere],
        scratch_shapes=all_tiles,
        compiler_params=params,
        name="behind_plane",
    )(tile_row, masks, tiles)
    back = swap_in_pairs(back)
    half_pre = pltpu.VMEM((POPS, 4, width, coarse), jnp.float32)
    half_main = pltpu.VMEM((POPS, 4, width, fine), jnp.float32)
    mid_pre, mid_main, inflow, awaited, matrices, part_pre, part_main = pl.pallas_call(
        middle_kernel,
        out_shape=(
            f32(POPS, rows - 2, width, coarse),
            f32(POPS, rows - 2, width, fine),
            f32(3, 5, width, fine),
            f32(3, 9, width, coarse),
            jax.ShapeDtypeStruct((3, coarse, fine), jnp.bfloat16),
            f32(*pre_pops.shape),
            f32(*main_pops.shape),
        ),
        in_specs=[whole] * 9 + [anywhere],
        out_specs=[whole] * 5 + [outside] * 2,
        scratch_shapes=[
            pltpu.VMEM((5, rows, lanes), jnp.float32),
            pltpu.VMEM((5, rows, lanes), jnp.float32),
            pltpu.VMEM((5, rows, lanes), jnp.float32),
            pltpu.VMEM((5, rows, lanes), jnp.float32),
            pltpu.VMEM((POPS, rows - 4, width, coarse), jnp.float32),
            pltpu.VMEM((POPS, rows - 4, width, fine), jnp.float32),
        ]
        + all_tiles
        + [pltpu.SemaphoreType.DMA((2, rows - 4))],
        compiler_params=params,
        name="middle_rows",
    )(tile_row, phase_row, masks, star_pre, star_main, cross, same, z_same, z_cross, tiles)
    out_pre, out_main, kept_rows = pl.pallas_call(
        last_kernel,
        out_shape=(f32(*pre_pops.shape), f32(*main_pops.shape), f32(5, width, fine)),
        in_specs=[whole] * 14 + [outside] * 2,
        out_specs=(outside, outside, whole),
        input_output_aliases={14: 0, 15: 1},
        scratch_shapes=[
            pltpu.VMEM((KEPT + 5, 24, lanes), jnp.float32),
            pltpu.VMEM((KEPT + 5, 24, lanes), jnp.float32),
            pltpu.VMEM((6, 16, lanes), jnp.float32),
            pltpu.VMEM((6, 16, lanes), jnp.float32),
            pltpu.VMEM((5, width, fine), jnp.float32),
            pltpu.VMEM((5, width, fine), jnp.float32),
            half_pre,
            half_main,
            pltpu.VMEM((5, 16, lanes), jnp.float32),
            pltpu.VMEM((5, 16, lanes), jnp.float32),
            half_pre,
            half_main,
            pltpu.SemaphoreType.DMA((2, 4)),
        ],
        compiler_params=pltpu.CompilerParams(vmem_limit_bytes=VMEM_LARGE),
        name="last_rows",
    )(
        masks,
        star_pre,
        star_main,
        mid_pre,
        mid_main,
        inflow,
        x_high,
        x_low,
        cross,
        same,
        z_same,
        z_cross,
        e_cross,
        e_same,
        part_pre,
        part_main,
    )
    out_main = pl.pallas_call(
        inlet_kernel,
        out_shape=f32(*main_pops.shape),
        in_specs=[whole] * 5 + [outside],
        out_specs=outside,
        input_output_aliases={5: 0},
        scratch_shapes=[
            pltpu.VMEM((5, width, fine), jnp.float32),
            pltpu.SemaphoreType.DMA((5,)),
        ],
        compiler_params=params,
        name="inlet_row",
    )(matrices, masks, awaited, back, kept_rows, out_main)
    return out_pre, out_main


def solution(mesh):
    return jax.shard_map(
        local,
        mesh=mesh,
        in_specs=(P(None, "stream", "span", None), P(None, "stream", "span", None), P(), P(), P()),
        out_specs=(P(None, "stream", "span", None), P(None, "stream", "span", None)),
        check_vma=False,
    )
```

```python
import jax
import jax.numpy as jnp
from jax import lax
from jax.experimental import pallas as pl
from jax.experimental.pallas import tpu as pltpu
from jax.sharding import PartitionSpec as P

velocities = (
    (0, 0, 0),
    (1, 0, 0),
    (-1, 0, 0),
    (0, 1, 0),
    (0, -1, 0),
    (0, 0, 1),
    (0, 0, -1),
    (1, 1, 0),
    (-1, -1, 0),
    (1, -1, 0),
    (-1, 1, 0),
    (1, 0, 1),
    (-1, 0, -1),
    (1, 0, -1),
    (-1, 0, 1),
    (0, 1, 1),
    (0, -1, -1),
    (0, 1, -1),
    (0, -1, 1),
)
opposite = (0, 2, 1, 4, 3, 6, 5, 8, 7, 10, 9, 12, 11, 14, 13, 16, 15, 18, 17)
pairs = tuple((k, k + 1) for k in range(1, 19, 2))
incoming = (1, 7, 9, 11, 13)
backward_x = (2, 8, 10, 12, 14)
forward_z = (5, 11, 14, 15, 18)
backward_z = (6, 12, 13, 16, 17)
POPS = 19
PLANE = 16
FACE = 14
SIDE = 16
stays_x = tuple(k for k in range(POPS) if velocities[k][0] == 0)
KEPT = POPS + 5
VMEM_SMALL = 10 * 1024 * 1024
VMEM_LARGE = 20 * 1024 * 1024


def moments_of(pops):
    density = None
    moment = [None, None, None]

    def add(total, value):
        return value if total is None else total + value

    for group, weight in ((range(1, 7), 1.0 / 18.0), (range(7, POPS), 1.0 / 36.0)):
        part = None
        parts = [None, None, None]
        for a, b in ((k, k + 1) for k in group[::2]):
            if pops[a] is None and pops[b] is None:
                continue
            if pops[b] is None:
                both, diff = pops[a], pops[a]
            elif pops[a] is None:
                both, diff = pops[b], -pops[b]
            else:
                both, diff = pops[a] + pops[b], pops[a] - pops[b]
            part = add(part, both)
            for axis_num, step in enumerate(velocities[a]):
                if step != 0:
                    parts[axis_num] = add(parts[axis_num], diff if step == 1 else -diff)
        if part is not None:
            density = add(density, part * weight)
        for axis_num in range(3):
            if parts[axis_num] is not None:
                moment[axis_num] = add(moment[axis_num], parts[axis_num] * weight)
    if pops[0] is not None:
        density = add(density, pops[0] * (1.0 / 3.0))
    return density, moment


def relax(pops, density, moment, wanted):
    inverse = 1.0 / density
    speed = [component * inverse for component in moment]
    kinetic = moment[0] * speed[0] + moment[1] * speed[1] + moment[2] * speed[2]
    base = 1.25 * density - 1.875 * kinetic
    result = [None] * POPS
    if 0 in wanted:
        result[0] = base - 0.25 * pops[0]
    for a, b in pairs:
        if a not in wanted and b not in wanted:
            continue
        flux = None
        along = None
        for axis_num, step in enumerate(velocities[a]):
            if step == 0:
                continue
            if flux is None:
                flux, along = moment[axis_num], speed[axis_num]
            elif step == 1:
                flux, along = flux + moment[axis_num], along + speed[axis_num]
            else:
                flux, along = flux - moment[axis_num], along - speed[axis_num]
        even = base + 5.625 * (flux * along)
        odd = 3.75 * flux
        if a in wanted:
            result[a] = even + odd - 0.25 * pops[a]
        if b in wanted:
            result[b] = even - odd - 0.25 * pops[b]
    return result


def collide(pops, wanted=range(POPS)):
    density, moment = moments_of(pops)
    return relax(pops, density, moment, wanted)


def shift_layers(value, step_y):
    if step_y == 0:
        return value
    size = value.shape[-1]
    return pltpu.roll(value, step_y % size, value.ndim - 1)


def moved_row(base, left, right, masks, x_at, wanted=range(POPS)):
    result = []
    sub = None
    for which_pop in range(POPS):
        if which_pop not in wanted:
            result.append(None)
            continue
        step_x, step_y, step_z = velocities[which_pop]
        source = base(which_pop, x_at - step_x)
        if step_z != 0 and sub is None:
            sub = lax.broadcasted_iota(jnp.int32, source.shape, 0)
        width = source.shape[0]
        if step_z == 1:
            source = jnp.where(
                sub == 0, left(which_pop, x_at - step_x), pltpu.roll(source, 1, 0)
            )
        elif step_z == -1:
            source = jnp.where(
                sub == width - 1,
                right(which_pop, x_at - step_x),
                pltpu.roll(source, width - 1, 0),
            )
        source = shift_layers(source, step_y)
        result.append(
            jnp.where(masks[step_y] != 0, base(opposite[which_pop], x_at), source)
        )
    return result


def fill_masks(walls, masks):
    fine = walls.shape[1]
    coarse = masks.shape[2] - fine

    def fill(solid, lanes):
        layers = solid.shape[1]
        lane = lax.broadcasted_iota(jnp.int32, solid.shape, 1)
        masks[0, :, lanes] = solid
        masks[1, :, lanes] = jnp.where(lane == 0, 1.0, pltpu.roll(solid, 1, 1))
        masks[2, :, lanes] = jnp.where(lane == layers - 1, 1.0, pltpu.roll(solid, layers - 1, 1))

    solid = jnp.broadcast_to(jnp.where(walls[...] > 0, 1.0, 0.0), (8, fine))
    fine_at = lax.broadcasted_iota(jnp.int32, (fine, coarse), 0)
    coarse_at = lax.broadcasted_iota(jnp.int32, (fine, coarse), 1)
    halves = jnp.where(lax.shift_right_logical(fine_at, 1) == coarse_at, 1.0, 0.0)
    hits = jnp.dot(solid, halves, preferred_element_type=jnp.float32)
    fill(jnp.where(hits > 0.5, 1.0, 0.0), slice(0, coarse))
    fill(solid, slice(coarse, coarse + fine))


def first_kernel(
    pre_hbm,
    main_hbm,
    star_pre,
    star_main,
    z_same,
    z_cross,
    pre,
    main,
    arrived,
):
    rows = pre.shape[1]
    coarse = pre.shape[3]
    parity = lax.rem(lax.axis_index("span"), 2)
    domains = ((pre, star_pre, slice(0, coarse)), (main, star_main, slice(coarse, None)))
    copies = [
        [
            pltpu.make_async_copy(source.at[:, x_at], target.at[:, x_at], arrived.at[at, x_at])
            for at, (source, target) in enumerate(((pre_hbm, pre), (main_hbm, main)))
        ]
        for x_at in range(rows)
    ]
    for row in copies:
        for copy in row:
            copy.start()
    for x_at in range(rows):
        for copy in copies[x_at]:
            copy.wait()
        for pops, star, lanes in domains:
            out = collide([pops[which_pop, x_at] for which_pop in range(POPS)])
            for which_pop in range(POPS):
                star[which_pop, x_at] = out[which_pop]

    def edges(hi, lo):
        for _, star, lanes in domains:
            width = star.shape[2]
            for which_pop in range(POPS):
                hi[which_pop, :, lanes] = star[which_pop, :, width - 1, :]
                lo[which_pop, :, lanes] = star[which_pop, :, 0, :]
            for k in range(5):
                hi[POPS + k, :, lanes] = star[forward_z[k], :, width - 2, :]
                lo[POPS + k, :, lanes] = star[backward_z[k], :, 1, :]

    @pl.when(parity == 0)
    def _():
        edges(z_same, z_cross)

    @pl.when(parity == 1)
    def _():
        edges(z_cross, z_same)


def edge_lines(pops, moving, rim, inner):
    return [(pop, rim) for pop in pops if pop in stays_x] + [
        (pop, inner) for pop in pops if pop in moving
    ]


def fill_face(star, lanes, blocked, at_top, face):
    last = star.shape[1] - 1
    moving = incoming if at_top else backward_x
    rim = last if at_top else 0
    none = lambda pop, x_at: 0.0
    base = lambda pop, x_at: star[pop, x_at]
    new = moved_row(base, none, none, blocked, rim, moving + stays_x)
    for k, pop in enumerate(moving):
        face[k, :, lanes] = star[pop, rim]
        face[5 + k, :, lanes] = new[pop]
        new[pop] = None
    density, moment = moments_of(new)
    face[10, :, lanes] = density
    face[11, :, lanes] = moment[1]
    face[12, :, lanes] = moment[2]
    inner = rim - 1 if at_top else rim + 1
    for first, pops, z_at in ((0, backward_z, 0), (4, forward_z, star.shape[2] - 1)):
        for k, (pop, x_at) in enumerate(edge_lines(pops, moving, rim, inner)):
            row = first + k
            face[13, row : row + 1, lanes] = star[pop, x_at, z_at : z_at + 1, :]


def face_kernel(walls, star_pre, star_main, masks, x_hi, x_lo, plane):
    coarse = star_pre.shape[3]
    fill_masks(walls, masks)
    for star, lanes in zip((star_pre, star_main), lanes_of(coarse, star_main.shape[3])):
        blocked = masks_of(masks, lanes)
        fill_face(star, lanes, blocked, True, x_hi)
        fill_face(star, lanes, blocked, False, x_lo)
    fill_plane(star_pre, masks_of(masks, slice(0, coarse)), plane)


def fill_plane(star, blocked, plane):
    width, coarse = plane.shape[1:]
    last = star.shape[1] - 1
    zero = jnp.zeros((width, coarse), jnp.float32)
    stream_pos = lax.axis_index("stream")

    @pl.when(stream_pos != 1)
    def _():
        base = lambda pop, x_at: zero if x_at > last else star[pop, x_at]
        none = lambda pop, x_at: 0.0
        new = moved_row(base, none, none, blocked, last)
        density, moment = moments_of(new)
        for k, pop in enumerate(incoming):
            plane[k] = star[pop, last]
            plane[5 + k] = new[pop]
        plane[10] = density
        for axis_num in range(3):
            plane[11 + axis_num] = moment[axis_num]
        plane[14] = zero
        plane[15] = zero
        for k in range(5):
            hi, lo = forward_z[k], backward_z[k]
            plane[14, k : k + 1, :] = base(hi, last - velocities[hi][0])[width - 1 : width]
            plane[15, k : k + 1, :] = base(lo, last - velocities[lo][0])[0:1]

    @pl.when(stream_pos == 1)
    def _():
        none = lambda pop, x_at: 0.0
        back = moved_row(
            lambda pop, x_at: star[pop, x_at] if pop in backward_x else zero,
            none,
            none,
            blocked,
            -1,
            backward_x,
        )
        density, moment = moments_of(back)
        for k, value in enumerate([density] + moment):
            plane[k] = value
        for k in range(4, PLANE):
            plane[k] = zero
        plane[14, 1:2, :] = star[14, 0, width - 1 : width, :]
        plane[15, 1:2, :] = star[12, 0, 0:1, :]


def column_values(is_left, first, second, inner, shift, blocked):
    inward, outward = (forward_z, backward_z) if is_left else (backward_z, forward_z)
    result = []
    for pop in range(POPS):
        step_x, step_y, _ = velocities[pop]
        if pop in inward:
            source = shift(second, inward.index(pop), step_x)
        elif pop in outward:
            source = shift(inner, outward.index(pop), step_x)
        else:
            source = shift(first, pop, step_x)
        result.append(
            jnp.where(blocked[step_y] != 0, first(opposite[pop]), shift_layers(source, step_y))
        )
    return result


def turned(read, at, step_x):
    value = read(at)
    return value if step_x == 0 else pltpu.roll(value, step_x % value.shape[0], 0)


def only(pops, values):
    return [values[pop] if pop in pops else None for pop in range(POPS)]


def corner_kernel(x_high, x_low, tiles, e_same, e_cross):
    def lines(is_left, target):
        inward = forward_z if is_left else backward_z
        edge, second, first = (7, 6, 4) if is_left else (0, 1, 0)
        for start, moving, face in ((0, incoming, x_low), (SIDE, backward_x, x_high)):
            turning = moving.index([pop for pop in moving if pop in inward][0])
            new = [None] * POPS
            for k, pop in enumerate(moving):
                new[pop] = face[5 + k]
            density, moment = moments_of(new)
            sums = [
                density + face[10],
                moment[0],
                moment[1] + face[11],
                moment[2] + face[12],
                face[5 + turning],
            ]
            found = [face[k, edge : edge + 1, :] for k in range(5)]
            found += [face[13, first + k : first + k + 1, :] for k in range(4)]
            found += [face[turning, second : second + 1, :]]
            found += [value[edge : edge + 1] for value in sums]
            for k, line in enumerate(found):
                target[start + k : start + k + 1, :] = line

    parity = lax.rem(lax.axis_index("span"), 2)

    @pl.when(parity == 0)
    def _():
        lines(True, e_same)
        lines(False, e_cross)

    @pl.when(parity == 1)
    def _():
        lines(False, e_same)
        lines(True, e_cross)


def back_kernel(tile_map, masks, tiles_hbm, back, tiles, arrived):
    @pl.when(lax.axis_index("stream") == 1)
    def _():
        copy = pltpu.make_async_copy(tiles_hbm, tiles, arrived)
        copy.start()
        copy.wait()
        width, coarse = tiles.shape[2:]
        sub = lax.broadcasted_iota(jnp.int32, (width, coarse), 0)
        open_layers = masks[0, :, :coarse] == 0
        for at, number in enumerate(neighbours(tile_map)):
            edges = [None] * POPS
            for pop, offset, row, slot in ((14, -1, 0, 14), (12, 1, width - 1, 15)):
                line = tile_at(tiles, number, (slot,), offset)[0][1:2]
                line = jnp.broadcast_to(line, (width, coarse))
                edges[pop] = jnp.where((sub == row) & open_layers, line, 0.0)
            density, moment = moments_of(edges)
            sums = tile_at(tiles, number, (0, 2, 3))
            for k, value in enumerate((sums[0] + density, sums[1], sums[2] + moment[2])):
                if at == 1:
                    back[k] = value
                else:
                    line, edge = (k, width - 1) if at == 0 else (3 + k, 0)
                    back[3, line : line + 1, :] = value[edge : edge + 1]


def build_columns(is_left, col, corner, halo, edge, lines, x_low, x_high, masks):
    inward, outward = (forward_z, backward_z) if is_left else (backward_z, forward_z)
    rim, first = (0, 0) if is_left else (7, 4)
    for k in range(KEPT):
        col[k, 8:16, :] = halo[k]
    for k in range(5):
        col[KEPT + k, 8:16, :] = edge[outward[k]]
    corner[...] = jnp.zeros(corner.shape, jnp.float32)
    for moving, face, start, near, beyond, row in (
        (incoming, x_low, 0, 7, 6, 0),
        (backward_x, x_high, SIDE, 16, 17, 9),
    ):
        line = lambda k: lines[start + k : start + k + 1, :]
        for k in range(5):
            col[moving[k], near : near + 1, :] = line(k)
        for k, pop in enumerate([pop for pop in inward if pop in stays_x]):
            col[pop, near : near + 1, :] = line(5 + k)
        turning = [pop for pop in moving if pop in inward][0]
        leaving = [pop for pop in moving if pop in outward][0]
        col[turning, beyond : beyond + 1, :] = line(8)
        at = POPS + inward.index(turning)
        col[at, near : near + 1, :] = line(9)
        at = KEPT + outward.index(leaving)
        col[at, near : near + 1, :] = face[moving.index(leaving), rim : rim + 1, :]
        for k in range(4):
            corner[k, row : row + 1, :] = line(10 + k)
        at = 4 if moving is incoming else 5
        corner[at, row : row + 1, :] = line(14)
        for lanes, blocked in masks:
            missing = [None] * POPS
            for k, (pop, _) in enumerate(edge_lines(outward, moving, 0, 0)):
                step_y = velocities[pop][1]
                value = face[13, first + k : first + k + 1, lanes]
                value = shift_layers(jnp.broadcast_to(value, blocked[0].shape), step_y)
                missing[pop] = jnp.where(blocked[step_y] != 0, 0.0, value)
            density, moment = moments_of(missing)
            for k, value in enumerate([density] + moment):
                corner[k, row : row + 1, lanes] += value[:1]


def entry_at(row, at):
    lane = lax.broadcasted_iota(jnp.int32, row.shape, 1)
    return jnp.sum(jnp.where(lane == at, row[...].astype(jnp.float32), 0.0), axis=1, keepdims=True)


def neighbours(row):
    count = row.shape[1]
    position = lax.axis_index("span")
    return [entry_at(row, lax.rem(position + step, count)) for step in (count - 1, 0, 1)]


def tile_at(tiles, number, slots, offset=0):
    count = tiles.shape[0]
    found = [tiles[offset % count, slot] for slot in slots]
    for tile in range(1, count):
        here = jnp.broadcast_to(number, found[0].shape) == float(tile)
        found = [
            jnp.where(here, tiles[(tile + offset) % count, slot], value)
            for slot, value in zip(slots, found)
        ]
    return found


def fill_matrices(layer_phase, matrices):
    shape = matrices.shape[1:]
    rows = lax.broadcasted_iota(jnp.int32, shape, 0)
    fine = lax.broadcasted_iota(jnp.int32, shape, 1)
    choices = []
    for phase in (0, 1):
        position = fine + phase
        lower = lax.shift_right_arithmetic(position - 1, 1)
        upper_wt = jnp.where(position % 2 == 0, 0.75, 0.25)
        low_idx = jnp.clip(lower, 0, shape[0] - 1)
        high_idx = jnp.clip(lower + 1, 0, shape[0] - 1)
        choices.append(
            jnp.where(rows == low_idx, 1.0 - upper_wt, 0.0)
            + jnp.where(rows == high_idx, upper_wt, 0.0)
        )
    for tile, phase in enumerate(neighbours(layer_phase)):
        chosen = jnp.where(jnp.broadcast_to(phase, shape) > 0.5, choices[1], choices[0])
        matrices[tile] = chosen.astype(jnp.bfloat16)


def refine(planes, matrices):
    refined = []
    for tile, group in enumerate(planes):
        parts = []
        rest = jnp.concatenate(group, axis=0)
        for _ in range(3):
            parts.append(rest.astype(jnp.bfloat16))
            rest = rest - parts[-1].astype(jnp.float32)
        total = None
        for part in reversed(parts):
            product = jnp.dot(part, matrices[tile], preferred_element_type=jnp.float32)
            total = product if total is None else total + product
        refined.append(total.reshape(len(group), group[0].shape[0], total.shape[1]))
    return refined


def lanes_of(coarse, fine):
    return slice(0, coarse), slice(coarse, coarse + fine)


def masks_of(masks, lanes, height=8):
    values = {step: masks[step % 3, :, lanes] for step in (0, 1, -1)}
    if height == 8:
        return values
    return {
        step: jnp.broadcast_to(value[:1], (height, value.shape[1]))
        for step, value in values.items()
    }


def middle_kernel(
    tile_map,
    layer_phase,
    masks,
    star_pre,
    star_main,
    cross,
    same,
    edge_same,
    edge_cross,
    tiles_hbm,
    mid_pre,
    mid_main,
    inflow,
    awaited,
    matrices,
    out_pre_hbm,
    out_main_hbm,
    ghost_left,
    ghost_right,
    rim_left,
    rim_right,
    out_pre,
    out_main,
    tiles,
    arrived,
    sent,
):
    rows, width, coarse = star_pre.shape[1:]
    fine = star_main.shape[3]
    parity = lax.rem(lax.axis_index("span"), 2)

    on_inlet = lax.axis_index("stream") == 0
    copy = pltpu.make_async_copy(tiles_hbm, tiles, arrived)

    @pl.when(on_inlet)
    def _():
        copy.start()

    def ghosts(is_left, ghost, halo, edge, rim):
        inward, outward = (forward_z, backward_z) if is_left else (backward_z, forward_z)
        for k in range(5):
            ghost[k] = halo[inward[k]]
        for lanes in lanes_of(coarse, fine):
            new = column_values(
                is_left,
                lambda pop: halo[pop, :, lanes],
                lambda k: halo[POPS + k, :, lanes],
                lambda k: edge[outward[k], :, lanes],
                turned,
                masks_of(masks, lanes),
            )
            out = collide(new, inward)
            for k in range(5):
                rim[k, :, lanes] = out[inward[k]]

    @pl.when(parity == 0)
    def _():
        ghosts(True, ghost_left, cross, edge_cross, rim_left)
        ghosts(False, ghost_right, same, edge_same, rim_right)

    @pl.when(parity == 1)
    def _():
        ghosts(True, ghost_left, same, edge_same, rim_left)
        ghosts(False, ghost_right, cross, edge_cross, rim_right)

    stars = (star_pre, star_main)

    def first_step(x_at):
        for domain, lanes in enumerate(lanes_of(coarse, fine)):
            new = moved_row(
                lambda pop, at: stars[domain][pop, at],
                lambda pop, at: ghost_left[forward_z.index(pop), at : at + 1, lanes],
                lambda pop, at: ghost_right[backward_z.index(pop), at : at + 1, lanes],
                masks_of(masks, lanes),
                x_at,
            )
            out = collide(new)
            for pop in range(POPS):
                (mid_pre, mid_main)[domain][pop, x_at - 1] = out[pop]

    copies = []

    def second_step(x_at):
        for domain, lanes in enumerate(lanes_of(coarse, fine)):
            new = moved_row(
                lambda pop, at: (mid_pre, mid_main)[domain][pop, at - 1],
                lambda pop, at: rim_left[forward_z.index(pop), at : at + 1, lanes],
                lambda pop, at: rim_right[backward_z.index(pop), at : at + 1, lanes],
                masks_of(masks, lanes),
                x_at,
            )
            kept = (out_pre, out_main)[domain]
            for pop in range(POPS):
                kept[pop, x_at - 2] = new[pop]
            copies.append(
                pltpu.make_async_copy(
                    kept.at[:, x_at - 2],
                    (out_pre_hbm, out_main_hbm)[domain].at[:, x_at],
                    sent.at[domain, x_at - 2],
                )
            )
            copies[-1].start()

    for x_at in range(1, rows - 1):
        first_step(x_at)
        if x_at >= 3:
            second_step(x_at - 1)

    @pl.when(on_inlet)
    def _():
        copy.wait()
        planes = []
        blocked = masks_of(masks, slice(0, coarse))
        sub = lax.broadcasted_iota(jnp.int32, (width, coarse), 0)
        for place, number in enumerate(neighbours(tile_map)):
            found = tile_at(tiles, number, range(14))
            planes.append(found[:5])
            edges = [None] * POPS
            for pops, offset, row, slot in (
                (forward_z, -1, 0, 14),
                (backward_z, 1, width - 1, 15),
            ):
                lines = tile_at(tiles, number, (slot,), offset)[0]
                for k, pop in enumerate(pops):
                    line = jnp.broadcast_to(lines[k : k + 1], (width, coarse))
                    line = shift_layers(line, velocities[pop][1])
                    keep = (sub == row) & (blocked[velocities[pop][1]] == 0)
                    edges[pop] = jnp.where(keep, line, 0.0)
            density, moment = moments_of(edges)
            for k, value in enumerate([density] + moment):
                awaited[place, k] = found[10 + k] + value
            for k, pop in enumerate(incoming):
                new = found[5 + k]
                awaited[place, 4 + k] = new if edges[pop] is None else new + edges[pop]
        fill_matrices(layer_phase, matrices)
        for place, value in enumerate(refine(planes, matrices)):
            inflow[place] = value

    for copy_out in copies:
        copy_out.wait()


def last_kernel(
    masks,
    star_pre,
    star_main,
    mid_pre,
    mid_main,
    inflow,
    x_high,
    x_low,
    cross,
    same,
    edge_same,
    edge_cross,
    e_cross,
    e_same,
    awaited,
    back,
    matrices,
    part_pre,
    part_main,
    out_pre_hbm,
    out_main_hbm,
    col_left,
    col_right,
    corner_left,
    corner_right,
    in_low,
    in_high,
    next_pre,
    next_main,
    rim_left,
    rim_right,
    out_pre,
    out_main,
    sent,
):
    rows, width, coarse = star_pre.shape[1:]
    fine = star_main.shape[3]
    pre_lanes, main_lanes = lanes_of(coarse, fine)
    is_first = lax.axis_index("stream") == 0
    is_last = lax.axis_index("stream") == lax.axis_size("stream") - 1
    parity = lax.rem(lax.axis_index("span"), 2)
    ends = (x_low, x_high, [(lanes, masks_of(masks, lanes)) for lanes in (pre_lanes, main_lanes)])

    @pl.when(parity == 0)
    def _():
        build_columns(True, col_left, corner_left, cross, edge_cross, e_cross, *ends)
        build_columns(False, col_right, corner_right, same, edge_same, e_same, *ends)

    @pl.when(parity == 1)
    def _():
        build_columns(True, col_left, corner_left, same, edge_same, e_same, *ends)
        build_columns(False, col_right, corner_right, cross, edge_cross, e_cross, *ends)

    for k in range(5):
        in_low[k] = x_low[k, :, main_lanes]
        in_high[k] = x_high[k, :, main_lanes]

    @pl.when(is_last)
    def _():
        for k in range(5):
            in_high[k] = star_main[backward_x[k], rows - 1]
        for col in (col_left, col_right):
            for k in range(KEPT + 5):
                col[k, 16:17, main_lanes] = col[k, 15:16, main_lanes]

    @pl.when(is_first)
    def _():
        before, own, after = (inflow.at[tile] for tile in range(3))
        for k in range(5):
            in_low[k] = own[k]
            col_left[incoming[k], 7:8, main_lanes] = before[k, width - 1 : width]
            col_right[incoming[k], 7:8, main_lanes] = after[k, 0:1]
        col_left[POPS + 1, 7:8, main_lanes] = before[3, width - 2 : width - 1]
        col_left[KEPT + 2, 7:8, main_lanes] = own[4, 0:1]
        col_right[POPS + 2, 7:8, main_lanes] = after[4, 1:2]
        col_right[KEPT + 1, 7:8, main_lanes] = own[3, width - 1 : width]

    for is_left, col, corner, rim in (
        (True, col_left, corner_left, rim_left),
        (False, col_right, corner_right, rim_right),
    ):
        moving = forward_z if is_left else backward_z
        for lanes in (pre_lanes, main_lanes):
            new = column_values(
                is_left,
                lambda pop, step_x=0: col[pop, 7 - step_x : 23 - step_x, lanes],
                lambda k, step_x: col[POPS + k, 7 - step_x : 23 - step_x, lanes],
                lambda k, step_x: col[KEPT + k, 7 - step_x : 23 - step_x, lanes],
                lambda read, at, step_x: read(at, step_x),
                masks_of(masks, lanes, 16),
            )
            row = lax.broadcasted_iota(jnp.int32, new[0].shape, 0)
            for pop in range(POPS):
                if pop not in backward_x:
                    new[pop] = jnp.where(row == 0, 0.0, new[pop])
                if pop not in incoming:
                    new[pop] = jnp.where(row == rows + 1, 0.0, new[pop])
            density, moment = moments_of(new)
            density = density + corner[0, :, lanes]
            moment = [moment[axis_num] + corner[1 + axis_num, :, lanes] for axis_num in range(3)]
            for at, ends_of in ((4, incoming), (5, backward_x)):
                pop = [pop for pop in moving if pop in ends_of][0]
                new[pop] = new[pop] + corner[at, :, lanes]
            out = relax(new, density, moment, moving)
            for k in range(5):
                rim[k, :, lanes] = out[moving[k]]

    stars = (star_pre, star_main)
    outer = {-1: 0, 0: 1, rows - 1: 2, rows: 3}

    def base_of(domain, lanes):
        def base(pop, x_at):
            if 0 <= x_at < rows:
                return stars[domain][pop, x_at]
            if x_at == -1:
                k = incoming.index(pop)
                return in_low[k] if domain == 1 else x_low[k, :, lanes]
            k = backward_x.index(pop)
            return in_high[k] if domain == 1 else x_high[k, :, lanes]

        return base

    def beside_tile(domain, lanes, x_at):
        star = stars[domain]
        face, moving, back = (
            (x_low, incoming, backward_x) if x_at < 0 else (x_high, backward_x, incoming)
        )
        blocked = masks_of(masks, lanes)
        left = lambda pop, at: col_left[pop, 8 + at : 9 + at, lanes]
        right = lambda pop, at: col_right[pop, 8 + at : 9 + at, lanes]

        def base(pop, at):
            return face[moving.index(pop), :, lanes] if at == x_at else star[pop, at]

        new = moved_row(base, left, right, blocked, x_at, back)
        sub = lax.broadcasted_iota(jnp.int32, new[back[0]].shape, 0)
        for pop in range(POPS):
            if pop in back:
                continue
            step_x, step_y, step_z = velocities[pop]
            if step_z != 0:
                line = (left if step_z == 1 else right)(pop, x_at - step_x)
                line = shift_layers(jnp.broadcast_to(line, sub.shape), step_y)
                keep = (sub == (0 if step_z == 1 else width - 1)) & (blocked[step_y] == 0)
                new[pop] = jnp.where(keep, line, 0.0)
            if pop in moving:
                part = face[5 + moving.index(pop), :, lanes]
                new[pop] = part if new[pop] is None else part + new[pop]
        density, moment = moments_of(new)
        density = density + face[10, :, lanes]
        moment = [moment[0], moment[1] + face[11, :, lanes], moment[2] + face[12, :, lanes]]
        return relax(new, density, moment, moving), moving

    def next_of(domain):
        def base(pop, x_at):
            if x_at in outer:
                return (next_pre, next_main)[domain][pop, outer[x_at]]
            return (mid_pre, mid_main)[domain][pop, x_at - 1]

        return base

    def end_row(x_at):
        for domain, lanes in enumerate((pre_lanes, main_lanes)):
            if 0 <= x_at < rows:
                new = moved_row(
                    base_of(domain, lanes),
                    lambda pop, at: col_left[pop, 8 + at : 9 + at, lanes],
                    lambda pop, at: col_right[pop, 8 + at : 9 + at, lanes],
                    masks_of(masks, lanes),
                    x_at,
                )
                out, wanted = collide(new), range(POPS)
            else:
                out, wanted = beside_tile(domain, lanes, x_at)
            for pop in wanted:
                (next_pre, next_main)[domain][pop, outer[x_at]] = out[pop]

    copies = []

    def second_step(at_end, x_at):
        for domain, lanes in enumerate((pre_lanes, main_lanes)):
            new = moved_row(
                next_of(domain),
                lambda pop, at: rim_left[forward_z.index(pop), at + 1 : at + 2, lanes],
                lambda pop, at: rim_right[backward_z.index(pop), at + 1 : at + 2, lanes],
                masks_of(masks, lanes),
                x_at,
            )
            kept = (out_pre, out_main)[domain]
            for pop in range(POPS):
                kept[pop, at_end] = new[pop]
            copies.append(
                pltpu.make_async_copy(
                    kept.at[:, at_end],
                    (out_pre_hbm, out_main_hbm)[domain].at[:, x_at],
                    sent.at[domain, at_end],
                )
            )
            copies[-1].start()

    end_row(rows - 1)
    second_step(2, rows - 2)
    end_row(rows)

    @pl.when(is_last)
    def _():
        for k in range(5):
            next_main[backward_x[k], 3] = next_main[backward_x[k], 2]
            for rim in (rim_left, rim_right):
                rim[k, rows + 1 : rows + 2, main_lanes] = rim[k, rows : rows + 1, main_lanes]

    second_step(3, rows - 1)
    end_row(0)
    second_step(0, 1)
    end_row(-1)

    @pl.when(is_first)
    def _():
        planes = []
        for place in range(3):
            first = 0 if place == 0 else 3
            rest = [back[k] if place == 1 else back[3, first + k : first + k + 1, :] for k in range(3)]
            density = awaited[place, 0] + rest[0]
            moment = [
                awaited[place, 1] - rest[0],
                awaited[place, 2] + rest[1],
                awaited[place, 3] + rest[2],
            ]
            new = [None] * POPS
            for k, pop in enumerate(incoming):
                new[pop] = awaited[place, 4 + k]
            out = relax(new, density, moment, incoming)
            planes.append([out[pop] for pop in incoming])
        before, own, after = refine(planes, matrices)
        for k in range(5):
            next_main[incoming[k], 0] = own[k]
        rim_left[1, 0:1, main_lanes] = before[3, width - 1 : width]
        rim_right[2, 0:1, main_lanes] = after[4, 0:1]

    second_step(1, 0)
    for copy in copies:
        copy.wait()


def f32(*shape):
    return jax.ShapeDtypeStruct(shape, jnp.float32)


def local(pre_pops, main_pops, tile_map, layer_phase, wall_flags):
    span_count = lax.axis_size("span")
    stream_count = lax.axis_size("stream")
    _, rows, width, coarse = pre_pops.shape
    fine = main_pops.shape[3]
    lanes = coarse + fine

    def send(value, step_x, place, only=range(stream_count)):
        moves = []
        for s in range(stream_count):
            if s not in only:
                continue
            for j in range(span_count):
                target = (s + step_x) % stream_count * span_count + place(j) % span_count
                moves.append((s * span_count + j, target))
        return lax.ppermute(value, ("stream", "span"), moves)

    def swap_in_pairs(value):
        moves = []
        for s in range(stream_count):
            other = min(s ^ 1, stream_count - 1)
            moves += [(s * span_count + j, other * span_count + j) for j in range(span_count)]
        return lax.ppermute(value, ("stream", "span"), moves)

    stay = lambda j: j
    sibling = lambda j: j + 1 if j % 2 == 0 else j - 1
    beyond = lambda j: j - 1 if j % 2 == 0 else j + 1
    params = pltpu.CompilerParams(vmem_limit_bytes=VMEM_SMALL)

    whole = pl.BlockSpec(memory_space=pltpu.VMEM)
    outside = pl.BlockSpec(memory_space=pltpu.HBM)
    tile_row, phase_row = (row.reshape(1, span_count) for row in (tile_map, layer_phase))

    in_hbm = lambda value: pltpu.with_memory_space_constraint(value, pltpu.HBM)
    star_pre, star_main, z_same, z_cross = pl.pallas_call(
        first_kernel,
        out_shape=(
            f32(*pre_pops.shape),
            f32(*main_pops.shape),
            f32(KEPT, rows, lanes),
            f32(KEPT, rows, lanes),
        ),
        in_specs=[outside, outside],
        scratch_shapes=[
            pltpu.VMEM(pre_pops.shape, jnp.float32),
            pltpu.VMEM(main_pops.shape, jnp.float32),
            pltpu.SemaphoreType.DMA((2, rows)),
        ],
        compiler_params=pltpu.CompilerParams(vmem_limit_bytes=VMEM_SMALL),
        name="collide_and_pack",
    )(in_hbm(pre_pops), in_hbm(main_pops))
    masks, x_hi, x_lo, plane = pl.pallas_call(
        face_kernel,
        out_shape=(
            f32(3, 8, lanes),
            f32(FACE, width, lanes),
            f32(FACE, width, lanes),
            f32(PLANE, width, coarse),
        ),
        compiler_params=params,
        name="faces",
    )(wall_flags.reshape(1, fine), star_pre, star_main)

    same = send(z_same, 0, sibling)
    cross = send(z_cross, 0, beyond)
    x_low = send(x_hi, 1, stay)
    x_high = send(x_lo, -1, stay)
    tiles = lax.all_gather(plane, "span", axis=0, tiled=False)
    anywhere = pl.BlockSpec(memory_space=pl.ANY)
    all_tiles = [
        pltpu.VMEM((span_count, PLANE, width, coarse), jnp.float32),
        pltpu.SemaphoreType.DMA,
    ]
    e_to_same, e_to_cross = pl.pallas_call(
        corner_kernel,
        out_shape=(f32(2 * SIDE, lanes), f32(2 * SIDE, lanes)),
        in_specs=[whole] * 2 + [anywhere],
        compiler_params=params,
        name="corners",
    )(x_high, x_low, tiles)
    e_same = send(e_to_same, 0, sibling)
    e_cross = send(e_to_cross, 0, beyond)
    back = pl.pallas_call(
        back_kernel,
        out_shape=f32(4, width, coarse),
        in_specs=[whole, whole, anywhere],
        scratch_shapes=all_tiles,
        compiler_params=params,
        name="behind_plane",
    )(tile_row, masks, tiles)
    back = swap_in_pairs(back)
    half_pre = pltpu.VMEM((POPS, 4, width, coarse), jnp.float32)
    half_main = pltpu.VMEM((POPS, 4, width, fine), jnp.float32)
    mid_pre, mid_main, inflow, awaited, matrices, part_pre, part_main = pl.pallas_call(
        middle_kernel,
        out_shape=(
            f32(POPS, rows - 2, width, coarse),
            f32(POPS, rows - 2, width, fine),
            f32(3, 5, width, fine),
            f32(3, 9, width, coarse),
            jax.ShapeDtypeStruct((3, coarse, fine), jnp.bfloat16),
            f32(*pre_pops.shape),
            f32(*main_pops.shape),
        ),
        in_specs=[whole] * 9 + [anywhere],
        out_specs=[whole] * 5 + [outside] * 2,
        scratch_shapes=[
            pltpu.VMEM((5, rows, lanes), jnp.float32),
            pltpu.VMEM((5, rows, lanes), jnp.float32),
            pltpu.VMEM((5, rows, lanes), jnp.float32),
            pltpu.VMEM((5, rows, lanes), jnp.float32),
            pltpu.VMEM((POPS, rows - 4, width, coarse), jnp.float32),
            pltpu.VMEM((POPS, rows - 4, width, fine), jnp.float32),
        ]
        + all_tiles
        + [pltpu.SemaphoreType.DMA((2, rows - 4))],
        compiler_params=params,
        name="middle_rows",
    )(tile_row, phase_row, masks, star_pre, star_main, cross, same, z_same, z_cross, tiles)
    return pl.pallas_call(
        last_kernel,
        out_shape=(f32(*pre_pops.shape), f32(*main_pops.shape)),
        in_specs=[whole] * 17 + [outside] * 2,
        out_specs=(outside, outside),
        input_output_aliases={17: 0, 18: 1},
        scratch_shapes=[
            pltpu.VMEM((KEPT + 5, 24, lanes), jnp.float32),
            pltpu.VMEM((KEPT + 5, 24, lanes), jnp.float32),
            pltpu.VMEM((6, 16, lanes), jnp.float32),
            pltpu.VMEM((6, 16, lanes), jnp.float32),
            pltpu.VMEM((5, width, fine), jnp.float32),
            pltpu.VMEM((5, width, fine), jnp.float32),
            half_pre,
            half_main,
            pltpu.VMEM((5, 16, lanes), jnp.float32),
            pltpu.VMEM((5, 16, lanes), jnp.float32),
            half_pre,
            half_main,
            pltpu.SemaphoreType.DMA((2, 4)),
        ],
        compiler_params=pltpu.CompilerParams(vmem_limit_bytes=VMEM_LARGE),
        name="last_rows",
    )(
        masks,
        star_pre,
        star_main,
        mid_pre,
        mid_main,
        inflow,
        x_high,
        x_low,
        cross,
        same,
        z_same,
        z_cross,
        e_cross,
        e_same,
        awaited,
        back,
        matrices,
        part_pre,
        part_main,
    )


def solution(mesh):
    return jax.shard_map(
        local,
        mesh=mesh,
        in_specs=(P(None, "stream", "span", None), P(None, "stream", "span", None), P(), P(), P()),
        out_specs=(P(None, "stream", "span", None), P(None, "stream", "span", None)),
        check_vma=False,
    )
```

```python
import jax
import jax.numpy as jnp
from jax import lax
from jax.experimental import pallas as pl
from jax.experimental.pallas import tpu as pltpu
from jax.sharding import PartitionSpec as P

velocities = (
    (0, 0, 0),
    (1, 0, 0),
    (-1, 0, 0),
    (0, 1, 0),
    (0, -1, 0),
    (0, 0, 1),
    (0, 0, -1),
    (1, 1, 0),
    (-1, -1, 0),
    (1, -1, 0),
    (-1, 1, 0),
    (1, 0, 1),
    (-1, 0, -1),
    (1, 0, -1),
    (-1, 0, 1),
    (0, 1, 1),
    (0, -1, -1),
    (0, 1, -1),
    (0, -1, 1),
)
opposite = (0, 2, 1, 4, 3, 6, 5, 8, 7, 10, 9, 12, 11, 14, 13, 16, 15, 18, 17)
pairs = tuple((k, k + 1) for k in range(1, 19, 2))
incoming = (1, 7, 9, 11, 13)
backward_x = (2, 8, 10, 12, 14)
forward_z = (5, 11, 14, 15, 18)
backward_z = (6, 12, 13, 16, 17)
POPS = 19
PLANE = 16
FACE = 14
SIDE = 16
stays_x = tuple(k for k in range(POPS) if velocities[k][0] == 0)
KEPT = POPS + 5
VMEM_SMALL = 10 * 1024 * 1024
VMEM_LARGE = 20 * 1024 * 1024


def moments_of(pops):
    density = None
    moment = [None, None, None]

    def add(total, value):
        return value if total is None else total + value

    for group, weight in ((range(1, 7), 1.0 / 18.0), (range(7, POPS), 1.0 / 36.0)):
        part = None
        parts = [None, None, None]
        for a, b in ((k, k + 1) for k in group[::2]):
            if pops[a] is None and pops[b] is None:
                continue
            if pops[b] is None:
                both, diff = pops[a], pops[a]
            elif pops[a] is None:
                both, diff = pops[b], -pops[b]
            else:
                both, diff = pops[a] + pops[b], pops[a] - pops[b]
            part = add(part, both)
            for axis_num, step in enumerate(velocities[a]):
                if step != 0:
                    parts[axis_num] = add(parts[axis_num], diff if step == 1 else -diff)
        if part is not None:
            density = add(density, part * weight)
        for axis_num in range(3):
            if parts[axis_num] is not None:
                moment[axis_num] = add(moment[axis_num], parts[axis_num] * weight)
    if pops[0] is not None:
        density = add(density, pops[0] * (1.0 / 3.0))
    return density, moment


def relax(pops, density, moment, wanted):
    inverse = 1.0 / density
    speed = [component * inverse for component in moment]
    kinetic = moment[0] * speed[0] + moment[1] * speed[1] + moment[2] * speed[2]
    base = 1.25 * density - 1.875 * kinetic
    result = [None] * POPS
    if 0 in wanted:
        result[0] = base - 0.25 * pops[0]
    for a, b in pairs:
        if a not in wanted and b not in wanted:
            continue
        flux = None
        along = None
        for axis_num, step in enumerate(velocities[a]):
            if step == 0:
                continue
            if flux is None:
                flux, along = moment[axis_num], speed[axis_num]
            elif step == 1:
                flux, along = flux + moment[axis_num], along + speed[axis_num]
            else:
                flux, along = flux - moment[axis_num], along - speed[axis_num]
        even = base + 5.625 * (flux * along)
        odd = 3.75 * flux
        if a in wanted:
            result[a] = even + odd - 0.25 * pops[a]
        if b in wanted:
            result[b] = even - odd - 0.25 * pops[b]
    return result


def collide(pops, wanted=range(POPS)):
    density, moment = moments_of(pops)
    return relax(pops, density, moment, wanted)


def shift_layers(value, step_y):
    if step_y == 0:
        return value
    size = value.shape[-1]
    return pltpu.roll(value, step_y % size, value.ndim - 1)


def moved_row(base, left, right, masks, x_at, wanted=range(POPS)):
    result = []
    sub = None
    for which_pop in range(POPS):
        if which_pop not in wanted:
            result.append(None)
            continue
        step_x, step_y, step_z = velocities[which_pop]
        source = base(which_pop, x_at - step_x)
        if step_z != 0 and sub is None:
            sub = lax.broadcasted_iota(jnp.int32, source.shape, 0)
        width = source.shape[0]
        if step_z == 1:
            source = jnp.where(
                sub == 0, left(which_pop, x_at - step_x), pltpu.roll(source, 1, 0)
            )
        elif step_z == -1:
            source = jnp.where(
                sub == width - 1,
                right(which_pop, x_at - step_x),
                pltpu.roll(source, width - 1, 0),
            )
        source = shift_layers(source, step_y)
        result.append(
            jnp.where(masks[step_y] != 0, base(opposite[which_pop], x_at), source)
        )
    return result


def fill_masks(walls, masks):
    fine = walls.shape[1]
    coarse = masks.shape[2] - fine

    def fill(solid, lanes):
        layers = solid.shape[1]
        lane = lax.broadcasted_iota(jnp.int32, solid.shape, 1)
        masks[0, :, lanes] = solid
        masks[1, :, lanes] = jnp.where(lane == 0, 1.0, pltpu.roll(solid, 1, 1))
        masks[2, :, lanes] = jnp.where(lane == layers - 1, 1.0, pltpu.roll(solid, layers - 1, 1))

    solid = jnp.broadcast_to(jnp.where(walls[...] > 0, 1.0, 0.0), (8, fine))
    fine_at = lax.broadcasted_iota(jnp.int32, (fine, coarse), 0)
    coarse_at = lax.broadcasted_iota(jnp.int32, (fine, coarse), 1)
    halves = jnp.where(lax.shift_right_logical(fine_at, 1) == coarse_at, 1.0, 0.0)
    hits = jnp.dot(solid, halves, preferred_element_type=jnp.float32)
    fill(jnp.where(hits > 0.5, 1.0, 0.0), slice(0, coarse))
    fill(solid, slice(coarse, coarse + fine))


def first_kernel(
    pre_hbm,
    main_hbm,
    star_pre,
    star_main,
    z_same,
    z_cross,
    pre,
    main,
    arrived,
):
    rows = pre.shape[1]
    coarse = pre.shape[3]
    parity = lax.rem(lax.axis_index("span"), 2)
    domains = ((pre, star_pre, slice(0, coarse)), (main, star_main, slice(coarse, None)))
    copies = [
        [
            pltpu.make_async_copy(source.at[:, x_at], target.at[:, x_at], arrived.at[at, x_at])
            for at, (source, target) in enumerate(((pre_hbm, pre), (main_hbm, main)))
        ]
        for x_at in range(rows)
    ]
    for row in copies:
        for copy in row:
            copy.start()
    for x_at in range(rows):
        for copy in copies[x_at]:
            copy.wait()
        for pops, star, lanes in domains:
            out = collide([pops[which_pop, x_at] for which_pop in range(POPS)])
            for which_pop in range(POPS):
                star[which_pop, x_at] = out[which_pop]

    def edges(hi, lo):
        for _, star, lanes in domains:
            width = star.shape[2]
            for which_pop in range(POPS):
                hi[which_pop, :, lanes] = star[which_pop, :, width - 1, :]
                lo[which_pop, :, lanes] = star[which_pop, :, 0, :]
            for k in range(5):
                hi[POPS + k, :, lanes] = star[forward_z[k], :, width - 2, :]
                lo[POPS + k, :, lanes] = star[backward_z[k], :, 1, :]

    @pl.when(parity == 0)
    def _():
        edges(z_same, z_cross)

    @pl.when(parity == 1)
    def _():
        edges(z_cross, z_same)


def edge_lines(pops, moving, rim, inner):
    return [(pop, rim) for pop in pops if pop in stays_x] + [
        (pop, inner) for pop in pops if pop in moving
    ]


def fill_face(star, lanes, blocked, at_top, face):
    last = star.shape[1] - 1
    moving = incoming if at_top else backward_x
    rim = last if at_top else 0
    none = lambda pop, x_at: 0.0
    base = lambda pop, x_at: star[pop, x_at]
    new = moved_row(base, none, none, blocked, rim, moving + stays_x)
    for k, pop in enumerate(moving):
        face[k, :, lanes] = star[pop, rim]
        face[5 + k, :, lanes] = new[pop]
        new[pop] = None
    density, moment = moments_of(new)
    face[10, :, lanes] = density
    face[11, :, lanes] = moment[1]
    face[12, :, lanes] = moment[2]
    inner = rim - 1 if at_top else rim + 1
    for first, pops, z_at in ((0, backward_z, 0), (4, forward_z, star.shape[2] - 1)):
        for k, (pop, x_at) in enumerate(edge_lines(pops, moving, rim, inner)):
            row = first + k
            face[13, row : row + 1, lanes] = star[pop, x_at, z_at : z_at + 1, :]


def face_kernel(walls, star_pre, star_main, masks, x_hi, x_lo, plane):
    coarse = star_pre.shape[3]
    fill_masks(walls, masks)
    for star, lanes in zip((star_pre, star_main), lanes_of(coarse, star_main.shape[3])):
        blocked = masks_of(masks, lanes)
        fill_face(star, lanes, blocked, True, x_hi)
        fill_face(star, lanes, blocked, False, x_lo)
    fill_plane(star_pre, masks_of(masks, slice(0, coarse)), plane)


def fill_plane(star, blocked, plane):
    width, coarse = plane.shape[1:]
    last = star.shape[1] - 1
    zero = jnp.zeros((width, coarse), jnp.float32)
    stream_pos = lax.axis_index("stream")

    @pl.when(stream_pos != 1)
    def _():
        base = lambda pop, x_at: zero if x_at > last else star[pop, x_at]
        none = lambda pop, x_at: 0.0
        new = moved_row(base, none, none, blocked, last)
        density, moment = moments_of(new)
        for k, pop in enumerate(incoming):
            plane[k] = star[pop, last]
            plane[5 + k] = new[pop]
        plane[10] = density
        for axis_num in range(3):
            plane[11 + axis_num] = moment[axis_num]
        plane[14] = zero
        plane[15] = zero
        for k in range(5):
            hi, lo = forward_z[k], backward_z[k]
            plane[14, k : k + 1, :] = base(hi, last - velocities[hi][0])[width - 1 : width]
            plane[15, k : k + 1, :] = base(lo, last - velocities[lo][0])[0:1]

    @pl.when(stream_pos == 1)
    def _():
        none = lambda pop, x_at: 0.0
        back = moved_row(
            lambda pop, x_at: star[pop, x_at] if pop in backward_x else zero,
            none,
            none,
            blocked,
            -1,
            backward_x,
        )
        density, moment = moments_of(back)
        for k, value in enumerate([density] + moment):
            plane[k] = value
        for k in range(4, PLANE):
            plane[k] = zero
        plane[14, 1:2, :] = star[14, 0, width - 1 : width, :]
        plane[15, 1:2, :] = star[12, 0, 0:1, :]


def column_values(is_left, first, second, inner, shift, blocked):
    inward, outward = (forward_z, backward_z) if is_left else (backward_z, forward_z)
    result = []
    for pop in range(POPS):
        step_x, step_y, _ = velocities[pop]
        if pop in inward:
            source = shift(second, inward.index(pop), step_x)
        elif pop in outward:
            source = shift(inner, outward.index(pop), step_x)
        else:
            source = shift(first, pop, step_x)
        result.append(
            jnp.where(blocked[step_y] != 0, first(opposite[pop]), shift_layers(source, step_y))
        )
    return result


def turned(read, at, step_x):
    value = read(at)
    return value if step_x == 0 else pltpu.roll(value, step_x % value.shape[0], 0)


def only(pops, values):
    return [values[pop] if pop in pops else None for pop in range(POPS)]


def corner_kernel(x_high, x_low, tiles, e_same, e_cross):
    def lines(is_left, target):
        inward = forward_z if is_left else backward_z
        edge, second, first = (7, 6, 4) if is_left else (0, 1, 0)
        for start, moving, face in ((0, incoming, x_low), (SIDE, backward_x, x_high)):
            turning = moving.index([pop for pop in moving if pop in inward][0])
            new = [None] * POPS
            for k, pop in enumerate(moving):
                new[pop] = face[5 + k]
            density, moment = moments_of(new)
            sums = [
                density + face[10],
                moment[0],
                moment[1] + face[11],
                moment[2] + face[12],
                face[5 + turning],
            ]
            found = [face[k, edge : edge + 1, :] for k in range(5)]
            found += [face[13, first + k : first + k + 1, :] for k in range(4)]
            found += [face[turning, second : second + 1, :]]
            found += [value[edge : edge + 1] for value in sums]
            for k, line in enumerate(found):
                target[start + k : start + k + 1, :] = line

    parity = lax.rem(lax.axis_index("span"), 2)

    @pl.when(parity == 0)
    def _():
        lines(True, e_same)
        lines(False, e_cross)

    @pl.when(parity == 1)
    def _():
        lines(False, e_same)
        lines(True, e_cross)


def back_kernel(tile_map, masks, tiles_hbm, back, tiles, arrived):
    @pl.when(lax.axis_index("stream") == 1)
    def _():
        copy = pltpu.make_async_copy(tiles_hbm, tiles, arrived)
        copy.start()
        copy.wait()
        width, coarse = tiles.shape[2:]
        sub = lax.broadcasted_iota(jnp.int32, (width, coarse), 0)
        open_layers = masks[0, :, :coarse] == 0
        for at, number in enumerate(neighbours(tile_map)):
            edges = [None] * POPS
            for pop, offset, row, slot in ((14, -1, 0, 14), (12, 1, width - 1, 15)):
                line = tile_at(tiles, number, (slot,), offset)[0][1:2]
                line = jnp.broadcast_to(line, (width, coarse))
                edges[pop] = jnp.where((sub == row) & open_layers, line, 0.0)
            density, moment = moments_of(edges)
            sums = tile_at(tiles, number, (0, 2, 3))
            for k, value in enumerate((sums[0] + density, sums[1], sums[2] + moment[2])):
                if at == 1:
                    back[k] = value
                else:
                    line, edge = (k, width - 1) if at == 0 else (3 + k, 0)
                    back[3, line : line + 1, :] = value[edge : edge + 1]


def build_columns(is_left, col, corner, halo, edge, lines, x_low, x_high, masks):
    inward, outward = (forward_z, backward_z) if is_left else (backward_z, forward_z)
    rim, first = (0, 0) if is_left else (7, 4)
    for k in range(KEPT):
        col[k, 8:16, :] = halo[k]
    for k in range(5):
        col[KEPT + k, 8:16, :] = edge[outward[k]]
    corner[...] = jnp.zeros(corner.shape, jnp.float32)
    for moving, face, start, near, beyond, row in (
        (incoming, x_low, 0, 7, 6, 0),
        (backward_x, x_high, SIDE, 16, 17, 9),
    ):
        line = lambda k: lines[start + k : start + k + 1, :]
        for k in range(5):
            col[moving[k], near : near + 1, :] = line(k)
        for k, pop in enumerate([pop for pop in inward if pop in stays_x]):
            col[pop, near : near + 1, :] = line(5 + k)
        turning = [pop for pop in moving if pop in inward][0]
        leaving = [pop for pop in moving if pop in outward][0]
        col[turning, beyond : beyond + 1, :] = line(8)
        at = POPS + inward.index(turning)
        col[at, near : near + 1, :] = line(9)
        at = KEPT + outward.index(leaving)
        col[at, near : near + 1, :] = face[moving.index(leaving), rim : rim + 1, :]
        for k in range(4):
            corner[k, row : row + 1, :] = line(10 + k)
        at = 4 if moving is incoming else 5
        corner[at, row : row + 1, :] = line(14)
        for lanes, blocked in masks:
            missing = [None] * POPS
            for k, (pop, _) in enumerate(edge_lines(outward, moving, 0, 0)):
                step_y = velocities[pop][1]
                value = face[13, first + k : first + k + 1, lanes]
                value = shift_layers(jnp.broadcast_to(value, blocked[0].shape), step_y)
                missing[pop] = jnp.where(blocked[step_y] != 0, 0.0, value)
            density, moment = moments_of(missing)
            for k, value in enumerate([density] + moment):
                corner[k, row : row + 1, lanes] += value[:1]


def entry_at(row, at):
    lane = lax.broadcasted_iota(jnp.int32, row.shape, 1)
    return jnp.sum(jnp.where(lane == at, row[...].astype(jnp.float32), 0.0), axis=1, keepdims=True)


def neighbours(row):
    count = row.shape[1]
    position = lax.axis_index("span")
    return [entry_at(row, lax.rem(position + step, count)) for step in (count - 1, 0, 1)]


def tile_at(tiles, number, slots, offset=0):
    count = tiles.shape[0]
    found = [tiles[offset % count, slot] for slot in slots]
    for tile in range(1, count):
        here = jnp.broadcast_to(number, found[0].shape) == float(tile)
        found = [
            jnp.where(here, tiles[(tile + offset) % count, slot], value)
            for slot, value in zip(slots, found)
        ]
    return found


def fill_matrices(layer_phase, matrices):
    shape = matrices.shape[1:]
    rows = lax.broadcasted_iota(jnp.int32, shape, 0)
    fine = lax.broadcasted_iota(jnp.int32, shape, 1)
    choices = []
    for phase in (0, 1):
        position = fine + phase
        lower = lax.shift_right_arithmetic(position - 1, 1)
        upper_wt = jnp.where(position % 2 == 0, 0.75, 0.25)
        low_idx = jnp.clip(lower, 0, shape[0] - 1)
        high_idx = jnp.clip(lower + 1, 0, shape[0] - 1)
        choices.append(
            jnp.where(rows == low_idx, 1.0 - upper_wt, 0.0)
            + jnp.where(rows == high_idx, upper_wt, 0.0)
        )
    for tile, phase in enumerate(neighbours(layer_phase)):
        chosen = jnp.where(jnp.broadcast_to(phase, shape) > 0.5, choices[1], choices[0])
        matrices[tile] = chosen.astype(jnp.bfloat16)


def refine(planes, matrices):
    refined = []
    for tile, group in enumerate(planes):
        parts = []
        rest = jnp.concatenate(group, axis=0)
        for _ in range(3):
            parts.append(rest.astype(jnp.bfloat16))
            rest = rest - parts[-1].astype(jnp.float32)
        total = None
        for part in reversed(parts):
            product = jnp.dot(part, matrices[tile], preferred_element_type=jnp.float32)
            total = product if total is None else total + product
        refined.append(total.reshape(len(group), group[0].shape[0], total.shape[1]))
    return refined


def lanes_of(coarse, fine):
    return slice(0, coarse), slice(coarse, coarse + fine)


def masks_of(masks, lanes, height=8):
    values = {step: masks[step % 3, :, lanes] for step in (0, 1, -1)}
    if height == 8:
        return values
    return {
        step: jnp.broadcast_to(value[:1], (height, value.shape[1]))
        for step, value in values.items()
    }


def middle_kernel(
    tile_map,
    layer_phase,
    masks,
    star_pre,
    star_main,
    cross,
    same,
    edge_same,
    edge_cross,
    tiles_hbm,
    mid_pre,
    mid_main,
    inflow,
    awaited,
    matrices,
    out_pre_hbm,
    out_main_hbm,
    ghost_left,
    ghost_right,
    rim_left,
    rim_right,
    out_pre,
    out_main,
    tiles,
    arrived,
    sent,
):
    rows, width, coarse = star_pre.shape[1:]
    fine = star_main.shape[3]
    parity = lax.rem(lax.axis_index("span"), 2)

    on_inlet = lax.axis_index("stream") == 0
    copy = pltpu.make_async_copy(tiles_hbm, tiles, arrived)

    @pl.when(on_inlet)
    def _():
        copy.start()

    def ghosts(is_left, ghost, halo, edge, rim):
        inward, outward = (forward_z, backward_z) if is_left else (backward_z, forward_z)
        for k in range(5):
            ghost[k] = halo[inward[k]]
        for lanes in lanes_of(coarse, fine):
            new = column_values(
                is_left,
                lambda pop: halo[pop, :, lanes],
                lambda k: halo[POPS + k, :, lanes],
                lambda k: edge[outward[k], :, lanes],
                turned,
                masks_of(masks, lanes),
            )
            out = collide(new, inward)
            for k in range(5):
                rim[k, :, lanes] = out[inward[k]]

    @pl.when(parity == 0)
    def _():
        ghosts(True, ghost_left, cross, edge_cross, rim_left)
        ghosts(False, ghost_right, same, edge_same, rim_right)

    @pl.when(parity == 1)
    def _():
        ghosts(True, ghost_left, same, edge_same, rim_left)
        ghosts(False, ghost_right, cross, edge_cross, rim_right)

    stars = (star_pre, star_main)

    def first_step(x_at):
        for domain, lanes in enumerate(lanes_of(coarse, fine)):
            new = moved_row(
                lambda pop, at: stars[domain][pop, at],
                lambda pop, at: ghost_left[forward_z.index(pop), at : at + 1, lanes],
                lambda pop, at: ghost_right[backward_z.index(pop), at : at + 1, lanes],
                masks_of(masks, lanes),
                x_at,
            )
            out = collide(new)
            for pop in range(POPS):
                (mid_pre, mid_main)[domain][pop, x_at - 1] = out[pop]

    copies = []

    def second_step(x_at):
        for domain, lanes in enumerate(lanes_of(coarse, fine)):
            new = moved_row(
                lambda pop, at: (mid_pre, mid_main)[domain][pop, at - 1],
                lambda pop, at: rim_left[forward_z.index(pop), at : at + 1, lanes],
                lambda pop, at: rim_right[backward_z.index(pop), at : at + 1, lanes],
                masks_of(masks, lanes),
                x_at,
            )
            kept = (out_pre, out_main)[domain]
            for pop in range(POPS):
                kept[pop, x_at - 2] = new[pop]
            if x_at % 2 == 1:
                copies.append(
                    pltpu.make_async_copy(
                        kept.at[:, x_at - 3 : x_at - 1],
                        (out_pre_hbm, out_main_hbm)[domain].at[:, x_at - 1 : x_at + 1],
                        sent.at[domain, x_at - 2],
                    )
                )
                copies[-1].start()

    for x_at in range(1, rows - 1):
        first_step(x_at)
        if x_at >= 3:
            second_step(x_at - 1)

    @pl.when(on_inlet)
    def _():
        copy.wait()
        planes = []
        blocked = masks_of(masks, slice(0, coarse))
        sub = lax.broadcasted_iota(jnp.int32, (width, coarse), 0)
        for place, number in enumerate(neighbours(tile_map)):
            found = tile_at(tiles, number, range(14))
            planes.append(found[:5])
            edges = [None] * POPS
            for pops, offset, row, slot in (
                (forward_z, -1, 0, 14),
                (backward_z, 1, width - 1, 15),
            ):
                lines = tile_at(tiles, number, (slot,), offset)[0]
                for k, pop in enumerate(pops):
                    line = jnp.broadcast_to(lines[k : k + 1], (width, coarse))
                    line = shift_layers(line, velocities[pop][1])
                    keep = (sub == row) & (blocked[velocities[pop][1]] == 0)
                    edges[pop] = jnp.where(keep, line, 0.0)
            density, moment = moments_of(edges)
            for k, value in enumerate([density] + moment):
                awaited[place, k] = found[10 + k] + value
            for k, pop in enumerate(incoming):
                new = found[5 + k]
                awaited[place, 4 + k] = new if edges[pop] is None else new + edges[pop]
        fill_matrices(layer_phase, matrices)
        for place, value in enumerate(refine(planes, matrices)):
            inflow[place] = value

    for copy_out in copies:
        copy_out.wait()


def last_kernel(
    masks,
    star_pre,
    star_main,
    mid_pre,
    mid_main,
    inflow,
    x_high,
    x_low,
    cross,
    same,
    edge_same,
    edge_cross,
    e_cross,
    e_same,
    awaited,
    back,
    matrices,
    part_pre,
    part_main,
    out_pre_hbm,
    out_main_hbm,
    col_left,
    col_right,
    corner_left,
    corner_right,
    in_low,
    in_high,
    next_pre,
    next_main,
    rim_left,
    rim_right,
    out_pre,
    out_main,
    sent,
):
    rows, width, coarse = star_pre.shape[1:]
    fine = star_main.shape[3]
    pre_lanes, main_lanes = lanes_of(coarse, fine)
    is_first = lax.axis_index("stream") == 0
    is_last = lax.axis_index("stream") == lax.axis_size("stream") - 1
    parity = lax.rem(lax.axis_index("span"), 2)
    ends = (x_low, x_high, [(lanes, masks_of(masks, lanes)) for lanes in (pre_lanes, main_lanes)])

    @pl.when(parity == 0)
    def _():
        build_columns(True, col_left, corner_left, cross, edge_cross, e_cross, *ends)
        build_columns(False, col_right, corner_right, same, edge_same, e_same, *ends)

    @pl.when(parity == 1)
    def _():
        build_columns(True, col_left, corner_left, same, edge_same, e_same, *ends)
        build_columns(False, col_right, corner_right, cross, edge_cross, e_cross, *ends)

    for k in range(5):
        in_low[k] = x_low[k, :, main_lanes]
        in_high[k] = x_high[k, :, main_lanes]

    @pl.when(is_last)
    def _():
        for k in range(5):
            in_high[k] = star_main[backward_x[k], rows - 1]
        for col in (col_left, col_right):
            for k in range(KEPT + 5):
                col[k, 16:17, main_lanes] = col[k, 15:16, main_lanes]

    @pl.when(is_first)
    def _():
        before, own, after = (inflow.at[tile] for tile in range(3))
        for k in range(5):
            in_low[k] = own[k]
            col_left[incoming[k], 7:8, main_lanes] = before[k, width - 1 : width]
            col_right[incoming[k], 7:8, main_lanes] = after[k, 0:1]
        col_left[POPS + 1, 7:8, main_lanes] = before[3, width - 2 : width - 1]
        col_left[KEPT + 2, 7:8, main_lanes] = own[4, 0:1]
        col_right[POPS + 2, 7:8, main_lanes] = after[4, 1:2]
        col_right[KEPT + 1, 7:8, main_lanes] = own[3, width - 1 : width]

    for is_left, col, corner, rim in (
        (True, col_left, corner_left, rim_left),
        (False, col_right, corner_right, rim_right),
    ):
        moving = forward_z if is_left else backward_z
        for lanes in (pre_lanes, main_lanes):
            new = column_values(
                is_left,
                lambda pop, step_x=0: col[pop, 7 - step_x : 23 - step_x, lanes],
                lambda k, step_x: col[POPS + k, 7 - step_x : 23 - step_x, lanes],
                lambda k, step_x: col[KEPT + k, 7 - step_x : 23 - step_x, lanes],
                lambda read, at, step_x: read(at, step_x),
                masks_of(masks, lanes, 16),
            )
            row = lax.broadcasted_iota(jnp.int32, new[0].shape, 0)
            for pop in range(POPS):
                if pop not in backward_x:
                    new[pop] = jnp.where(row == 0, 0.0, new[pop])
                if pop not in incoming:
                    new[pop] = jnp.where(row == rows + 1, 0.0, new[pop])
            density, moment = moments_of(new)
            density = density + corner[0, :, lanes]
            moment = [moment[axis_num] + corner[1 + axis_num, :, lanes] for axis_num in range(3)]
            for at, ends_of in ((4, incoming), (5, backward_x)):
                pop = [pop for pop in moving if pop in ends_of][0]
                new[pop] = new[pop] + corner[at, :, lanes]
            out = relax(new, density, moment, moving)
            for k in range(5):
                rim[k, :, lanes] = out[moving[k]]

    stars = (star_pre, star_main)
    outer = {-1: 0, 0: 1, rows - 1: 2, rows: 3}

    def base_of(domain, lanes):
        def base(pop, x_at):
            if 0 <= x_at < rows:
                return stars[domain][pop, x_at]
            if x_at == -1:
                k = incoming.index(pop)
                return in_low[k] if domain == 1 else x_low[k, :, lanes]
            k = backward_x.index(pop)
            return in_high[k] if domain == 1 else x_high[k, :, lanes]

        return base

    def beside_tile(domain, lanes, x_at):
        star = stars[domain]
        face, moving, back = (
            (x_low, incoming, backward_x) if x_at < 0 else (x_high, backward_x, incoming)
        )
        blocked = masks_of(masks, lanes)
        left = lambda pop, at: col_left[pop, 8 + at : 9 + at, lanes]
        right = lambda pop, at: col_right[pop, 8 + at : 9 + at, lanes]

        def base(pop, at):
            return face[moving.index(pop), :, lanes] if at == x_at else star[pop, at]

        new = moved_row(base, left, right, blocked, x_at, back)
        sub = lax.broadcasted_iota(jnp.int32, new[back[0]].shape, 0)
        for pop in range(POPS):
            if pop in back:
                continue
            step_x, step_y, step_z = velocities[pop]
            if step_z != 0:
                line = (left if step_z == 1 else right)(pop, x_at - step_x)
                line = shift_layers(jnp.broadcast_to(line, sub.shape), step_y)
                keep = (sub == (0 if step_z == 1 else width - 1)) & (blocked[step_y] == 0)
                new[pop] = jnp.where(keep, line, 0.0)
            if pop in moving:
                part = face[5 + moving.index(pop), :, lanes]
                new[pop] = part if new[pop] is None else part + new[pop]
        density, moment = moments_of(new)
        density = density + face[10, :, lanes]
        moment = [moment[0], moment[1] + face[11, :, lanes], moment[2] + face[12, :, lanes]]
        return relax(new, density, moment, moving), moving

    def next_of(domain):
        def base(pop, x_at):
            if x_at in outer:
                return (next_pre, next_main)[domain][pop, outer[x_at]]
            return (mid_pre, mid_main)[domain][pop, x_at - 1]

        return base

    def end_row(x_at):
        for domain, lanes in enumerate((pre_lanes, main_lanes)):
            if 0 <= x_at < rows:
                new = moved_row(
                    base_of(domain, lanes),
                    lambda pop, at: col_left[pop, 8 + at : 9 + at, lanes],
                    lambda pop, at: col_right[pop, 8 + at : 9 + at, lanes],
                    masks_of(masks, lanes),
                    x_at,
                )
                out, wanted = collide(new), range(POPS)
            else:
                out, wanted = beside_tile(domain, lanes, x_at)
            for pop in wanted:
                (next_pre, next_main)[domain][pop, outer[x_at]] = out[pop]

    copies = []

    def second_step(at_end, x_at):
        for domain, lanes in enumerate((pre_lanes, main_lanes)):
            new = moved_row(
                next_of(domain),
                lambda pop, at: rim_left[forward_z.index(pop), at + 1 : at + 2, lanes],
                lambda pop, at: rim_right[backward_z.index(pop), at + 1 : at + 2, lanes],
                masks_of(masks, lanes),
                x_at,
            )
            kept = (out_pre, out_main)[domain]
            for pop in range(POPS):
                kept[pop, at_end] = new[pop]
            if at_end % 2 == 1:
                first = x_at - x_at % 2
                copies.append(
                    pltpu.make_async_copy(
                        kept.at[:, at_end - 1 : at_end + 1],
                        (out_pre_hbm, out_main_hbm)[domain].at[:, first : first + 2],
                        sent.at[domain, at_end],
                    )
                )
                copies[-1].start()

    end_row(rows - 1)
    second_step(2, rows - 2)
    end_row(rows)

    @pl.when(is_last)
    def _():
        for k in range(5):
            next_main[backward_x[k], 3] = next_main[backward_x[k], 2]
            for rim in (rim_left, rim_right):
                rim[k, rows + 1 : rows + 2, main_lanes] = rim[k, rows : rows + 1, main_lanes]

    second_step(3, rows - 1)
    end_row(0)
    end_row(-1)

    @pl.when(is_first)
    def _():
        planes = []
        for place in range(3):
            first = 0 if place == 0 else 3
            rest = [back[k] if place == 1 else back[3, first + k : first + k + 1, :] for k in range(3)]
            density = awaited[place, 0] + rest[0]
            moment = [
                awaited[place, 1] - rest[0],
                awaited[place, 2] + rest[1],
                awaited[place, 3] + rest[2],
            ]
            new = [None] * POPS
            for k, pop in enumerate(incoming):
                new[pop] = awaited[place, 4 + k]
            out = relax(new, density, moment, incoming)
            planes.append([out[pop] for pop in incoming])
        before, own, after = refine(planes, matrices)
        for k in range(5):
            next_main[incoming[k], 0] = own[k]
        rim_left[1, 0:1, main_lanes] = before[3, width - 1 : width]
        rim_right[2, 0:1, main_lanes] = after[4, 0:1]

    second_step(0, 0)
    second_step(1, 1)
    for copy in copies:
        copy.wait()


def f32(*shape):
    return jax.ShapeDtypeStruct(shape, jnp.float32)


def local(pre_pops, main_pops, tile_map, layer_phase, wall_flags):
    span_count = lax.axis_size("span")
    stream_count = lax.axis_size("stream")
    _, rows, width, coarse = pre_pops.shape
    fine = main_pops.shape[3]
    lanes = coarse + fine

    def send(value, step_x, place, only=range(stream_count)):
        moves = []
        for s in range(stream_count):
            if s not in only:
                continue
            for j in range(span_count):
                target = (s + step_x) % stream_count * span_count + place(j) % span_count
                moves.append((s * span_count + j, target))
        return lax.ppermute(value, ("stream", "span"), moves)

    def swap_in_pairs(value):
        moves = []
        for s in range(stream_count):
            other = min(s ^ 1, stream_count - 1)
            moves += [(s * span_count + j, other * span_count + j) for j in range(span_count)]
        return lax.ppermute(value, ("stream", "span"), moves)

    stay = lambda j: j
    sibling = lambda j: j + 1 if j % 2 == 0 else j - 1
    beyond = lambda j: j - 1 if j % 2 == 0 else j + 1
    params = pltpu.CompilerParams(vmem_limit_bytes=VMEM_SMALL)

    whole = pl.BlockSpec(memory_space=pltpu.VMEM)
    outside = pl.BlockSpec(memory_space=pltpu.HBM)
    tile_row, phase_row = (row.reshape(1, span_count) for row in (tile_map, layer_phase))

    in_hbm = lambda value: pltpu.with_memory_space_constraint(value, pltpu.HBM)
    star_pre, star_main, z_same, z_cross = pl.pallas_call(
        first_kernel,
        out_shape=(
            f32(*pre_pops.shape),
            f32(*main_pops.shape),
            f32(KEPT, rows, lanes),
            f32(KEPT, rows, lanes),
        ),
        in_specs=[outside, outside],
        scratch_shapes=[
            pltpu.VMEM(pre_pops.shape, jnp.float32),
            pltpu.VMEM(main_pops.shape, jnp.float32),
            pltpu.SemaphoreType.DMA((2, rows)),
        ],
        compiler_params=pltpu.CompilerParams(vmem_limit_bytes=VMEM_SMALL),
        name="collide_and_pack",
    )(in_hbm(pre_pops), in_hbm(main_pops))
    masks, x_hi, x_lo, plane = pl.pallas_call(
        face_kernel,
        out_shape=(
            f32(3, 8, lanes),
            f32(FACE, width, lanes),
            f32(FACE, width, lanes),
            f32(PLANE, width, coarse),
        ),
        compiler_params=params,
        name="faces",
    )(wall_flags.reshape(1, fine), star_pre, star_main)

    same = send(z_same, 0, sibling)
    cross = send(z_cross, 0, beyond)
    x_low = send(x_hi, 1, stay)
    x_high = send(x_lo, -1, stay)
    tiles = lax.all_gather(plane, "span", axis=0, tiled=False)
    anywhere = pl.BlockSpec(memory_space=pl.ANY)
    all_tiles = [
        pltpu.VMEM((span_count, PLANE, width, coarse), jnp.float32),
        pltpu.SemaphoreType.DMA,
    ]
    e_to_same, e_to_cross = pl.pallas_call(
        corner_kernel,
        out_shape=(f32(2 * SIDE, lanes), f32(2 * SIDE, lanes)),
        in_specs=[whole] * 2 + [anywhere],
        compiler_params=params,
        name="corners",
    )(x_high, x_low, tiles)
    e_same = send(e_to_same, 0, sibling)
    e_cross = send(e_to_cross, 0, beyond)
    back = pl.pallas_call(
        back_kernel,
        out_shape=f32(4, width, coarse),
        in_specs=[whole, whole, anywhere],
        scratch_shapes=all_tiles,
        compiler_params=params,
        name="behind_plane",
    )(tile_row, masks, tiles)
    back = swap_in_pairs(back)
    half_pre = pltpu.VMEM((POPS, 4, width, coarse), jnp.float32)
    half_main = pltpu.VMEM((POPS, 4, width, fine), jnp.float32)
    mid_pre, mid_main, inflow, awaited, matrices, part_pre, part_main = pl.pallas_call(
        middle_kernel,
        out_shape=(
            f32(POPS, rows - 2, width, coarse),
            f32(POPS, rows - 2, width, fine),
            f32(3, 5, width, fine),
            f32(3, 9, width, coarse),
            jax.ShapeDtypeStruct((3, coarse, fine), jnp.bfloat16),
            f32(*pre_pops.shape),
            f32(*main_pops.shape),
        ),
        in_specs=[whole] * 9 + [anywhere],
        out_specs=[whole] * 5 + [outside] * 2,
        scratch_shapes=[
            pltpu.VMEM((5, rows, lanes), jnp.float32),
            pltpu.VMEM((5, rows, lanes), jnp.float32),
            pltpu.VMEM((5, rows, lanes), jnp.float32),
            pltpu.VMEM((5, rows, lanes), jnp.float32),
            pltpu.VMEM((POPS, rows - 4, width, coarse), jnp.float32),
            pltpu.VMEM((POPS, rows - 4, width, fine), jnp.float32),
        ]
        + all_tiles
        + [pltpu.SemaphoreType.DMA((2, rows - 4))],
        compiler_params=params,
        name="middle_rows",
    )(tile_row, phase_row, masks, star_pre, star_main, cross, same, z_same, z_cross, tiles)
    return pl.pallas_call(
        last_kernel,
        out_shape=(f32(*pre_pops.shape), f32(*main_pops.shape)),
        in_specs=[whole] * 17 + [outside] * 2,
        out_specs=(outside, outside),
        input_output_aliases={17: 0, 18: 1},
        scratch_shapes=[
            pltpu.VMEM((KEPT + 5, 24, lanes), jnp.float32),
            pltpu.VMEM((KEPT + 5, 24, lanes), jnp.float32),
            pltpu.VMEM((6, 16, lanes), jnp.float32),
            pltpu.VMEM((6, 16, lanes), jnp.float32),
            pltpu.VMEM((5, width, fine), jnp.float32),
            pltpu.VMEM((5, width, fine), jnp.float32),
            half_pre,
            half_main,
            pltpu.VMEM((5, 16, lanes), jnp.float32),
            pltpu.VMEM((5, 16, lanes), jnp.float32),
            half_pre,
            half_main,
            pltpu.SemaphoreType.DMA((2, 4)),
        ],
        compiler_params=pltpu.CompilerParams(vmem_limit_bytes=VMEM_LARGE),
        name="last_rows",
    )(
        masks,
        star_pre,
        star_main,
        mid_pre,
        mid_main,
        inflow,
        x_high,
        x_low,
        cross,
        same,
        z_same,
        z_cross,
        e_cross,
        e_same,
        awaited,
        back,
        matrices,
        part_pre,
        part_main,
    )


def solution(mesh):
    return jax.shard_map(
        local,
        mesh=mesh,
        in_specs=(P(None, "stream", "span", None), P(None, "stream", "span", None), P(), P(), P()),
        out_specs=(P(None, "stream", "span", None), P(None, "stream", "span", None)),
        check_vma=False,
    )
```

```python
import jax
import jax.numpy as jnp
from jax import lax
from jax.experimental import pallas as pl
from jax.experimental.pallas import tpu as pltpu
from jax.sharding import PartitionSpec as P

velocities = (
    (0, 0, 0),
    (1, 0, 0),
    (-1, 0, 0),
    (0, 1, 0),
    (0, -1, 0),
    (0, 0, 1),
    (0, 0, -1),
    (1, 1, 0),
    (-1, -1, 0),
    (1, -1, 0),
    (-1, 1, 0),
    (1, 0, 1),
    (-1, 0, -1),
    (1, 0, -1),
    (-1, 0, 1),
    (0, 1, 1),
    (0, -1, -1),
    (0, 1, -1),
    (0, -1, 1),
)
opposite = (0, 2, 1, 4, 3, 6, 5, 8, 7, 10, 9, 12, 11, 14, 13, 16, 15, 18, 17)
pairs = tuple((k, k + 1) for k in range(1, 19, 2))
incoming = (1, 7, 9, 11, 13)
backward_x = (2, 8, 10, 12, 14)
forward_z = (5, 11, 14, 15, 18)
backward_z = (6, 12, 13, 16, 17)
POPS = 19
PLANE = 16
FACE = 14
SIDE = 16
stays_x = tuple(k for k in range(POPS) if velocities[k][0] == 0)
KEPT = POPS + 5
VMEM_SMALL = 10 * 1024 * 1024
VMEM_LARGE = 20 * 1024 * 1024


def moments_of(pops):
    density = None
    moment = [None, None, None]

    def add(total, value):
        return value if total is None else total + value

    for group, weight in ((range(1, 7), 1.0 / 18.0), (range(7, POPS), 1.0 / 36.0)):
        part = None
        parts = [None, None, None]
        for a, b in ((k, k + 1) for k in group[::2]):
            if pops[a] is None and pops[b] is None:
                continue
            if pops[b] is None:
                both, diff = pops[a], pops[a]
            elif pops[a] is None:
                both, diff = pops[b], -pops[b]
            else:
                both, diff = pops[a] + pops[b], pops[a] - pops[b]
            part = add(part, both)
            for axis_num, step in enumerate(velocities[a]):
                if step != 0:
                    parts[axis_num] = add(parts[axis_num], diff if step == 1 else -diff)
        if part is not None:
            density = add(density, part * weight)
        for axis_num in range(3):
            if parts[axis_num] is not None:
                moment[axis_num] = add(moment[axis_num], parts[axis_num] * weight)
    if pops[0] is not None:
        density = add(density, pops[0] * (1.0 / 3.0))
    return density, moment


def relax(pops, density, moment, wanted):
    inverse = 1.0 / density
    speed = [component * inverse for component in moment]
    kinetic = moment[0] * speed[0] + moment[1] * speed[1] + moment[2] * speed[2]
    base = 1.25 * density - 1.875 * kinetic
    result = [None] * POPS
    if 0 in wanted:
        result[0] = base - 0.25 * pops[0]
    for a, b in pairs:
        if a not in wanted and b not in wanted:
            continue
        flux = None
        along = None
        for axis_num, step in enumerate(velocities[a]):
            if step == 0:
                continue
            if flux is None:
                flux, along = moment[axis_num], speed[axis_num]
            elif step == 1:
                flux, along = flux + moment[axis_num], along + speed[axis_num]
            else:
                flux, along = flux - moment[axis_num], along - speed[axis_num]
        even = base + 5.625 * (flux * along)
        odd = 3.75 * flux
        if a in wanted:
            result[a] = even + odd - 0.25 * pops[a]
        if b in wanted:
            result[b] = even - odd - 0.25 * pops[b]
    return result


def collide(pops, wanted=range(POPS)):
    density, moment = moments_of(pops)
    return relax(pops, density, moment, wanted)


def shift_layers(value, step_y):
    if step_y == 0:
        return value
    size = value.shape[-1]
    return pltpu.roll(value, step_y % size, value.ndim - 1)


def moved_row(base, left, right, masks, x_at, wanted=range(POPS)):
    result = []
    sub = None
    for which_pop in range(POPS):
        if which_pop not in wanted:
            result.append(None)
            continue
        step_x, step_y, step_z = velocities[which_pop]
        source = base(which_pop, x_at - step_x)
        if step_z != 0 and sub is None:
            sub = lax.broadcasted_iota(jnp.int32, source.shape, 0)
        width = source.shape[0]
        if step_z == 1:
            source = jnp.where(
                sub == 0, left(which_pop, x_at - step_x), pltpu.roll(source, 1, 0)
            )
        elif step_z == -1:
            source = jnp.where(
                sub == width - 1,
                right(which_pop, x_at - step_x),
                pltpu.roll(source, width - 1, 0),
            )
        source = shift_layers(source, step_y)
        result.append(
            jnp.where(masks[step_y] != 0, base(opposite[which_pop], x_at), source)
        )
    return result


def fill_masks(walls, masks):
    fine = walls.shape[1]
    coarse = masks.shape[2] - fine

    def fill(solid, lanes):
        layers = solid.shape[1]
        lane = lax.broadcasted_iota(jnp.int32, solid.shape, 1)
        masks[0, :, lanes] = solid
        masks[1, :, lanes] = jnp.where(lane == 0, 1.0, pltpu.roll(solid, 1, 1))
        masks[2, :, lanes] = jnp.where(lane == layers - 1, 1.0, pltpu.roll(solid, layers - 1, 1))

    solid = jnp.broadcast_to(jnp.where(walls[...] > 0, 1.0, 0.0), (8, fine))
    fine_at = lax.broadcasted_iota(jnp.int32, (fine, coarse), 0)
    coarse_at = lax.broadcasted_iota(jnp.int32, (fine, coarse), 1)
    halves = jnp.where(lax.shift_right_logical(fine_at, 1) == coarse_at, 1.0, 0.0)
    hits = jnp.dot(solid, halves, preferred_element_type=jnp.float32)
    fill(jnp.where(hits > 0.5, 1.0, 0.0), slice(0, coarse))
    fill(solid, slice(coarse, coarse + fine))


def first_kernel(
    walls_hbm,
    pre_hbm,
    main_hbm,
    star_pre,
    star_main,
    z_same,
    z_cross,
    masks,
    pre,
    main,
    walls,
    arrived,
    walls_arrived,
):
    rows = pre.shape[1]
    coarse = pre.shape[3]
    parity = lax.rem(lax.axis_index("span"), 2)
    domains = ((pre, star_pre, slice(0, coarse)), (main, star_main, slice(coarse, None)))
    copies = [
        [
            pltpu.make_async_copy(source.at[:, x_at], target.at[:, x_at], arrived.at[at, x_at])
            for at, (source, target) in enumerate(((pre_hbm, pre), (main_hbm, main)))
        ]
        for x_at in range(rows)
    ]
    copy_walls = pltpu.make_async_copy(walls_hbm, walls.at[0], walls_arrived)
    copy_walls.start()
    for row in copies:
        for copy in row:
            copy.start()
    copy_walls.wait()
    fill_masks(walls, masks)
    for x_at in range(rows):
        for copy in copies[x_at]:
            copy.wait()
        for pops, star, lanes in domains:
            out = collide([pops[which_pop, x_at] for which_pop in range(POPS)])
            for which_pop in range(POPS):
                star[which_pop, x_at] = out[which_pop]

    def edges(hi, lo):
        for _, star, lanes in domains:
            width = star.shape[2]
            for which_pop in range(POPS):
                hi[which_pop, :, lanes] = star[which_pop, :, width - 1, :]
                lo[which_pop, :, lanes] = star[which_pop, :, 0, :]
            for k in range(5):
                hi[POPS + k, :, lanes] = star[forward_z[k], :, width - 2, :]
                lo[POPS + k, :, lanes] = star[backward_z[k], :, 1, :]

    @pl.when(parity == 0)
    def _():
        edges(z_same, z_cross)

    @pl.when(parity == 1)
    def _():
        edges(z_cross, z_same)


def edge_lines(pops, moving, rim, inner):
    return [(pop, rim) for pop in pops if pop in stays_x] + [
        (pop, inner) for pop in pops if pop in moving
    ]


def fill_face(star, lanes, blocked, at_top, face):
    last = star.shape[1] - 1
    moving = incoming if at_top else backward_x
    rim = last if at_top else 0
    none = lambda pop, x_at: 0.0
    base = lambda pop, x_at: star[pop, x_at]
    new = moved_row(base, none, none, blocked, rim, moving + stays_x)
    for k, pop in enumerate(moving):
        face[k, :, lanes] = star[pop, rim]
        face[5 + k, :, lanes] = new[pop]
        new[pop] = None
    density, moment = moments_of(new)
    face[10, :, lanes] = density
    face[11, :, lanes] = moment[1]
    face[12, :, lanes] = moment[2]
    inner = rim - 1 if at_top else rim + 1
    for first, pops, z_at in ((0, backward_z, 0), (4, forward_z, star.shape[2] - 1)):
        for k, (pop, x_at) in enumerate(edge_lines(pops, moving, rim, inner)):
            row = first + k
            face[13, row : row + 1, lanes] = star[pop, x_at, z_at : z_at + 1, :]


def face_kernel(masks, star_pre, star_main, x_hi, x_lo, plane):
    coarse = star_pre.shape[3]
    for star, lanes in zip((star_pre, star_main), lanes_of(coarse, star_main.shape[3])):
        blocked = masks_of(masks, lanes)
        fill_face(star, lanes, blocked, True, x_hi)
        fill_face(star, lanes, blocked, False, x_lo)
    fill_plane(star_pre, masks_of(masks, slice(0, coarse)), plane)


def fill_plane(star, blocked, plane):
    width, coarse = plane.shape[1:]
    last = star.shape[1] - 1
    zero = jnp.zeros((width, coarse), jnp.float32)
    stream_pos = lax.axis_index("stream")

    @pl.when(stream_pos != 1)
    def _():
        base = lambda pop, x_at: zero if x_at > last else star[pop, x_at]
        none = lambda pop, x_at: 0.0
        new = moved_row(base, none, none, blocked, last)
        density, moment = moments_of(new)
        for k, pop in enumerate(incoming):
            plane[k] = star[pop, last]
            plane[5 + k] = new[pop]
        plane[10] = density
        for axis_num in range(3):
            plane[11 + axis_num] = moment[axis_num]
        plane[14] = zero
        plane[15] = zero
        for k in range(5):
            hi, lo = forward_z[k], backward_z[k]
            plane[14, k : k + 1, :] = base(hi, last - velocities[hi][0])[width - 1 : width]
            plane[15, k : k + 1, :] = base(lo, last - velocities[lo][0])[0:1]

    @pl.when(stream_pos == 1)
    def _():
        none = lambda pop, x_at: 0.0
        back = moved_row(
            lambda pop, x_at: star[pop, x_at] if pop in backward_x else zero,
            none,
            none,
            blocked,
            -1,
            backward_x,
        )
        density, moment = moments_of(back)
        for k, value in enumerate([density] + moment):
            plane[k] = value
        for k in range(4, PLANE):
            plane[k] = zero
        plane[14, 1:2, :] = star[14, 0, width - 1 : width, :]
        plane[15, 1:2, :] = star[12, 0, 0:1, :]


def column_values(is_left, first, second, inner, shift, blocked):
    inward, outward = (forward_z, backward_z) if is_left else (backward_z, forward_z)
    result = []
    for pop in range(POPS):
        step_x, step_y, _ = velocities[pop]
        if pop in inward:
            source = shift(second, inward.index(pop), step_x)
        elif pop in outward:
            source = shift(inner, outward.index(pop), step_x)
        else:
            source = shift(first, pop, step_x)
        result.append(
            jnp.where(blocked[step_y] != 0, first(opposite[pop]), shift_layers(source, step_y))
        )
    return result


def turned(read, at, step_x):
    value = read(at)
    return value if step_x == 0 else pltpu.roll(value, step_x % value.shape[0], 0)


def only(pops, values):
    return [values[pop] if pop in pops else None for pop in range(POPS)]


def corner_kernel(x_high, x_low, tiles, e_same, e_cross):
    def lines(is_left, target):
        inward = forward_z if is_left else backward_z
        edge, second, first = (7, 6, 4) if is_left else (0, 1, 0)
        for start, moving, face in ((0, incoming, x_low), (SIDE, backward_x, x_high)):
            turning = moving.index([pop for pop in moving if pop in inward][0])
            new = [None] * POPS
            for k, pop in enumerate(moving):
                new[pop] = face[5 + k]
            density, moment = moments_of(new)
            sums = [
                density + face[10],
                moment[0],
                moment[1] + face[11],
                moment[2] + face[12],
                face[5 + turning],
            ]
            found = [face[k, edge : edge + 1, :] for k in range(5)]
            found += [face[13, first + k : first + k + 1, :] for k in range(4)]
            found += [face[turning, second : second + 1, :]]
            found += [value[edge : edge + 1] for value in sums]
            for k, line in enumerate(found):
                target[start + k : start + k + 1, :] = line

    parity = lax.rem(lax.axis_index("span"), 2)

    @pl.when(parity == 0)
    def _():
        lines(True, e_same)
        lines(False, e_cross)

    @pl.when(parity == 1)
    def _():
        lines(False, e_same)
        lines(True, e_cross)


def back_kernel(tile_map, masks, tiles_hbm, back, tiles, arrived):
    @pl.when(lax.axis_index("stream") == 1)
    def _():
        copy = pltpu.make_async_copy(tiles_hbm, tiles, arrived)
        copy.start()
        copy.wait()
        width, coarse = tiles.shape[2:]
        sub = lax.broadcasted_iota(jnp.int32, (width, coarse), 0)
        open_layers = masks[0, :, :coarse] == 0
        for at, number in enumerate(neighbours(tile_map)):
            edges = [None] * POPS
            for pop, offset, row, slot in ((14, -1, 0, 14), (12, 1, width - 1, 15)):
                line = tile_at(tiles, number, (slot,), offset)[0][1:2]
                line = jnp.broadcast_to(line, (width, coarse))
                edges[pop] = jnp.where((sub == row) & open_layers, line, 0.0)
            density, moment = moments_of(edges)
            sums = tile_at(tiles, number, (0, 2, 3))
            for k, value in enumerate((sums[0] + density, sums[1], sums[2] + moment[2])):
                if at == 1:
                    back[k] = value
                else:
                    line, edge = (k, width - 1) if at == 0 else (3 + k, 0)
                    back[3, line : line + 1, :] = value[edge : edge + 1]


def build_columns(is_left, col, corner, halo, edge, lines, x_low, x_high, masks):
    inward, outward = (forward_z, backward_z) if is_left else (backward_z, forward_z)
    rim, first = (0, 0) if is_left else (7, 4)
    for k in range(KEPT):
        col[k, 8:16, :] = halo[k]
    for k in range(5):
        col[KEPT + k, 8:16, :] = edge[outward[k]]
    corner[...] = jnp.zeros(corner.shape, jnp.float32)
    for moving, face, start, near, beyond, row in (
        (incoming, x_low, 0, 7, 6, 0),
        (backward_x, x_high, SIDE, 16, 17, 9),
    ):
        line = lambda k: lines[start + k : start + k + 1, :]
        for k in range(5):
            col[moving[k], near : near + 1, :] = line(k)
        for k, pop in enumerate([pop for pop in inward if pop in stays_x]):
            col[pop, near : near + 1, :] = line(5 + k)
        turning = [pop for pop in moving if pop in inward][0]
        leaving = [pop for pop in moving if pop in outward][0]
        col[turning, beyond : beyond + 1, :] = line(8)
        at = POPS + inward.index(turning)
        col[at, near : near + 1, :] = line(9)
        at = KEPT + outward.index(leaving)
        col[at, near : near + 1, :] = face[moving.index(leaving), rim : rim + 1, :]
        for k in range(4):
            corner[k, row : row + 1, :] = line(10 + k)
        at = 4 if moving is incoming else 5
        corner[at, row : row + 1, :] = line(14)
        for lanes, blocked in masks:
            missing = [None] * POPS
            for k, (pop, _) in enumerate(edge_lines(outward, moving, 0, 0)):
                step_y = velocities[pop][1]
                value = face[13, first + k : first + k + 1, lanes]
                value = shift_layers(jnp.broadcast_to(value, blocked[0].shape), step_y)
                missing[pop] = jnp.where(blocked[step_y] != 0, 0.0, value)
            density, moment = moments_of(missing)
            for k, value in enumerate([density] + moment):
                corner[k, row : row + 1, lanes] += value[:1]


def entry_at(row, at):
    lane = lax.broadcasted_iota(jnp.int32, row.shape, 1)
    return jnp.sum(jnp.where(lane == at, row[...].astype(jnp.float32), 0.0), axis=1, keepdims=True)


def neighbours(row):
    count = row.shape[1]
    position = lax.axis_index("span")
    return [entry_at(row, lax.rem(position + step, count)) for step in (count - 1, 0, 1)]


def tile_at(tiles, number, slots, offset=0):
    count = tiles.shape[0]
    found = [tiles[offset % count, slot] for slot in slots]
    for tile in range(1, count):
        here = jnp.broadcast_to(number, found[0].shape) == float(tile)
        found = [
            jnp.where(here, tiles[(tile + offset) % count, slot], value)
            for slot, value in zip(slots, found)
        ]
    return found


def fill_matrices(layer_phase, matrices):
    shape = matrices.shape[1:]
    rows = lax.broadcasted_iota(jnp.int32, shape, 0)
    fine = lax.broadcasted_iota(jnp.int32, shape, 1)
    choices = []
    for phase in (0, 1):
        position = fine + phase
        lower = lax.shift_right_arithmetic(position - 1, 1)
        upper_wt = jnp.where(position % 2 == 0, 0.75, 0.25)
        low_idx = jnp.clip(lower, 0, shape[0] - 1)
        high_idx = jnp.clip(lower + 1, 0, shape[0] - 1)
        choices.append(
            jnp.where(rows == low_idx, 1.0 - upper_wt, 0.0)
            + jnp.where(rows == high_idx, upper_wt, 0.0)
        )
    for tile, phase in enumerate(neighbours(layer_phase)):
        chosen = jnp.where(jnp.broadcast_to(phase, shape) > 0.5, choices[1], choices[0])
        matrices[tile] = chosen.astype(jnp.bfloat16)


def refine(planes, matrices):
    refined = []
    for tile, group in enumerate(planes):
        parts = []
        rest = jnp.concatenate(group, axis=0)
        for _ in range(3):
            parts.append(rest.astype(jnp.bfloat16))
            rest = rest - parts[-1].astype(jnp.float32)
        total = None
        for part in reversed(parts):
            product = jnp.dot(part, matrices[tile], preferred_element_type=jnp.float32)
            total = product if total is None else total + product
        refined.append(total.reshape(len(group), group[0].shape[0], total.shape[1]))
    return refined


def lanes_of(coarse, fine):
    return slice(0, coarse), slice(coarse, coarse + fine)


def masks_of(masks, lanes, height=8):
    values = {step: masks[step % 3, :, lanes] for step in (0, 1, -1)}
    if height == 8:
        return values
    return {
        step: jnp.broadcast_to(value[:1], (height, value.shape[1]))
        for step, value in values.items()
    }


def middle_kernel(
    tile_map,
    layer_phase,
    masks,
    star_pre,
    star_main,
    cross,
    same,
    edge_same,
    edge_cross,
    tiles_hbm,
    mid_pre,
    mid_main,
    inflow,
    awaited,
    matrices,
    out_pre_hbm,
    out_main_hbm,
    ghost_left,
    ghost_right,
    rim_left,
    rim_right,
    out_pre,
    out_main,
    tiles,
    arrived,
    sent,
):
    rows, width, coarse = star_pre.shape[1:]
    fine = star_main.shape[3]
    parity = lax.rem(lax.axis_index("span"), 2)

    on_inlet = lax.axis_index("stream") == 0
    copy = pltpu.make_async_copy(tiles_hbm, tiles, arrived)

    @pl.when(on_inlet)
    def _():
        copy.start()

    def ghosts(is_left, ghost, halo, edge, rim):
        inward, outward = (forward_z, backward_z) if is_left else (backward_z, forward_z)
        for k in range(5):
            ghost[k] = halo[inward[k]]
        for lanes in lanes_of(coarse, fine):
            new = column_values(
                is_left,
                lambda pop: halo[pop, :, lanes],
                lambda k: halo[POPS + k, :, lanes],
                lambda k: edge[outward[k], :, lanes],
                turned,
                masks_of(masks, lanes),
            )
            out = collide(new, inward)
            for k in range(5):
                rim[k, :, lanes] = out[inward[k]]

    @pl.when(parity == 0)
    def _():
        ghosts(True, ghost_left, cross, edge_cross, rim_left)
        ghosts(False, ghost_right, same, edge_same, rim_right)

    @pl.when(parity == 1)
    def _():
        ghosts(True, ghost_left, same, edge_same, rim_left)
        ghosts(False, ghost_right, cross, edge_cross, rim_right)

    stars = (star_pre, star_main)

    def first_step(x_at):
        for domain, lanes in enumerate(lanes_of(coarse, fine)):
            new = moved_row(
                lambda pop, at: stars[domain][pop, at],
                lambda pop, at: ghost_left[forward_z.index(pop), at : at + 1, lanes],
                lambda pop, at: ghost_right[backward_z.index(pop), at : at + 1, lanes],
                masks_of(masks, lanes),
                x_at,
            )
            out = collide(new)
            for pop in range(POPS):
                (mid_pre, mid_main)[domain][pop, x_at - 1] = out[pop]

    copies = []

    def second_step(x_at):
        for domain, lanes in enumerate(lanes_of(coarse, fine)):
            new = moved_row(
                lambda pop, at: (mid_pre, mid_main)[domain][pop, at - 1],
                lambda pop, at: rim_left[forward_z.index(pop), at : at + 1, lanes],
                lambda pop, at: rim_right[backward_z.index(pop), at : at + 1, lanes],
                masks_of(masks, lanes),
                x_at,
            )
            kept = (out_pre, out_main)[domain]
            for pop in range(POPS):
                kept[pop, x_at - 2] = new[pop]
            if x_at % 2 == 1:
                copies.append(
                    pltpu.make_async_copy(
                        kept.at[:, x_at - 3 : x_at - 1],
                        (out_pre_hbm, out_main_hbm)[domain].at[:, x_at - 1 : x_at + 1],
                        sent.at[domain, x_at - 2],
                    )
                )
                copies[-1].start()

    for x_at in range(1, rows - 1):
        first_step(x_at)
        if x_at >= 3:
            second_step(x_at - 1)

    @pl.when(on_inlet)
    def _():
        copy.wait()
        planes = []
        blocked = masks_of(masks, slice(0, coarse))
        sub = lax.broadcasted_iota(jnp.int32, (width, coarse), 0)
        for place, number in enumerate(neighbours(tile_map)):
            found = tile_at(tiles, number, range(14))
            planes.append(found[:5])
            edges = [None] * POPS
            for pops, offset, row, slot in (
                (forward_z, -1, 0, 14),
                (backward_z, 1, width - 1, 15),
            ):
                lines = tile_at(tiles, number, (slot,), offset)[0]
                for k, pop in enumerate(pops):
                    line = jnp.broadcast_to(lines[k : k + 1], (width, coarse))
                    line = shift_layers(line, velocities[pop][1])
                    keep = (sub == row) & (blocked[velocities[pop][1]] == 0)
                    edges[pop] = jnp.where(keep, line, 0.0)
            density, moment = moments_of(edges)
            for k, value in enumerate([density] + moment):
                awaited[place, k] = found[10 + k] + value
            for k, pop in enumerate(incoming):
                new = found[5 + k]
                awaited[place, 4 + k] = new if edges[pop] is None else new + edges[pop]
        fill_matrices(layer_phase, matrices)
        for place, value in enumerate(refine(planes, matrices)):
            inflow[place] = value

    for copy_out in copies:
        copy_out.wait()


def last_kernel(
    masks,
    star_pre,
    star_main,
    mid_pre,
    mid_main,
    inflow,
    x_high,
    x_low,
    cross,
    same,
    edge_same,
    edge_cross,
    e_cross,
    e_same,
    awaited,
    back,
    matrices,
    part_pre,
    part_main,
    out_pre_hbm,
    out_main_hbm,
    col_left,
    col_right,
    corner_left,
    corner_right,
    in_low,
    in_high,
    next_pre,
    next_main,
    rim_left,
    rim_right,
    out_pre,
    out_main,
    sent,
):
    rows, width, coarse = star_pre.shape[1:]
    fine = star_main.shape[3]
    pre_lanes, main_lanes = lanes_of(coarse, fine)
    is_first = lax.axis_index("stream") == 0
    is_last = lax.axis_index("stream") == lax.axis_size("stream") - 1
    parity = lax.rem(lax.axis_index("span"), 2)
    ends = (x_low, x_high, [(lanes, masks_of(masks, lanes)) for lanes in (pre_lanes, main_lanes)])

    @pl.when(parity == 0)
    def _():
        build_columns(True, col_left, corner_left, cross, edge_cross, e_cross, *ends)
        build_columns(False, col_right, corner_right, same, edge_same, e_same, *ends)

    @pl.when(parity == 1)
    def _():
        build_columns(True, col_left, corner_left, same, edge_same, e_same, *ends)
        build_columns(False, col_right, corner_right, cross, edge_cross, e_cross, *ends)

    for k in range(5):
        in_low[k] = x_low[k, :, main_lanes]
        in_high[k] = x_high[k, :, main_lanes]

    @pl.when(is_last)
    def _():
        for k in range(5):
            in_high[k] = star_main[backward_x[k], rows - 1]
        for col in (col_left, col_right):
            for k in range(KEPT + 5):
                col[k, 16:17, main_lanes] = col[k, 15:16, main_lanes]

    @pl.when(is_first)
    def _():
        before, own, after = (inflow.at[tile] for tile in range(3))
        for k in range(5):
            in_low[k] = own[k]
            col_left[incoming[k], 7:8, main_lanes] = before[k, width - 1 : width]
            col_right[incoming[k], 7:8, main_lanes] = after[k, 0:1]
        col_left[POPS + 1, 7:8, main_lanes] = before[3, width - 2 : width - 1]
        col_left[KEPT + 2, 7:8, main_lanes] = own[4, 0:1]
        col_right[POPS + 2, 7:8, main_lanes] = after[4, 1:2]
        col_right[KEPT + 1, 7:8, main_lanes] = own[3, width - 1 : width]

    for is_left, col, corner, rim in (
        (True, col_left, corner_left, rim_left),
        (False, col_right, corner_right, rim_right),
    ):
        moving = forward_z if is_left else backward_z
        for lanes in (pre_lanes, main_lanes):
            new = column_values(
                is_left,
                lambda pop, step_x=0: col[pop, 7 - step_x : 23 - step_x, lanes],
                lambda k, step_x: col[POPS + k, 7 - step_x : 23 - step_x, lanes],
                lambda k, step_x: col[KEPT + k, 7 - step_x : 23 - step_x, lanes],
                lambda read, at, step_x: read(at, step_x),
                masks_of(masks, lanes, 16),
            )
            row = lax.broadcasted_iota(jnp.int32, new[0].shape, 0)
            for pop in range(POPS):
                if pop not in backward_x:
                    new[pop] = jnp.where(row == 0, 0.0, new[pop])
                if pop not in incoming:
                    new[pop] = jnp.where(row == rows + 1, 0.0, new[pop])
            density, moment = moments_of(new)
            density = density + corner[0, :, lanes]
            moment = [moment[axis_num] + corner[1 + axis_num, :, lanes] for axis_num in range(3)]
            for at, ends_of in ((4, incoming), (5, backward_x)):
                pop = [pop for pop in moving if pop in ends_of][0]
                new[pop] = new[pop] + corner[at, :, lanes]
            out = relax(new, density, moment, moving)
            for k in range(5):
                rim[k, :, lanes] = out[moving[k]]

    stars = (star_pre, star_main)
    outer = {-1: 0, 0: 1, rows - 1: 2, rows: 3}

    def base_of(domain, lanes):
        def base(pop, x_at):
            if 0 <= x_at < rows:
                return stars[domain][pop, x_at]
            if x_at == -1:
                k = incoming.index(pop)
                return in_low[k] if domain == 1 else x_low[k, :, lanes]
            k = backward_x.index(pop)
            return in_high[k] if domain == 1 else x_high[k, :, lanes]

        return base

    def beside_tile(domain, lanes, x_at):
        star = stars[domain]
        face, moving, back = (
            (x_low, incoming, backward_x) if x_at < 0 else (x_high, backward_x, incoming)
        )
        blocked = masks_of(masks, lanes)
        left = lambda pop, at: col_left[pop, 8 + at : 9 + at, lanes]
        right = lambda pop, at: col_right[pop, 8 + at : 9 + at, lanes]

        def base(pop, at):
            return face[moving.index(pop), :, lanes] if at == x_at else star[pop, at]

        new = moved_row(base, left, right, blocked, x_at, back)
        sub = lax.broadcasted_iota(jnp.int32, new[back[0]].shape, 0)
        for pop in range(POPS):
            if pop in back:
                continue
            step_x, step_y, step_z = velocities[pop]
            if step_z != 0:
                line = (left if step_z == 1 else right)(pop, x_at - step_x)
                line = shift_layers(jnp.broadcast_to(line, sub.shape), step_y)
                keep = (sub == (0 if step_z == 1 else width - 1)) & (blocked[step_y] == 0)
                new[pop] = jnp.where(keep, line, 0.0)
            if pop in moving:
                part = face[5 + moving.index(pop), :, lanes]
                new[pop] = part if new[pop] is None else part + new[pop]
        density, moment = moments_of(new)
        density = density + face[10, :, lanes]
        moment = [moment[0], moment[1] + face[11, :, lanes], moment[2] + face[12, :, lanes]]
        return relax(new, density, moment, moving), moving

    def next_of(domain):
        def base(pop, x_at):
            if x_at in outer:
                return (next_pre, next_main)[domain][pop, outer[x_at]]
            return (mid_pre, mid_main)[domain][pop, x_at - 1]

        return base

    def end_row(x_at):
        for domain, lanes in enumerate((pre_lanes, main_lanes)):
            if 0 <= x_at < rows:
                new = moved_row(
                    base_of(domain, lanes),
                    lambda pop, at: col_left[pop, 8 + at : 9 + at, lanes],
                    lambda pop, at: col_right[pop, 8 + at : 9 + at, lanes],
                    masks_of(masks, lanes),
                    x_at,
                )
                out, wanted = collide(new), range(POPS)
            else:
                out, wanted = beside_tile(domain, lanes, x_at)
            for pop in wanted:
                (next_pre, next_main)[domain][pop, outer[x_at]] = out[pop]

    copies = []

    def second_step(at_end, x_at):
        for domain, lanes in enumerate((pre_lanes, main_lanes)):
            new = moved_row(
                next_of(domain),
                lambda pop, at: rim_left[forward_z.index(pop), at + 1 : at + 2, lanes],
                lambda pop, at: rim_right[backward_z.index(pop), at + 1 : at + 2, lanes],
                masks_of(masks, lanes),
                x_at,
            )
            kept = (out_pre, out_main)[domain]
            for pop in range(POPS):
                kept[pop, at_end] = new[pop]
            if at_end % 2 == 1:
                first = x_at - x_at % 2
                copies.append(
                    pltpu.make_async_copy(
                        kept.at[:, at_end - 1 : at_end + 1],
                        (out_pre_hbm, out_main_hbm)[domain].at[:, first : first + 2],
                        sent.at[domain, at_end],
                    )
                )
                copies[-1].start()

    end_row(rows - 1)
    second_step(2, rows - 2)
    end_row(rows)

    @pl.when(is_last)
    def _():
        for k in range(5):
            next_main[backward_x[k], 3] = next_main[backward_x[k], 2]
            for rim in (rim_left, rim_right):
                rim[k, rows + 1 : rows + 2, main_lanes] = rim[k, rows : rows + 1, main_lanes]

    second_step(3, rows - 1)
    end_row(0)
    end_row(-1)

    @pl.when(is_first)
    def _():
        planes = []
        for place in range(3):
            first = 0 if place == 0 else 3
            rest = [back[k] if place == 1 else back[3, first + k : first + k + 1, :] for k in range(3)]
            density = awaited[place, 0] + rest[0]
            moment = [
                awaited[place, 1] - rest[0],
                awaited[place, 2] + rest[1],
                awaited[place, 3] + rest[2],
            ]
            new = [None] * POPS
            for k, pop in enumerate(incoming):
                new[pop] = awaited[place, 4 + k]
            out = relax(new, density, moment, incoming)
            planes.append([out[pop] for pop in incoming])
        before, own, after = refine(planes, matrices)
        for k in range(5):
            next_main[incoming[k], 0] = own[k]
        rim_left[1, 0:1, main_lanes] = before[3, width - 1 : width]
        rim_right[2, 0:1, main_lanes] = after[4, 0:1]

    second_step(0, 0)
    second_step(1, 1)
    for copy in copies:
        copy.wait()


def f32(*shape):
    return jax.ShapeDtypeStruct(shape, jnp.float32)


def local(pre_pops, main_pops, tile_map, layer_phase, wall_flags):
    span_count = lax.axis_size("span")
    stream_count = lax.axis_size("stream")
    _, rows, width, coarse = pre_pops.shape
    fine = main_pops.shape[3]
    lanes = coarse + fine

    def send(value, step_x, place, only=range(stream_count)):
        moves = []
        for s in range(stream_count):
            if s not in only:
                continue
            for j in range(span_count):
                target = (s + step_x) % stream_count * span_count + place(j) % span_count
                moves.append((s * span_count + j, target))
        return lax.ppermute(value, ("stream", "span"), moves)

    def swap_in_pairs(value):
        moves = []
        for s in range(stream_count):
            other = min(s ^ 1, stream_count - 1)
            moves += [(s * span_count + j, other * span_count + j) for j in range(span_count)]
        return lax.ppermute(value, ("stream", "span"), moves)

    stay = lambda j: j
    sibling = lambda j: j + 1 if j % 2 == 0 else j - 1
    beyond = lambda j: j - 1 if j % 2 == 0 else j + 1
    params = pltpu.CompilerParams(vmem_limit_bytes=VMEM_SMALL)

    whole = pl.BlockSpec(memory_space=pltpu.VMEM)
    outside = pl.BlockSpec(memory_space=pltpu.HBM)
    tile_row, phase_row = (row.reshape(1, span_count) for row in (tile_map, layer_phase))

    in_hbm = lambda value: pltpu.with_memory_space_constraint(value, pltpu.HBM)
    star_pre, star_main, z_same, z_cross, masks = pl.pallas_call(
        first_kernel,
        out_shape=(
            f32(*pre_pops.shape),
            f32(*main_pops.shape),
            f32(KEPT, rows, lanes),
            f32(KEPT, rows, lanes),
            f32(3, 8, lanes),
        ),
        in_specs=[outside, outside, outside],
        scratch_shapes=[
            pltpu.VMEM(pre_pops.shape, jnp.float32),
            pltpu.VMEM(main_pops.shape, jnp.float32),
            pltpu.VMEM((1, fine), jnp.int32),
            pltpu.SemaphoreType.DMA((2, rows)),
            pltpu.SemaphoreType.DMA,
        ],
        compiler_params=pltpu.CompilerParams(vmem_limit_bytes=VMEM_SMALL),
        name="collide_and_pack",
    )(in_hbm(wall_flags), in_hbm(pre_pops), in_hbm(main_pops))
    x_hi, x_lo, plane = pl.pallas_call(
        face_kernel,
        out_shape=(
            f32(FACE, width, lanes),
            f32(FACE, width, lanes),
            f32(PLANE, width, coarse),
        ),
        compiler_params=params,
        name="faces",
    )(masks, star_pre, star_main)

    same = send(z_same, 0, sibling)
    cross = send(z_cross, 0, beyond)
    x_low = send(x_hi, 1, stay)
    x_high = send(x_lo, -1, stay)
    tiles = lax.all_gather(plane, "span", axis=0, tiled=False)
    anywhere = pl.BlockSpec(memory_space=pl.ANY)
    all_tiles = [
        pltpu.VMEM((span_count, PLANE, width, coarse), jnp.float32),
        pltpu.SemaphoreType.DMA,
    ]
    e_to_same, e_to_cross = pl.pallas_call(
        corner_kernel,
        out_shape=(f32(2 * SIDE, lanes), f32(2 * SIDE, lanes)),
        in_specs=[whole] * 2 + [anywhere],
        compiler_params=params,
        name="corners",
    )(x_high, x_low, tiles)
    e_same = send(e_to_same, 0, sibling)
    e_cross = send(e_to_cross, 0, beyond)
    back = pl.pallas_call(
        back_kernel,
        out_shape=f32(4, width, coarse),
        in_specs=[whole, whole, anywhere],
        scratch_shapes=all_tiles,
        compiler_params=params,
        name="behind_plane",
    )(tile_row, masks, tiles)
    back = swap_in_pairs(back)
    half_pre = pltpu.VMEM((POPS, 4, width, coarse), jnp.float32)
    half_main = pltpu.VMEM((POPS, 4, width, fine), jnp.float32)
    mid_pre, mid_main, inflow, awaited, matrices, part_pre, part_main = pl.pallas_call(
        middle_kernel,
        out_shape=(
            f32(POPS, rows - 2, width, coarse),
            f32(POPS, rows - 2, width, fine),
            f32(3, 5, width, fine),
            f32(3, 9, width, coarse),
            jax.ShapeDtypeStruct((3, coarse, fine), jnp.bfloat16),
            f32(*pre_pops.shape),
            f32(*main_pops.shape),
        ),
        in_specs=[whole] * 9 + [anywhere],
        out_specs=[whole] * 5 + [outside] * 2,
        scratch_shapes=[
            pltpu.VMEM((5, rows, lanes), jnp.float32),
            pltpu.VMEM((5, rows, lanes), jnp.float32),
            pltpu.VMEM((5, rows, lanes), jnp.float32),
            pltpu.VMEM((5, rows, lanes), jnp.float32),
            pltpu.VMEM((POPS, rows - 4, width, coarse), jnp.float32),
            pltpu.VMEM((POPS, rows - 4, width, fine), jnp.float32),
        ]
        + all_tiles
        + [pltpu.SemaphoreType.DMA((2, rows - 4))],
        compiler_params=params,
        name="middle_rows",
    )(tile_row, phase_row, masks, star_pre, star_main, cross, same, z_same, z_cross, tiles)
    return pl.pallas_call(
        last_kernel,
        out_shape=(f32(*pre_pops.shape), f32(*main_pops.shape)),
        in_specs=[whole] * 17 + [outside] * 2,
        out_specs=(outside, outside),
        input_output_aliases={17: 0, 18: 1},
        scratch_shapes=[
            pltpu.VMEM((KEPT + 5, 24, lanes), jnp.float32),
            pltpu.VMEM((KEPT + 5, 24, lanes), jnp.float32),
            pltpu.VMEM((6, 16, lanes), jnp.float32),
            pltpu.VMEM((6, 16, lanes), jnp.float32),
            pltpu.VMEM((5, width, fine), jnp.float32),
            pltpu.VMEM((5, width, fine), jnp.float32),
            half_pre,
            half_main,
            pltpu.VMEM((5, 16, lanes), jnp.float32),
            pltpu.VMEM((5, 16, lanes), jnp.float32),
            half_pre,
            half_main,
            pltpu.SemaphoreType.DMA((2, 4)),
        ],
        compiler_params=pltpu.CompilerParams(vmem_limit_bytes=VMEM_LARGE),
        name="last_rows",
    )(
        masks,
        star_pre,
        star_main,
        mid_pre,
        mid_main,
        inflow,
        x_high,
        x_low,
        cross,
        same,
        z_same,
        z_cross,
        e_cross,
        e_same,
        awaited,
        back,
        matrices,
        part_pre,
        part_main,
    )


def solution(mesh):
    return jax.shard_map(
        local,
        mesh=mesh,
        in_specs=(P(None, "stream", "span", None), P(None, "stream", "span", None), P(), P(), P()),
        out_specs=(P(None, "stream", "span", None), P(None, "stream", "span", None)),
        check_vma=False,
    )
```

```python
import jax
import jax.numpy as jnp
from jax import lax
from jax.experimental import pallas as pl
from jax.experimental.pallas import tpu as pltpu
from jax.sharding import PartitionSpec as P

velocities = (
    (0, 0, 0),
    (1, 0, 0),
    (-1, 0, 0),
    (0, 1, 0),
    (0, -1, 0),
    (0, 0, 1),
    (0, 0, -1),
    (1, 1, 0),
    (-1, -1, 0),
    (1, -1, 0),
    (-1, 1, 0),
    (1, 0, 1),
    (-1, 0, -1),
    (1, 0, -1),
    (-1, 0, 1),
    (0, 1, 1),
    (0, -1, -1),
    (0, 1, -1),
    (0, -1, 1),
)
opposite = (0, 2, 1, 4, 3, 6, 5, 8, 7, 10, 9, 12, 11, 14, 13, 16, 15, 18, 17)
pairs = tuple((k, k + 1) for k in range(1, 19, 2))
incoming = (1, 7, 9, 11, 13)
backward_x = (2, 8, 10, 12, 14)
forward_z = (5, 11, 14, 15, 18)
backward_z = (6, 12, 13, 16, 17)
POPS = 19
PLANE = 16
FACE = 14
SIDE = 16
stays_x = tuple(k for k in range(POPS) if velocities[k][0] == 0)
KEPT = POPS + 5
VMEM_SMALL = 10 * 1024 * 1024
VMEM_LARGE = 20 * 1024 * 1024


def moments_of(pops):
    density = None
    moment = [None, None, None]

    def add(total, value):
        return value if total is None else total + value

    for group, weight in ((range(1, 7), 1.0 / 18.0), (range(7, POPS), 1.0 / 36.0)):
        part = None
        parts = [None, None, None]
        for a, b in ((k, k + 1) for k in group[::2]):
            if pops[a] is None and pops[b] is None:
                continue
            if pops[b] is None:
                both, diff = pops[a], pops[a]
            elif pops[a] is None:
                both, diff = pops[b], -pops[b]
            else:
                both, diff = pops[a] + pops[b], pops[a] - pops[b]
            part = add(part, both)
            for axis_num, step in enumerate(velocities[a]):
                if step != 0:
                    parts[axis_num] = add(parts[axis_num], diff if step == 1 else -diff)
        if part is not None:
            density = add(density, part * weight)
        for axis_num in range(3):
            if parts[axis_num] is not None:
                moment[axis_num] = add(moment[axis_num], parts[axis_num] * weight)
    if pops[0] is not None:
        density = add(density, pops[0] * (1.0 / 3.0))
    return density, moment


def relax(pops, density, moment, wanted):
    inverse = 1.0 / density
    speed = [component * inverse for component in moment]
    kinetic = moment[0] * speed[0] + moment[1] * speed[1] + moment[2] * speed[2]
    base = 1.25 * density - 1.875 * kinetic
    result = [None] * POPS
    if 0 in wanted:
        result[0] = base - 0.25 * pops[0]
    for a, b in pairs:
        if a not in wanted and b not in wanted:
            continue
        flux = None
        along = None
        for axis_num, step in enumerate(velocities[a]):
            if step == 0:
                continue
            if flux is None:
                flux, along = moment[axis_num], speed[axis_num]
            elif step == 1:
                flux, along = flux + moment[axis_num], along + speed[axis_num]
            else:
                flux, along = flux - moment[axis_num], along - speed[axis_num]
        even = base + 5.625 * (flux * along)
        odd = 3.75 * flux
        if a in wanted:
            result[a] = even + odd - 0.25 * pops[a]
        if b in wanted:
            result[b] = even - odd - 0.25 * pops[b]
    return result


def collide(pops, wanted=range(POPS)):
    density, moment = moments_of(pops)
    return relax(pops, density, moment, wanted)


def shift_layers(value, step_y):
    if step_y == 0:
        return value
    size = value.shape[-1]
    return pltpu.roll(value, step_y % size, value.ndim - 1)


def moved_row(base, left, right, masks, x_at, wanted=range(POPS)):
    result = []
    sub = None
    for which_pop in range(POPS):
        if which_pop not in wanted:
            result.append(None)
            continue
        step_x, step_y, step_z = velocities[which_pop]
        source = base(which_pop, x_at - step_x)
        if which_pop == 0:
            result.append(source)
            continue
        if step_z != 0 and sub is None:
            sub = lax.broadcasted_iota(jnp.int32, source.shape, 0)
        width = source.shape[0]
        if step_z == 1:
            source = jnp.where(
                sub == 0, left(which_pop, x_at - step_x), pltpu.roll(source, 1, 0)
            )
        elif step_z == -1:
            source = jnp.where(
                sub == width - 1,
                right(which_pop, x_at - step_x),
                pltpu.roll(source, width - 1, 0),
            )
        source = shift_layers(source, step_y)
        result.append(
            jnp.where(masks[step_y] != 0, base(opposite[which_pop], x_at), source)
        )
    return result


def fill_masks(walls, masks):
    fine = walls.shape[1]
    coarse = masks.shape[2] - fine

    def fill(solid, lanes):
        layers = solid.shape[1]
        lane = lax.broadcasted_iota(jnp.int32, solid.shape, 1)
        masks[0, :, lanes] = solid
        masks[1, :, lanes] = jnp.where(lane == 0, 1.0, pltpu.roll(solid, 1, 1))
        masks[2, :, lanes] = jnp.where(lane == layers - 1, 1.0, pltpu.roll(solid, layers - 1, 1))

    solid = jnp.broadcast_to(jnp.where(walls[...] > 0, 1.0, 0.0), (8, fine))
    fine_at = lax.broadcasted_iota(jnp.int32, (fine, coarse), 0)
    coarse_at = lax.broadcasted_iota(jnp.int32, (fine, coarse), 1)
    halves = jnp.where(lax.shift_right_logical(fine_at, 1) == coarse_at, 1.0, 0.0)
    hits = jnp.dot(solid, halves, preferred_element_type=jnp.float32)
    fill(jnp.where(hits > 0.5, 1.0, 0.0), slice(0, coarse))
    fill(solid, slice(coarse, coarse + fine))


def first_kernel(
    pre_hbm,
    main_hbm,
    star_pre,
    star_main,
    z_same,
    z_cross,
    pre,
    main,
    arrived,
):
    rows = pre.shape[1]
    coarse = pre.shape[3]
    parity = lax.rem(lax.axis_index("span"), 2)
    domains = ((pre, star_pre, slice(0, coarse)), (main, star_main, slice(coarse, None)))
    copies = [
        [
            pltpu.make_async_copy(source.at[:, x_at], target.at[:, x_at], arrived.at[at, x_at])
            for at, (source, target) in enumerate(((pre_hbm, pre), (main_hbm, main)))
        ]
        for x_at in range(rows)
    ]
    for row in copies:
        for copy in row:
            copy.start()
    for x_at in range(rows):
        for copy in copies[x_at]:
            copy.wait()
        for pops, star, lanes in domains:
            out = collide([pops[which_pop, x_at] for which_pop in range(POPS)])
            for which_pop in range(POPS):
                star[which_pop, x_at] = out[which_pop]

    def edges(hi, lo):
        for _, star, lanes in domains:
            width = star.shape[2]
            for which_pop in range(POPS):
                hi[which_pop, :, lanes] = star[which_pop, :, width - 1, :]
                lo[which_pop, :, lanes] = star[which_pop, :, 0, :]
            for k in range(5):
                hi[POPS + k, :, lanes] = star[forward_z[k], :, width - 2, :]
                lo[POPS + k, :, lanes] = star[backward_z[k], :, 1, :]

    @pl.when(parity == 0)
    def _():
        edges(z_same, z_cross)

    @pl.when(parity == 1)
    def _():
        edges(z_cross, z_same)


def edge_lines(pops, moving, rim, inner):
    return [(pop, rim) for pop in pops if pop in stays_x] + [
        (pop, inner) for pop in pops if pop in moving
    ]


def fill_face(star, lanes, blocked, at_top, face):
    last = star.shape[1] - 1
    moving = incoming if at_top else backward_x
    rim = last if at_top else 0
    none = lambda pop, x_at: 0.0
    base = lambda pop, x_at: star[pop, x_at]
    new = moved_row(base, none, none, blocked, rim, moving + stays_x)
    for k, pop in enumerate(moving):
        face[k, :, lanes] = star[pop, rim]
        face[5 + k, :, lanes] = new[pop]
        new[pop] = None
    density, moment = moments_of(new)
    face[10, :, lanes] = density
    face[11, :, lanes] = moment[1]
    face[12, :, lanes] = moment[2]
    inner = rim - 1 if at_top else rim + 1
    for first, pops, z_at in ((0, backward_z, 0), (4, forward_z, star.shape[2] - 1)):
        for k, (pop, x_at) in enumerate(edge_lines(pops, moving, rim, inner)):
            row = first + k
            face[13, row : row + 1, lanes] = star[pop, x_at, z_at : z_at + 1, :]


def face_kernel(walls, star_pre, star_main, masks, x_hi, x_lo, plane):
    coarse = star_pre.shape[3]
    fill_masks(walls, masks)
    for star, lanes in zip((star_pre, star_main), lanes_of(coarse, star_main.shape[3])):
        blocked = masks_of(masks, lanes)
        fill_face(star, lanes, blocked, True, x_hi)
        fill_face(star, lanes, blocked, False, x_lo)
    fill_plane(star_pre, masks_of(masks, slice(0, coarse)), plane)


def fill_plane(star, blocked, plane):
    width, coarse = plane.shape[1:]
    last = star.shape[1] - 1
    zero = jnp.zeros((width, coarse), jnp.float32)
    stream_pos = lax.axis_index("stream")

    @pl.when(stream_pos != 1)
    def _():
        base = lambda pop, x_at: zero if x_at > last else star[pop, x_at]
        none = lambda pop, x_at: 0.0
        new = moved_row(base, none, none, blocked, last)
        density, moment = moments_of(new)
        for k, pop in enumerate(incoming):
            plane[k] = star[pop, last]
            plane[5 + k] = new[pop]
        plane[10] = density
        for axis_num in range(3):
            plane[11 + axis_num] = moment[axis_num]
        plane[14] = zero
        plane[15] = zero
        for k in range(5):
            hi, lo = forward_z[k], backward_z[k]
            plane[14, k : k + 1, :] = base(hi, last - velocities[hi][0])[width - 1 : width]
            plane[15, k : k + 1, :] = base(lo, last - velocities[lo][0])[0:1]

    @pl.when(stream_pos == 1)
    def _():
        none = lambda pop, x_at: 0.0
        back = moved_row(
            lambda pop, x_at: star[pop, x_at] if pop in backward_x else zero,
            none,
            none,
            blocked,
            -1,
            backward_x,
        )
        density, moment = moments_of(back)
        for k, value in enumerate([density] + moment):
            plane[k] = value
        for k in range(4, PLANE):
            plane[k] = zero
        plane[14, 1:2, :] = star[14, 0, width - 1 : width, :]
        plane[15, 1:2, :] = star[12, 0, 0:1, :]


def column_values(is_left, first, second, inner, shift, blocked):
    inward, outward = (forward_z, backward_z) if is_left else (backward_z, forward_z)
    result = []
    result.append(first(0))
    for pop in range(1, POPS):
        step_x, step_y, _ = velocities[pop]
        if pop in inward:
            source = shift(second, inward.index(pop), step_x)
        elif pop in outward:
            source = shift(inner, outward.index(pop), step_x)
        else:
            source = shift(first, pop, step_x)
        result.append(
            jnp.where(blocked[step_y] != 0, first(opposite[pop]), shift_layers(source, step_y))
        )
    return result


def turned(read, at, step_x):
    value = read(at)
    return value if step_x == 0 else pltpu.roll(value, step_x % value.shape[0], 0)


def only(pops, values):
    return [values[pop] if pop in pops else None for pop in range(POPS)]


def corner_kernel(x_high, x_low, tiles, e_same, e_cross):
    def lines(is_left, target):
        inward = forward_z if is_left else backward_z
        edge, second, first = (7, 6, 4) if is_left else (0, 1, 0)
        for start, moving, face in ((0, incoming, x_low), (SIDE, backward_x, x_high)):
            turning = moving.index([pop for pop in moving if pop in inward][0])
            new = [None] * POPS
            for k, pop in enumerate(moving):
                new[pop] = face[5 + k]
            density, moment = moments_of(new)
            sums = [
                density + face[10],
                moment[0],
                moment[1] + face[11],
                moment[2] + face[12],
                face[5 + turning],
            ]
            found = [face[k, edge : edge + 1, :] for k in range(5)]
            found += [face[13, first + k : first + k + 1, :] for k in range(4)]
            found += [face[turning, second : second + 1, :]]
            found += [value[edge : edge + 1] for value in sums]
            for k, line in enumerate(found):
                target[start + k : start + k + 1, :] = line

    parity = lax.rem(lax.axis_index("span"), 2)

    @pl.when(parity == 0)
    def _():
        lines(True, e_same)
        lines(False, e_cross)

    @pl.when(parity == 1)
    def _():
        lines(False, e_same)
        lines(True, e_cross)


def back_kernel(tile_map, masks, tiles_hbm, back, tiles, arrived):
    @pl.when(lax.axis_index("stream") == 1)
    def _():
        copy = pltpu.make_async_copy(tiles_hbm, tiles, arrived)
        copy.start()
        copy.wait()
        width, coarse = tiles.shape[2:]
        sub = lax.broadcasted_iota(jnp.int32, (width, coarse), 0)
        open_layers = masks[0, :, :coarse] == 0
        for at, number in enumerate(neighbours(tile_map)):
            edges = [None] * POPS
            for pop, offset, row, slot in ((14, -1, 0, 14), (12, 1, width - 1, 15)):
                line = tile_at(tiles, number, (slot,), offset)[0][1:2]
                line = jnp.broadcast_to(line, (width, coarse))
                edges[pop] = jnp.where((sub == row) & open_layers, line, 0.0)
            density, moment = moments_of(edges)
            sums = tile_at(tiles, number, (0, 2, 3))
            for k, value in enumerate((sums[0] + density, sums[1], sums[2] + moment[2])):
                if at == 1:
                    back[k] = value
                else:
                    line, edge = (k, width - 1) if at == 0 else (3 + k, 0)
                    back[3, line : line + 1, :] = value[edge : edge + 1]


def build_columns(is_left, col, corner, halo, edge, lines, x_low, x_high, masks):
    inward, outward = (forward_z, backward_z) if is_left else (backward_z, forward_z)
    rim, first = (0, 0) if is_left else (7, 4)
    for k in range(KEPT):
        col[k, 8:16, :] = halo[k]
    for k in range(5):
        col[KEPT + k, 8:16, :] = edge[outward[k]]
    corner[...] = jnp.zeros(corner.shape, jnp.float32)
    for moving, face, start, near, beyond, row in (
        (incoming, x_low, 0, 7, 6, 0),
        (backward_x, x_high, SIDE, 16, 17, 9),
    ):
        line = lambda k: lines[start + k : start + k + 1, :]
        for k in range(5):
            col[moving[k], near : near + 1, :] = line(k)
        for k, pop in enumerate([pop for pop in inward if pop in stays_x]):
            col[pop, near : near + 1, :] = line(5 + k)
        turning = [pop for pop in moving if pop in inward][0]
        leaving = [pop for pop in moving if pop in outward][0]
        col[turning, beyond : beyond + 1, :] = line(8)
        at = POPS + inward.index(turning)
        col[at, near : near + 1, :] = line(9)
        at = KEPT + outward.index(leaving)
        col[at, near : near + 1, :] = face[moving.index(leaving), rim : rim + 1, :]
        for k in range(4):
            corner[k, row : row + 1, :] = line(10 + k)
        at = 4 if moving is incoming else 5
        corner[at, row : row + 1, :] = line(14)
        for lanes, blocked in masks:
            missing = [None] * POPS
            for k, (pop, _) in enumerate(edge_lines(outward, moving, 0, 0)):
                step_y = velocities[pop][1]
                value = face[13, first + k : first + k + 1, lanes]
                value = shift_layers(jnp.broadcast_to(value, blocked[0].shape), step_y)
                missing[pop] = jnp.where(blocked[step_y] != 0, 0.0, value)
            density, moment = moments_of(missing)
            for k, value in enumerate([density] + moment):
                corner[k, row : row + 1, lanes] += value[:1]


def entry_at(row, at):
    lane = lax.broadcasted_iota(jnp.int32, row.shape, 1)
    return jnp.sum(jnp.where(lane == at, row[...].astype(jnp.float32), 0.0), axis=1, keepdims=True)


def neighbours(row):
    count = row.shape[1]
    position = lax.axis_index("span")
    return [entry_at(row, lax.rem(position + step, count)) for step in (count - 1, 0, 1)]


def tile_at(tiles, number, slots, offset=0):
    count = tiles.shape[0]
    found = [tiles[offset % count, slot] for slot in slots]
    for tile in range(1, count):
        here = jnp.broadcast_to(number, found[0].shape) == float(tile)
        found = [
            jnp.where(here, tiles[(tile + offset) % count, slot], value)
            for slot, value in zip(slots, found)
        ]
    return found


def fill_matrices(layer_phase, matrices):
    shape = matrices.shape[1:]
    rows = lax.broadcasted_iota(jnp.int32, shape, 0)
    fine = lax.broadcasted_iota(jnp.int32, shape, 1)
    choices = []
    for phase in (0, 1):
        position = fine + phase
        lower = lax.shift_right_arithmetic(position - 1, 1)
        upper_wt = jnp.where(position % 2 == 0, 0.75, 0.25)
        low_idx = jnp.clip(lower, 0, shape[0] - 1)
        high_idx = jnp.clip(lower + 1, 0, shape[0] - 1)
        choices.append(
            jnp.where(rows == low_idx, 1.0 - upper_wt, 0.0)
            + jnp.where(rows == high_idx, upper_wt, 0.0)
        )
    for tile, phase in enumerate(neighbours(layer_phase)):
        chosen = jnp.where(jnp.broadcast_to(phase, shape) > 0.5, choices[1], choices[0])
        matrices[tile] = chosen.astype(jnp.bfloat16)


def refine(planes, matrices):
    refined = []
    for tile, group in enumerate(planes):
        parts = []
        rest = jnp.concatenate(group, axis=0)
        for _ in range(3):
            parts.append(rest.astype(jnp.bfloat16))
            rest = rest - parts[-1].astype(jnp.float32)
        total = None
        for part in reversed(parts):
            product = jnp.dot(part, matrices[tile], preferred_element_type=jnp.float32)
            total = product if total is None else total + product
        refined.append(total.reshape(len(group), group[0].shape[0], total.shape[1]))
    return refined


def lanes_of(coarse, fine):
    return slice(0, coarse), slice(coarse, coarse + fine)


def masks_of(masks, lanes, height=8):
    values = {step: masks[step % 3, :, lanes] for step in (0, 1, -1)}
    if height == 8:
        return values
    return {
        step: jnp.broadcast_to(value[:1], (height, value.shape[1]))
        for step, value in values.items()
    }


def middle_kernel(
    tile_map,
    layer_phase,
    masks,
    star_pre,
    star_main,
    cross,
    same,
    edge_same,
    edge_cross,
    tiles_hbm,
    mid_pre,
    mid_main,
    inflow,
    awaited,
    matrices,
    out_pre_hbm,
    out_main_hbm,
    ghost_left,
    ghost_right,
    rim_left,
    rim_right,
    out_pre,
    out_main,
    tiles,
    arrived,
    sent,
):
    rows, width, coarse = star_pre.shape[1:]
    fine = star_main.shape[3]
    parity = lax.rem(lax.axis_index("span"), 2)

    on_inlet = lax.axis_index("stream") == 0
    copy = pltpu.make_async_copy(tiles_hbm, tiles, arrived)

    @pl.when(on_inlet)
    def _():
        copy.start()

    def ghosts(is_left, ghost, halo, edge, rim):
        inward, outward = (forward_z, backward_z) if is_left else (backward_z, forward_z)
        for k in range(5):
            ghost[k] = halo[inward[k]]
        for lanes in lanes_of(coarse, fine):
            new = column_values(
                is_left,
                lambda pop: halo[pop, :, lanes],
                lambda k: halo[POPS + k, :, lanes],
                lambda k: edge[outward[k], :, lanes],
                turned,
                masks_of(masks, lanes),
            )
            out = collide(new, inward)
            for k in range(5):
                rim[k, :, lanes] = out[inward[k]]

    @pl.when(parity == 0)
    def _():
        ghosts(True, ghost_left, cross, edge_cross, rim_left)
        ghosts(False, ghost_right, same, edge_same, rim_right)

    @pl.when(parity == 1)
    def _():
        ghosts(True, ghost_left, same, edge_same, rim_left)
        ghosts(False, ghost_right, cross, edge_cross, rim_right)

    stars = (star_pre, star_main)

    def first_step(x_at):
        for domain, lanes in enumerate(lanes_of(coarse, fine)):
            new = moved_row(
                lambda pop, at: stars[domain][pop, at],
                lambda pop, at: ghost_left[forward_z.index(pop), at : at + 1, lanes],
                lambda pop, at: ghost_right[backward_z.index(pop), at : at + 1, lanes],
                masks_of(masks, lanes),
                x_at,
            )
            out = collide(new)
            for pop in range(POPS):
                (mid_pre, mid_main)[domain][pop, x_at - 1] = out[pop]

    copies = []

    def second_step(x_at):
        for domain, lanes in enumerate(lanes_of(coarse, fine)):
            new = moved_row(
                lambda pop, at: (mid_pre, mid_main)[domain][pop, at - 1],
                lambda pop, at: rim_left[forward_z.index(pop), at : at + 1, lanes],
                lambda pop, at: rim_right[backward_z.index(pop), at : at + 1, lanes],
                masks_of(masks, lanes),
                x_at,
            )
            kept = (out_pre, out_main)[domain]
            for pop in range(POPS):
                kept[pop, x_at - 2] = new[pop]
            if x_at % 2 == 1:
                copies.append(
                    pltpu.make_async_copy(
                        kept.at[:, x_at - 3 : x_at - 1],
                        (out_pre_hbm, out_main_hbm)[domain].at[:, x_at - 1 : x_at + 1],
                        sent.at[domain, x_at - 2],
                    )
                )
                copies[-1].start()

    for x_at in range(1, rows - 1):
        first_step(x_at)
        if x_at >= 3:
            second_step(x_at - 1)

    @pl.when(on_inlet)
    def _():
        copy.wait()
        planes = []
        blocked = masks_of(masks, slice(0, coarse))
        sub = lax.broadcasted_iota(jnp.int32, (width, coarse), 0)
        for place, number in enumerate(neighbours(tile_map)):
            found = tile_at(tiles, number, range(14))
            planes.append(found[:5])
            edges = [None] * POPS
            for pops, offset, row, slot in (
                (forward_z, -1, 0, 14),
                (backward_z, 1, width - 1, 15),
            ):
                lines = tile_at(tiles, number, (slot,), offset)[0]
                for k, pop in enumerate(pops):
                    line = jnp.broadcast_to(lines[k : k + 1], (width, coarse))
                    line = shift_layers(line, velocities[pop][1])
                    keep = (sub == row) & (blocked[velocities[pop][1]] == 0)
                    edges[pop] = jnp.where(keep, line, 0.0)
            density, moment = moments_of(edges)
            for k, value in enumerate([density] + moment):
                awaited[place, k] = found[10 + k] + value
            for k, pop in enumerate(incoming):
                new = found[5 + k]
                awaited[place, 4 + k] = new if edges[pop] is None else new + edges[pop]
        fill_matrices(layer_phase, matrices)
        for place, value in enumerate(refine(planes, matrices)):
            inflow[place] = value

    for copy_out in copies:
        copy_out.wait()


def last_kernel(
    masks,
    star_pre,
    star_main,
    mid_pre,
    mid_main,
    inflow,
    x_high,
    x_low,
    cross,
    same,
    edge_same,
    edge_cross,
    e_cross,
    e_same,
    awaited,
    back,
    matrices,
    part_pre,
    part_main,
    out_pre_hbm,
    out_main_hbm,
    col_left,
    col_right,
    corner_left,
    corner_right,
    in_low,
    in_high,
    next_pre,
    next_main,
    rim_left,
    rim_right,
    out_pre,
    out_main,
    sent,
):
    rows, width, coarse = star_pre.shape[1:]
    fine = star_main.shape[3]
    pre_lanes, main_lanes = lanes_of(coarse, fine)
    is_first = lax.axis_index("stream") == 0
    is_last = lax.axis_index("stream") == lax.axis_size("stream") - 1
    parity = lax.rem(lax.axis_index("span"), 2)
    ends = (x_low, x_high, [(lanes, masks_of(masks, lanes)) for lanes in (pre_lanes, main_lanes)])

    @pl.when(parity == 0)
    def _():
        build_columns(True, col_left, corner_left, cross, edge_cross, e_cross, *ends)
        build_columns(False, col_right, corner_right, same, edge_same, e_same, *ends)

    @pl.when(parity == 1)
    def _():
        build_columns(True, col_left, corner_left, same, edge_same, e_same, *ends)
        build_columns(False, col_right, corner_right, cross, edge_cross, e_cross, *ends)

    for k in range(5):
        in_low[k] = x_low[k, :, main_lanes]
        in_high[k] = x_high[k, :, main_lanes]

    @pl.when(is_last)
    def _():
        for k in range(5):
            in_high[k] = star_main[backward_x[k], rows - 1]
        for col in (col_left, col_right):
            for k in range(KEPT + 5):
                col[k, 16:17, main_lanes] = col[k, 15:16, main_lanes]

    @pl.when(is_first)
    def _():
        before, own, after = (inflow.at[tile] for tile in range(3))
        for k in range(5):
            in_low[k] = own[k]
            col_left[incoming[k], 7:8, main_lanes] = before[k, width - 1 : width]
            col_right[incoming[k], 7:8, main_lanes] = after[k, 0:1]
        col_left[POPS + 1, 7:8, main_lanes] = before[3, width - 2 : width - 1]
        col_left[KEPT + 2, 7:8, main_lanes] = own[4, 0:1]
        col_right[POPS + 2, 7:8, main_lanes] = after[4, 1:2]
        col_right[KEPT + 1, 7:8, main_lanes] = own[3, width - 1 : width]

    for is_left, col, corner, rim in (
        (True, col_left, corner_left, rim_left),
        (False, col_right, corner_right, rim_right),
    ):
        moving = forward_z if is_left else backward_z
        for lanes in (pre_lanes, main_lanes):
            new = column_values(
                is_left,
                lambda pop, step_x=0: col[pop, 7 - step_x : 23 - step_x, lanes],
                lambda k, step_x: col[POPS + k, 7 - step_x : 23 - step_x, lanes],
                lambda k, step_x: col[KEPT + k, 7 - step_x : 23 - step_x, lanes],
                lambda read, at, step_x: read(at, step_x),
                masks_of(masks, lanes, 16),
            )
            row = lax.broadcasted_iota(jnp.int32, new[0].shape, 0)
            for pop in range(POPS):
                if pop not in backward_x:
                    new[pop] = jnp.where(row == 0, 0.0, new[pop])
                if pop not in incoming:
                    new[pop] = jnp.where(row == rows + 1, 0.0, new[pop])
            density, moment = moments_of(new)
            density = density + corner[0, :, lanes]
            moment = [moment[axis_num] + corner[1 + axis_num, :, lanes] for axis_num in range(3)]
            for at, ends_of in ((4, incoming), (5, backward_x)):
                pop = [pop for pop in moving if pop in ends_of][0]
                new[pop] = new[pop] + corner[at, :, lanes]
            out = relax(new, density, moment, moving)
            for k in range(5):
                rim[k, :, lanes] = out[moving[k]]

    stars = (star_pre, star_main)
    outer = {-1: 0, 0: 1, rows - 1: 2, rows: 3}

    def base_of(domain, lanes):
        def base(pop, x_at):
            if 0 <= x_at < rows:
                return stars[domain][pop, x_at]
            if x_at == -1:
                k = incoming.index(pop)
                return in_low[k] if domain == 1 else x_low[k, :, lanes]
            k = backward_x.index(pop)
            return in_high[k] if domain == 1 else x_high[k, :, lanes]

        return base

    def beside_tile(domain, lanes, x_at):
        star = stars[domain]
        face, moving, back = (
            (x_low, incoming, backward_x) if x_at < 0 else (x_high, backward_x, incoming)
        )
        blocked = masks_of(masks, lanes)
        left = lambda pop, at: col_left[pop, 8 + at : 9 + at, lanes]
        right = lambda pop, at: col_right[pop, 8 + at : 9 + at, lanes]

        def base(pop, at):
            return face[moving.index(pop), :, lanes] if at == x_at else star[pop, at]

        new = moved_row(base, left, right, blocked, x_at, back)
        sub = lax.broadcasted_iota(jnp.int32, new[back[0]].shape, 0)
        for pop in range(POPS):
            if pop in back:
                continue
            step_x, step_y, step_z = velocities[pop]
            if step_z != 0:
                line = (left if step_z == 1 else right)(pop, x_at - step_x)
                line = shift_layers(jnp.broadcast_to(line, sub.shape), step_y)
                keep = (sub == (0 if step_z == 1 else width - 1)) & (blocked[step_y] == 0)
                new[pop] = jnp.where(keep, line, 0.0)
            if pop in moving:
                part = face[5 + moving.index(pop), :, lanes]
                new[pop] = part if new[pop] is None else part + new[pop]
        density, moment = moments_of(new)
        density = density + face[10, :, lanes]
        moment = [moment[0], moment[1] + face[11, :, lanes], moment[2] + face[12, :, lanes]]
        return relax(new, density, moment, moving), moving

    def next_of(domain):
        def base(pop, x_at):
            if x_at in outer:
                return (next_pre, next_main)[domain][pop, outer[x_at]]
            return (mid_pre, mid_main)[domain][pop, x_at - 1]

        return base

    def end_row(x_at):
        for domain, lanes in enumerate((pre_lanes, main_lanes)):
            if 0 <= x_at < rows:
                new = moved_row(
                    base_of(domain, lanes),
                    lambda pop, at: col_left[pop, 8 + at : 9 + at, lanes],
                    lambda pop, at: col_right[pop, 8 + at : 9 + at, lanes],
                    masks_of(masks, lanes),
                    x_at,
                )
                out, wanted = collide(new), range(POPS)
            else:
                out, wanted = beside_tile(domain, lanes, x_at)
            for pop in wanted:
                (next_pre, next_main)[domain][pop, outer[x_at]] = out[pop]

    copies = []

    def second_step(at_end, x_at):
        for domain, lanes in enumerate((pre_lanes, main_lanes)):
            new = moved_row(
                next_of(domain),
                lambda pop, at: rim_left[forward_z.index(pop), at + 1 : at + 2, lanes],
                lambda pop, at: rim_right[backward_z.index(pop), at + 1 : at + 2, lanes],
                masks_of(masks, lanes),
                x_at,
            )
            kept = (out_pre, out_main)[domain]
            for pop in range(POPS):
                kept[pop, at_end] = new[pop]
            if at_end % 2 == 1:
                first = x_at - x_at % 2
                copies.append(
                    pltpu.make_async_copy(
                        kept.at[:, at_end - 1 : at_end + 1],
                        (out_pre_hbm, out_main_hbm)[domain].at[:, first : first + 2],
                        sent.at[domain, at_end],
                    )
                )
                copies[-1].start()

    end_row(rows - 1)
    second_step(2, rows - 2)
    end_row(rows)

    @pl.when(is_last)
    def _():
        for k in range(5):
            next_main[backward_x[k], 3] = next_main[backward_x[k], 2]
            for rim in (rim_left, rim_right):
                rim[k, rows + 1 : rows + 2, main_lanes] = rim[k, rows : rows + 1, main_lanes]

    second_step(3, rows - 1)
    end_row(0)
    end_row(-1)

    @pl.when(is_first)
    def _():
        planes = []
        for place in range(3):
            first = 0 if place == 0 else 3
            rest = [back[k] if place == 1 else back[3, first + k : first + k + 1, :] for k in range(3)]
            density = awaited[place, 0] + rest[0]
            moment = [
                awaited[place, 1] - rest[0],
                awaited[place, 2] + rest[1],
                awaited[place, 3] + rest[2],
            ]
            new = [None] * POPS
            for k, pop in enumerate(incoming):
                new[pop] = awaited[place, 4 + k]
            out = relax(new, density, moment, incoming)
            planes.append([out[pop] for pop in incoming])
        before, own, after = refine(planes, matrices)
        for k in range(5):
            next_main[incoming[k], 0] = own[k]
        rim_left[1, 0:1, main_lanes] = before[3, width - 1 : width]
        rim_right[2, 0:1, main_lanes] = after[4, 0:1]

    second_step(0, 0)
    second_step(1, 1)
    for copy in copies:
        copy.wait()


def f32(*shape):
    return jax.ShapeDtypeStruct(shape, jnp.float32)


def local(pre_pops, main_pops, tile_map, layer_phase, wall_flags):
    span_count = lax.axis_size("span")
    stream_count = lax.axis_size("stream")
    _, rows, width, coarse = pre_pops.shape
    fine = main_pops.shape[3]
    lanes = coarse + fine

    def send(value, step_x, place, only=range(stream_count)):
        moves = []
        for s in range(stream_count):
            if s not in only:
                continue
            for j in range(span_count):
                target = (s + step_x) % stream_count * span_count + place(j) % span_count
                moves.append((s * span_count + j, target))
        return lax.ppermute(value, ("stream", "span"), moves)

    def swap_in_pairs(value):
        moves = []
        for s in range(stream_count):
            other = min(s ^ 1, stream_count - 1)
            moves += [(s * span_count + j, other * span_count + j) for j in range(span_count)]
        return lax.ppermute(value, ("stream", "span"), moves)

    stay = lambda j: j
    sibling = lambda j: j + 1 if j % 2 == 0 else j - 1
    beyond = lambda j: j - 1 if j % 2 == 0 else j + 1
    params = pltpu.CompilerParams(vmem_limit_bytes=VMEM_SMALL)

    whole = pl.BlockSpec(memory_space=pltpu.VMEM)
    outside = pl.BlockSpec(memory_space=pltpu.HBM)
    tile_row, phase_row = (row.reshape(1, span_count) for row in (tile_map, layer_phase))

    in_hbm = lambda value: pltpu.with_memory_space_constraint(value, pltpu.HBM)
    star_pre, star_main, z_same, z_cross = pl.pallas_call(
        first_kernel,
        out_shape=(
            f32(*pre_pops.shape),
            f32(*main_pops.shape),
            f32(KEPT, rows, lanes),
            f32(KEPT, rows, lanes),
        ),
        in_specs=[outside, outside],
        scratch_shapes=[
            pltpu.VMEM(pre_pops.shape, jnp.float32),
            pltpu.VMEM(main_pops.shape, jnp.float32),
            pltpu.SemaphoreType.DMA((2, rows)),
        ],
        compiler_params=pltpu.CompilerParams(vmem_limit_bytes=VMEM_SMALL),
        name="collide_and_pack",
    )(in_hbm(pre_pops), in_hbm(main_pops))
    masks, x_hi, x_lo, plane = pl.pallas_call(
        face_kernel,
        out_shape=(
            f32(3, 8, lanes),
            f32(FACE, width, lanes),
            f32(FACE, width, lanes),
            f32(PLANE, width, coarse),
        ),
        compiler_params=params,
        name="faces",
    )(wall_flags.reshape(1, fine), star_pre, star_main)

    same = send(z_same, 0, sibling)
    cross = send(z_cross, 0, beyond)
    x_low = send(x_hi, 1, stay)
    x_high = send(x_lo, -1, stay)
    tiles = lax.all_gather(plane, "span", axis=0, tiled=False)
    anywhere = pl.BlockSpec(memory_space=pl.ANY)
    all_tiles = [
        pltpu.VMEM((span_count, PLANE, width, coarse), jnp.float32),
        pltpu.SemaphoreType.DMA,
    ]
    e_to_same, e_to_cross = pl.pallas_call(
        corner_kernel,
        out_shape=(f32(2 * SIDE, lanes), f32(2 * SIDE, lanes)),
        in_specs=[whole] * 2 + [anywhere],
        compiler_params=params,
        name="corners",
    )(x_high, x_low, tiles)
    e_same = send(e_to_same, 0, sibling)
    e_cross = send(e_to_cross, 0, beyond)
    back = pl.pallas_call(
        back_kernel,
        out_shape=f32(4, width, coarse),
        in_specs=[whole, whole, anywhere],
        scratch_shapes=all_tiles,
        compiler_params=params,
        name="behind_plane",
    )(tile_row, masks, tiles)
    back = swap_in_pairs(back)
    half_pre = pltpu.VMEM((POPS, 4, width, coarse), jnp.float32)
    half_main = pltpu.VMEM((POPS, 4, width, fine), jnp.float32)
    mid_pre, mid_main, inflow, awaited, matrices, part_pre, part_main = pl.pallas_call(
        middle_kernel,
        out_shape=(
            f32(POPS, rows - 2, width, coarse),
            f32(POPS, rows - 2, width, fine),
            f32(3, 5, width, fine),
            f32(3, 9, width, coarse),
            jax.ShapeDtypeStruct((3, coarse, fine), jnp.bfloat16),
            f32(*pre_pops.shape),
            f32(*main_pops.shape),
        ),
        in_specs=[whole] * 9 + [anywhere],
        out_specs=[whole] * 5 + [outside] * 2,
        scratch_shapes=[
            pltpu.VMEM((5, rows, lanes), jnp.float32),
            pltpu.VMEM((5, rows, lanes), jnp.float32),
            pltpu.VMEM((5, rows, lanes), jnp.float32),
            pltpu.VMEM((5, rows, lanes), jnp.float32),
            pltpu.VMEM((POPS, rows - 4, width, coarse), jnp.float32),
            pltpu.VMEM((POPS, rows - 4, width, fine), jnp.float32),
        ]
        + all_tiles
        + [pltpu.SemaphoreType.DMA((2, rows - 4))],
        compiler_params=params,
        name="middle_rows",
    )(tile_row, phase_row, masks, star_pre, star_main, cross, same, z_same, z_cross, tiles)
    return pl.pallas_call(
        last_kernel,
        out_shape=(f32(*pre_pops.shape), f32(*main_pops.shape)),
        in_specs=[whole] * 17 + [outside] * 2,
        out_specs=(outside, outside),
        input_output_aliases={17: 0, 18: 1},
        scratch_shapes=[
            pltpu.VMEM((KEPT + 5, 24, lanes), jnp.float32),
            pltpu.VMEM((KEPT + 5, 24, lanes), jnp.float32),
            pltpu.VMEM((6, 16, lanes), jnp.float32),
            pltpu.VMEM((6, 16, lanes), jnp.float32),
            pltpu.VMEM((5, width, fine), jnp.float32),
            pltpu.VMEM((5, width, fine), jnp.float32),
            half_pre,
            half_main,
            pltpu.VMEM((5, 16, lanes), jnp.float32),
            pltpu.VMEM((5, 16, lanes), jnp.float32),
            half_pre,
            half_main,
            pltpu.SemaphoreType.DMA((2, 4)),
        ],
        compiler_params=pltpu.CompilerParams(vmem_limit_bytes=VMEM_LARGE),
        name="last_rows",
    )(
        masks,
        star_pre,
        star_main,
        mid_pre,
        mid_main,
        inflow,
        x_high,
        x_low,
        cross,
        same,
        z_same,
        z_cross,
        e_cross,
        e_same,
        awaited,
        back,
        matrices,
        part_pre,
        part_main,
    )


def solution(mesh):
    return jax.shard_map(
        local,
        mesh=mesh,
        in_specs=(P(None, "stream", "span", None), P(None, "stream", "span", None), P(), P(), P()),
        out_specs=(P(None, "stream", "span", None), P(None, "stream", "span", None)),
        check_vma=False,
    )
```
